32 devices in a mesh: shard: 2 (over core), context: 4 (over y, x), tensor: 4 (over z).
Axes of the slice: x: 2, y: 2, z: 4, core: 2. Of those that a mesh axis runs over, the one named last changes fastest.
Arguments:
- inputs: bfloat16 [2, 4096, 768], P('shard', 'context'), may hold values from -6 to 6
- segments: int32 [2, 4096], P('shard'), may hold values from 0 to 4, as said below
- w_qkv: bfloat16 [768, 3, 768], P('shard', None, 'tensor'), may hold values from -0.21875 to 0.21875
- w_out: bfloat16 [768, 768], P('tensor', 'shard'), may hold values from -3 to 3
- w_fc: bfloat16 [768, 3072], P('shard', 'tensor'), may hold values from -0.21875 to 0.21875
- w_down: bfloat16 [3072, 768], P('tensor', 'shard'), may hold values from -0.109375 to 0.109375
- b_qv: float32 [2, 768], P(None, 'tensor'), may hold values from -3 to 3
- b_out: float32 [768], replicated, may hold values from -2 to 2
- b_fc: float32 [3072], P('tensor'), may hold values from -3 to 3
- b_down: float32 [768], replicated, may hold values from -2 to 2
- first_norm_gain: float32 [768], replicated, may hold values from 0.5 to 1.5
- first_norm_bias: float32 [768], replicated, may hold values from -2 to 2
- second_norm_gain: float32 [768], replicated, may hold values from 0.5 to 1.5
- second_norm_bias: float32 [768], replicated, may hold values from -2 to 2
- cotangent: bfloat16 [2, 4096, 768], P('shard', 'context'), may hold values from -6 to 6
Outputs:
- outputs: float32 [2, 4096, 768], P('shard', 'context')
- block_input_gradient: float32 [2, 4096, 768], P('shard', 'context')
- grad_qkv: float32 [768, 3, 768], P(('shard', 'context'), None, 'tensor')
- grad_out: float32 [768, 768], P('tensor', ('shard', 'context'))
- grad_fc: float32 [768, 3072], P(('shard', 'context'), 'tensor')
- grad_down: float32 [3072, 768], P('tensor', ('shard', 'context'))
- grad_qv_bias: float32 [2, 768], P(None, 'tensor')
- grad_out_bias: float32 [768], replicated
- grad_fc_bias: float32 [3072], P('tensor')
- grad_down_bias: float32 [768], replicated
- first_norm_gain_gradient: float32 [768], replicated
- grad_ln1_bias: float32 [768], replicated
- second_norm_gain_gradient: float32 [768], replicated
- grad_ln2_bias: float32 [768], replicated
The draws below stay inside these ranges and needn't reach their ends.
Inputs may be any that keep to these rules, and one draw needn't show every extreme that they name: `segments`: in each sequence the document numbers start at 0, never fall, rise by one at each new document and end at 4 or below. Of the 1 sequence of each index of shard, one, chosen by the seed, holds five documents 0 to 4: documents 0 and 1 lie within the first 1024 positions, 3 and 4 within the last 1024, and document 2 begins within the first 1024 positions and ends within the last 1024. In the other sequences every document but the last has between max(1, min(200, 256)) and min(2000, 2048) tokens, and the last takes the rest.
All inputs are finite; a program needn't handle non-finite values.
Results may differ from the reference program's by a relative error of at most 0.02.
Values may be sent and summed in bfloat16 or wider, within the bound.
No kernel may reach another device: no remote copies, remote signals or barrier semaphores. Data moves between devices by JAX's collectives and lax.ppermute only.
A program may use at most 192 MiB of HBM per device.

```python
from functools import partial
import jax
import jax.numpy as jnp
from jax import lax

D = 768
FF = 3072
HD = 64
SEQ_DEV = 1
LENGTH = 4096
BATCH = 2
N_SHARD = 2
N_CONTEXT = 4


def draw_segments(key, part):
    tok = LENGTH // N_CONTEXT
    half = tok // 2
    keys = jax.random.split(key, 6)
    rows = (BATCH, 1)
    first_cut = jax.random.randint(keys[0], rows, 1, half)
    second_cut = jax.random.randint(keys[1], rows, half, tok)
    third_cut = jax.random.randint(keys[2], rows, LENGTH - tok, LENGTH - half)
    fourth_cut = jax.random.randint(keys[3], rows, LENGTH - half, LENGTH - 1)
    position = jnp.arange(LENGTH, dtype=jnp.int32)[None, :]
    spanning = (position >= first_cut).astype(jnp.int32) + (position >= second_cut).astype(jnp.int32)
    spanning = spanning + (position >= third_cut).astype(jnp.int32) + (position >= fourth_cut).astype(jnp.int32)
    shortest = max(1, min(200, LENGTH // 16))
    longest = max(shortest + 1, min(2000, LENGTH // 2) + 1)
    count = LENGTH // shortest + 1
    doc_sizes = jax.random.randint(keys[4], (BATCH, count), shortest, longest)
    ends = jnp.cumsum(doc_sizes, axis=1).astype(jnp.int32)
    packed = jnp.sum((position[:, :, None] >= ends[:, None, :]).astype(jnp.int32), axis=-1).astype(jnp.int32)
    packed = jnp.minimum(packed, 4).astype(jnp.int32)
    chosen = jax.random.randint(keys[5], (N_SHARD,), 0, SEQ_DEV)
    sequence = jnp.arange(BATCH, dtype=jnp.int32)
    picked = sequence % SEQ_DEV == chosen[sequence // SEQ_DEV]
    return jnp.where(picked[:, None], spanning, packed).astype(jnp.int32)


def block_scale(rng, dims, pieces, low, top_value):
    factor_of, own = 1.0, jax.random.fold_in(rng, 6)
    for dim, blocks in pieces:
        draws = jnp.exp(jax.random.uniform(jax.random.fold_in(own, dim), (blocks,), jnp.float32, low / len(pieces), top_value / len(pieces)))
        factor_of = factor_of * jnp.repeat(draws, dims[dim] // blocks).reshape([-1 if axis == dim else 1 for axis in range(len(dims))])
    return factor_of


def normal_values(key, extent, deviation, limit, shards=(), kind=jnp.bfloat16):
    entries = deviation * jax.random.normal(key, extent, jnp.float32)
    if shards:
        entries = entries * block_scale(key, extent, shards, -0.22, 0.18)
    return jnp.clip(entries, -limit, limit).astype(kind)


def setup_inputs(seed: int = 0) -> dict:
    key_list = jax.random.split(jax.random.key(seed), 16)
    return {
        "inputs": normal_values(key_list[0], (BATCH, LENGTH, D), 1.0, 6.0, ((0, 2), (1, 4))),
        "segments": draw_segments(jax.random.fold_in(key_list[15], 71), 0),
        "w_qkv": normal_values(key_list[2], (D, 3, D), D ** -0.5, 0.21875, ((0, 2), (2, 4))),
        "w_out": normal_values(key_list[3], (D, D), (max(4, D // 192)) ** -0.5, 3.0, ((0, 4), (1, 2))),
        "w_fc": normal_values(key_list[4], (D, FF), D ** -0.5, 0.21875, ((0, 2), (1, 4))),
        "w_down": normal_values(key_list[5], (FF, D), FF ** -0.5, 0.109375, ((0, 4), (1, 2))),
        "b_qv": normal_values(key_list[6], (2, D), 0.5, 3.0, ((1, 4),), jnp.float32),
        "b_out": normal_values(key_list[7], (D,), 0.3, 2.0, (), jnp.float32),
        "b_fc": normal_values(key_list[8], (FF,), 0.5, 3.0, ((0, 4),), jnp.float32),
        "b_down": normal_values(key_list[9], (D,), 0.3, 2.0, (), jnp.float32),
        "first_norm_gain": jnp.clip(1.0 + 0.1 * jax.random.normal(key_list[10], (D,), jnp.float32), 0.5, 1.5),
        "first_norm_bias": normal_values(key_list[11], (D,), 0.3, 2.0, (), jnp.float32),
        "second_norm_gain": jnp.clip(1.0 + 0.1 * jax.random.normal(key_list[12], (D,), jnp.float32), 0.5, 1.5),
        "second_norm_bias": normal_values(key_list[13], (D,), 0.3, 2.0, (), jnp.float32),
        "cotangent": normal_values(key_list[14], (BATCH, LENGTH, D), 1.0, 6.0, ((0, 2), (1, 4))),
    }


EPS = 1e-05
NEG = -1e+30
HIGH = lax.Precision.HIGHEST

@jax.custom_vjp
def low(v):
    return lax.optimization_barrier(v.astype(jnp.bfloat16)).astype(jnp.float32)

@jax.custom_vjp
def low_back(v):
    return v

def low_keep(v):
    return (low(v), None)

def low_pass(kept, grad):
    return (grad,)

def back_keep(v):
    return (v, None)

def back_low(kept, grad):
    return (low(grad),)
low.defvjp(low_keep, low_pass)
low_back.defvjp(back_keep, back_low)

def layer_norm(value, gain, shift):
    mean = lax.optimization_barrier(jnp.mean(value, axis=-1, keepdims=True))
    centred = value - mean
    return centred * lax.rsqrt(lax.optimization_barrier(jnp.mean(centred * centred, axis=-1, keepdims=True)) + EPS) * gain + shift

def attention(query, keys, values, segments):
    batch, length, cols = query.shape
    heads = cols // HD
    scale = float(HD) ** (-0.5)
    q_four = query.reshape(batch, length, heads, HD)
    k_four = keys.reshape(batch, length, heads, HD)
    v_four = values.reshape(batch, length, heads, HD)
    qblock = min(256, length)
    count = length // qblock
    key_pos = jnp.arange(length, dtype=jnp.int32)

    def one_block(q_blk, start):
        q_pos = start + jnp.arange(qblock, dtype=jnp.int32)
        q_seg = lax.dynamic_slice_in_dim(segments, start, qblock, 1)
        scores = low_back(jnp.einsum('bqhd,bkhd->bhqk', q_blk, k_four, precision=HIGH) * scale)
        causal = key_pos[None, :] <= q_pos[:, None]
        allowed = (causal[None] & (segments[:, None, :] == q_seg[:, :, None]))[:, None]
        scores = jnp.where(allowed, scores, NEG)
        probs = low(jax.nn.softmax(scores, axis=-1))
        return jnp.einsum('bhqk,bkhd->bqhd', probs, v_four, precision=HIGH)
    checked = jax.checkpoint(one_block)
    blocks_q = q_four.reshape(batch, count, qblock, heads, HD).transpose(1, 0, 2, 3, 4)
    starts = jnp.arange(count, dtype=jnp.int32) * qblock
    result = lax.map(lambda pair: checked(pair[0], pair[1]), (blocks_q, starts))
    return result.transpose(1, 0, 2, 3, 4).reshape(batch, length, cols)

def forward(segments, residual_stream, w_qkv, w_out, w_fc, w_down, b_qv, b_out, b_fc, b_down, first_norm_gain, first_norm_bias, second_norm_gain, second_norm_bias):
    first_normalized_input = low(layer_norm(residual_stream, first_norm_gain, first_norm_bias))
    projected = jnp.einsum('bld,dgc->blgc', first_normalized_input, w_qkv, precision=HIGH)
    query = low_back(low(projected[:, :, 0] + b_qv[0]))
    keys = low_back(low(projected[:, :, 1]))
    values = low_back(low(projected[:, :, 2] + b_qv[1]))
    attended = low_back(low(attention(query, keys, values, segments)))
    middle_residual = residual_stream + low_back(jnp.einsum('blc,cd->bld', attended, w_out, precision=HIGH)) + b_out
    second_normalized_input = low(layer_norm(middle_residual, second_norm_gain, second_norm_bias))
    hidden_pre = low_back(jnp.einsum('bld,df->blf', second_normalized_input, w_fc, precision=HIGH) + b_fc)
    act = low(jax.nn.gelu(hidden_pre, approximate=True))
    return middle_residual + jnp.einsum('blf,fd->bld', act, w_down, precision=HIGH) + b_down

def reference(inputs, segments, w_qkv, w_out, w_fc, w_down, b_qv, b_out, b_fc, b_down, first_norm_gain, first_norm_bias, second_norm_gain, second_norm_bias, cotangent):
    floats = tuple((item.astype(jnp.float32) for item in (inputs, w_qkv, w_out, w_fc, w_down, b_qv, b_out, b_fc, b_down, first_norm_gain, first_norm_bias, second_norm_gain, second_norm_bias)))
    outputs, backward = jax.vjp(partial(forward, segments), *floats)
    grads = backward(cotangent.astype(jnp.float32))
    return (outputs, grads[0], grads[1], grads[2], grads[3], grads[4], grads[5], grads[6], grads[7], grads[8], grads[9], grads[10], grads[11], grads[12])
```

```python
import functools

import jax
import jax.numpy as jnp
from jax import lax
from jax.experimental import pallas as pl
from jax.experimental.pallas import tpu as pltpu
from jax.sharding import PartitionSpec as P

HD = 64
EPS = 1e-05
NEG = -1e30
SCALE = float(HD) ** -0.5
VMEM_LIMIT = 56 * 1024 * 1024
GROUPS = (3,)
BK_F, BQ_F = 512, 512
BK_B, BQ_B = 512, 512
f32 = jnp.float32
bf16 = jnp.bfloat16
VM = pl.BlockSpec(memory_space=pltpu.VMEM)
SM = pl.BlockSpec(memory_space=pltpu.SMEM)
HBM = pl.BlockSpec(memory_space=pl.ANY)


def nn(a, b):
    return lax.dot_general(a, b, (((1,), (0,)), ((), ())), preferred_element_type=f32)


def tn(a, b):
    return lax.dot_general(a, b, (((0,), (0,)), ((), ())), preferred_element_type=f32)


def nt(a, b):
    return lax.dot_general(a, b, (((1,), (1,)), ((), ())), preferred_element_type=f32)


def params():
    return pltpu.CompilerParams(vmem_limit_bytes=VMEM_LIMIT)


def shape(dims, kind=bf16):
    return jax.ShapeDtypeStruct(dims, kind)


def halves(core, width):
    half = width // 2
    own = pl.ds(pl.multiple_of(core * half, 128), half)
    other = pl.ds(pl.multiple_of((1 - core) * half, 128), half)
    return own, other


def norm(value):
    centred = value - jnp.mean(value, axis=-1, keepdims=True)
    inverse = lax.rsqrt(jnp.mean(centred * centred, axis=-1, keepdims=True) + EPS)
    return centred * inverse, inverse


def norm_gradient(grad, normed, inverse, gain):
    scaled = grad * gain
    return inverse * (
        scaled
        - jnp.mean(scaled, axis=-1, keepdims=True)
        - normed * jnp.mean(scaled * normed, axis=-1, keepdims=True)
    )


def project_kernel(sc, x, w_own, w_other, b_qv, gain, shift, low, qt, kt, vt):
    own, other = halves(sc[2], x.shape[1])
    cols = qt.shape[0]
    normed, _ = norm(x[...].astype(f32))
    low[...] = (normed * gain[...] + shift[...]).astype(bf16)
    projected = nn(low[:, own], w_own[...]) + nn(low[:, other], w_other[...])
    qt[...] = ((projected[:, :cols] + b_qv[0:1, :]) * SCALE).T.astype(bf16)
    kt[...] = projected[:, cols : 2 * cols].T.astype(bf16)
    vt[...] = (projected[:, 2 * cols :] + b_qv[1:2, :]).T.astype(bf16)


def project(place, x, w_own, w_other, b_qv, gain, shift):
    tok, width = x.shape
    cols = b_qv.shape[1]
    rows = min(256, tok)
    fixed = lambda a: pl.BlockSpec(a.shape, lambda i: (0,) * a.ndim)
    across = pl.BlockSpec((cols, rows), lambda i: (0, i))
    return pl.pallas_call(
        project_kernel,
        grid=(tok // rows,),
        in_specs=[SM, pl.BlockSpec((rows, width), lambda i: (i, 0))]
        + [fixed(a) for a in (w_own, w_other, b_qv, gain, shift)],
        out_specs=[pl.BlockSpec((rows, width), lambda i: (i, 0)), across, across, across],
        out_shape=[shape((tok, width))] + [shape((cols, tok))] * 3,
        compiler_params=params(),
        name="project",
    )(place, x, w_own, w_other, b_qv, gain, shift)


def key_loop(sc, i, step, carry):
    lo, full, diag, end = sc[4 * i + 4], sc[4 * i + 5], sc[4 * i + 6], sc[4 * i + 7]
    carry = lax.fori_loop(lo, full, functools.partial(step, True), carry)
    carry = lax.fori_loop(full, diag, functools.partial(step, False), carry)
    return lax.fori_loop(diag, end, functools.partial(step, True), carry)


def tile_mask(j, bk, bq, start, qpos):
    kpos = j * bk + lax.broadcasted_iota(jnp.int32, (bk, bq), 0)
    return (kpos >= start) & (kpos <= qpos)


def load_keys(sc, kv, held, sems):
    if len(kv) == 1:
        copies = [pltpu.make_async_copy(kv[0], held, sems.at[0])]
    else:
        rows = kv[0].shape[0]
        copies = [
            pltpu.make_async_copy(
                kv[n], held.at[sc[1] ^ (n % 4), pl.ds((n // 4) * rows, rows), :], sems.at[n]
            )
            for n in range(8)
        ]
    for copy in copies:
        copy.start()
    for copy in copies:
        copy.wait()


def attend_kernel(first_head, heads, bk, bq, parts, n_kv, sc, qt, st, *refs):
    kv, refs = refs[:n_kv], refs[n_kv:]
    lse, ot, out, (held, acc, sems) = refs[0], refs[1], refs[2 : 2 + parts], refs[2 + parts :]
    i = pl.program_id(0)
    per = held.shape[2] // bk
    cols = heads * HD
    start = st[...]
    qpos = sc[0] + i * bq + lax.broadcasted_iota(jnp.int32, (1, bq), 1)

    @pl.when(i == 0)
    def _():
        load_keys(sc, kv, held, sems)

    acc[...] = jnp.zeros_like(acc)

    def step(masked, j, carry):
        r = j // per
        off = pl.multiple_of((j % per) * bk, bk)
        new = []
        if masked:
            ok = tile_mask(j, bk, bq, start, qpos)
        for h in range(heads):
            m, l = carry[h]
            hs = slice(h * HD, (h + 1) * HD)
            s = tn(
                held[r, hs, pl.ds(off, bk)],
                qt[(first_head + h) * HD : (first_head + h + 1) * HD, :],
            )
            if masked:
                s = jnp.where(ok, s, NEG)
            m2 = jnp.maximum(m, jnp.max(s, axis=0, keepdims=True))
            p = jnp.exp(s - m2)
            al = jnp.exp(m - m2)
            l = l * al + jnp.sum(p, axis=0, keepdims=True)
            v = held[r, cols + h * HD : cols + (h + 1) * HD, pl.ds(off, bk)]
            acc[hs, :] = acc[hs, :] * al + nn(v, p.astype(bf16))
            new.append((m2, l))
        return tuple(new)

    one = (jnp.full((1, bq), NEG, f32), jnp.zeros((1, bq), f32))
    res = key_loop(sc, i, step, (one,) * heads)
    here = pl.ds(pl.multiple_of(i * bq, bq), bq)
    for h in range(heads):
        m, l = res[h]
        ot[h * HD : (h + 1) * HD, here] = (acc[h * HD : (h + 1) * HD, :] / l).astype(bf16)
        lse[h : h + 1, :] = m + jnp.log(l)

    @pl.when(i == pl.num_programs(0) - 1)
    def _():
        send_parts(sc[3], ot, out)


def send_parts(me, source, out):
    parts, size = len(out), out[0].shape[1]
    for d in range(parts):
        if size % 128 == 0:
            at = pl.multiple_of(lax.rem(me + d, parts) * size, 128)
            out[d][...] = source[:, pl.ds(at, size)].astype(out[d].dtype)
        else:
            for n in range(parts):

                @pl.when(lax.rem(me + d, parts) == n)
                def _():
                    out[d][...] = source[:, n * size : (n + 1) * size].astype(out[d].dtype)


def take_parts(me, rows, parts, target):
    size = parts[0].shape[1]
    for d in range(len(parts)):
        if size % 128 == 0:
            at = pl.multiple_of(lax.rem(me + d, len(parts)) * size, 128)
            target[:, pl.ds(at, size)] = parts[d][rows, :]
        else:
            for n in range(len(parts)):

                @pl.when(lax.rem(me + d, len(parts)) == n)
                def _():
                    target[:, n * size : (n + 1) * size] = parts[d][rows, :]


def attend(scalars, starts, qt, kv, first_head, heads, bk, bq, parts):
    tok = qt.shape[1]
    cols = heads * HD
    runs = kv[0].shape[0] if len(kv) == 1 else 4
    bk, bq = min(bk, tok), min(bq, tok)
    whole = lambda a, b: pl.BlockSpec((a, b), lambda i: (0, 0))
    return pl.pallas_call(
        functools.partial(attend_kernel, first_head, heads, bk, bq, parts, len(kv)),
        grid=(tok // bq,),
        in_specs=[
            SM,
            pl.BlockSpec((qt.shape[0], bq), lambda i: (0, i)),
            pl.BlockSpec((1, bq), lambda i: (0, i)),
        ]
        + [HBM] * len(kv),
        out_specs=[pl.BlockSpec((heads, bq), lambda i: (0, i)), whole(cols, tok)]
        + [whole(cols, tok // parts)] * parts,
        scratch_shapes=[
            pltpu.VMEM((runs, 2 * cols, tok), bf16),
            pltpu.VMEM((cols, bq), f32),
            pltpu.SemaphoreType.DMA((len(kv),)),
        ],
        out_shape=[shape((heads, tok), f32), shape((cols, tok))]
        + [shape((cols, tok // parts))] * parts,
        compiler_params=params(),
        name="attend",
    )(scalars(bk, bq), qt, starts, *kv)


def attend_back_kernel(first_head, heads, bk, bq, parts, n_kv, sc, qt, st, lse, ot, *refs):
    do_parts, refs = refs[:parts], refs[parts:]
    kv, refs = refs[:n_kv], refs[n_kv:]
    n_out = 1 if n_kv == 1 else 4
    dq, dkv, (held, acc, dqa, do_all, sems) = (
        refs[:parts],
        refs[parts : parts + n_out],
        refs[parts + n_out :],
    )
    i = pl.program_id(0)
    per = held.shape[2] // bk
    cols = heads * HD
    start = st[...]
    qpos = sc[0] + i * bq + lax.broadcasted_iota(jnp.int32, (1, bq), 1)
    here = pl.ds(pl.multiple_of(i * bq, bq), bq)

    @pl.when(i == 0)
    def _():
        acc[...] = jnp.zeros_like(acc)
        dqa[...] = jnp.zeros_like(dqa)
        take_parts(sc[3], slice(first_head * HD, (first_head + heads) * HD), do_parts, do_all)
        load_keys(sc, kv, held, sems)

    delta = [
        jnp.sum(
            do_all[h * HD : (h + 1) * HD, here].astype(f32)
            * ot[h * HD : (h + 1) * HD, :].astype(f32),
            axis=0,
            keepdims=True,
        )
        for h in range(heads)
    ]

    def step(masked, j, carry):
        r = j // per
        off = pl.multiple_of((j % per) * bk, bk)
        if masked:
            ok = tile_mask(j, bk, bq, start, qpos)
        for h in range(heads):
            hs = slice(h * HD, (h + 1) * HD)
            vs = slice(cols + h * HD, cols + (h + 1) * HD)
            k = held[r, hs, pl.ds(off, bk)]
            v = held[r, vs, pl.ds(off, bk)]
            q = qt[(first_head + h) * HD : (first_head + h + 1) * HD, :]
            do = do_all[hs, here]
            s = tn(k, q) - lse[h : h + 1, :]
            if masked:
                s = jnp.where(ok, s, NEG)
            p = jnp.exp(s)
            ds = (p * (tn(v, do) - delta[h])).astype(bf16)
            acc[r, vs, pl.ds(off, bk)] += nt(do, p.astype(bf16))
            acc[r, hs, pl.ds(off, bk)] += nt(q, ds)
            dqa[hs, here] += nn(k, ds)
        return carry

    key_loop(sc, i, step, 0)

    @pl.when(i == pl.num_programs(0) - 1)
    def _():
        dqa[...] = dqa[...] * SCALE
        send_parts(sc[3], dqa, dq)
        if n_out == 1:
            dkv[0][...] = acc[...].astype(bf16)
        else:
            for target, pair, rows in (
                (0, (0, 2), slice(0, cols)),
                (1, (1, 3), slice(0, cols)),
                (2, (0, 1), slice(cols, 2 * cols)),
                (3, (2, 3), slice(cols, 2 * cols)),
            ):
                for n in range(2):
                    dkv[target][n] = acc[sc[1] ^ pair[n], rows, :].astype(bf16)


def attend_back(scalars, starts, qt, lse, ot, do_parts, kv, first_head, heads, bk, bq):
    tok = qt.shape[1]
    cols = heads * HD
    parts = len(do_parts)
    runs = kv[0].shape[0] if len(kv) == 1 else 4
    bk, bq = min(bk, tok), min(bq, tok)
    whole = lambda *dims: pl.BlockSpec(dims, lambda i: (0,) * len(dims))
    out_kv = [(runs, 2 * cols, tok)] if len(kv) == 1 else [(2, cols, tok)] * 4
    return pl.pallas_call(
        functools.partial(attend_back_kernel, first_head, heads, bk, bq, parts, len(kv)),
        grid=(tok // bq,),
        in_specs=[
            SM,
            pl.BlockSpec((qt.shape[0], bq), lambda i: (0, i)),
            pl.BlockSpec((1, bq), lambda i: (0, i)),
            pl.BlockSpec((heads, bq), lambda i: (0, i)),
            pl.BlockSpec((cols, bq), lambda i: (0, i)),
        ]
        + [whole(*d.shape) for d in do_parts]
        + [HBM] * len(kv),
        out_specs=[whole(cols, tok // parts)] * parts + [whole(*d) for d in out_kv],
        scratch_shapes=[
            pltpu.VMEM((runs, 2 * cols, tok), bf16),
            pltpu.VMEM((runs, 2 * cols, tok), f32),
            pltpu.VMEM((cols, tok), f32),
            pltpu.VMEM((cols, tok), bf16),
            pltpu.SemaphoreType.DMA((len(kv),)),
        ],
        out_shape=[shape((cols, tok // parts))] * parts + [shape(d) for d in out_kv],
        compiler_params=params(),
        name="attend_back",
    )(scalars(bk, bq), qt, starts, lse, ot, *do_parts, *kv)


ROOT = 0.7978845608028654


def middle_kernel(n_att, parts, sc, *refs):
    att, refs = refs[:n_att], refs[n_att:]
    (x, cot, wo_own, wo_other, fc_own, fc_other, dn_own, dn_other, b_out, b_fc, b_down, gain, shift) = refs[:13]
    refs = refs[13:]
    outputs, grad_mid, sums, fc_sums = refs[:4]
    d_att, (g_own, g_other, go_own, go_other) = refs[4 : 4 + parts], refs[4 + parts : 8 + parts]
    mid, att_t, low, low_t, cot_t, mlp, back = refs[8 + parts :]
    d = pl.program_id(0)
    width = x.shape[1]
    own, other = halves(sc[2], width)
    half = width // 2
    ffw = fc_own.shape[2]

    @pl.when(d == 0)
    def _():
        group = n_att // parts
        row = 0
        for part in range(parts):
            for g in range(group):
                piece = att[part * group + g]
                att_t[row : row + piece.shape[0], :] = piece[...]
                row += piece.shape[0]
        att_low = att_t[...].T
        mid[:, own] = nn(att_low, wo_own[...])
        mid[:, other] = nn(att_low, wo_other[...])
        mid[...] = x[...].astype(f32) + mid[...] + b_out[...]
        normed, _ = norm(mid[...])
        low[...] = (normed * gain[...] + shift[...]).astype(bf16)
        low_t[...] = low[...].T
        cot_t[...] = cot[...].T
        mlp[...] = jnp.zeros_like(mlp)
        back[...] = jnp.zeros_like(back)

    own_rows = pl.ds(pl.multiple_of(sc[2] * half, half), half)
    other_rows = pl.ds(pl.multiple_of((1 - sc[2]) * half, half), half)
    u = nn(low[:, own], fc_own[0]) + nn(low[:, other], fc_other[0]) + b_fc[0]
    t = jnp.tanh(ROOT * (u + 0.044715 * (u * u * u)))
    act = (0.5 * u * (1.0 + t)).astype(bf16)
    slope = 0.5 * (1.0 + t) + (0.5 * ROOT) * u * (1.0 - t * t) * (1.0 + 0.134145 * (u * u))
    d_act = nt(cot[:, own], dn_own[0]) + nt(cot[:, other], dn_other[0])
    dh = (d_act * slope).astype(bf16)
    mlp[:, own] += nn(act, dn_own[0])
    mlp[:, other] += nn(act, dn_other[0])
    back[:, own] += nt(dh, fc_own[0])
    back[:, other] += nt(dh, fc_other[0])
    g_own[0, :, :ffw] = nn(low_t[own_rows, :], dh).astype(bf16)
    g_other[0, :, :ffw] = nn(low_t[other_rows, :], dh).astype(bf16)
    g_own[0, :, ffw:] = nn(cot_t[own_rows, :], act).astype(bf16)
    g_other[0, :, ffw:] = nn(cot_t[other_rows, :], act).astype(bf16)
    fc_sums[0] = jnp.sum(dh.astype(f32), axis=0, keepdims=True)

    @pl.when(d == parts - 1)
    def _():
        normed, inverse = norm(mid[...])
        outputs[...] = (mid[...] + mlp[...] + b_down[...]).astype(bf16)
        upper = cot[...].astype(f32)
        grad = back[...]
        down = upper + norm_gradient(grad, normed, inverse, gain[...])
        grad_mid[...] = down
        sums[0:1, :] = jnp.sum(down, axis=0, keepdims=True)
        sums[1:2, :] = jnp.sum(upper, axis=0, keepdims=True)
        sums[2:3, :] = jnp.sum(grad * normed, axis=0, keepdims=True)
        sums[3:4, :] = jnp.sum(grad, axis=0, keepdims=True)
        low[...] = down.astype(bf16)
        low_t[...] = low[...].T
        cols = att_t.shape[0] // parts
        go_own[...] = nt(low_t[own_rows, :], att_t[...]).astype(bf16)
        go_other[...] = nt(low_t[other_rows, :], att_t[...]).astype(bf16)
        for part in range(parts):
            rows = slice(part * cols, (part + 1) * cols)
            d_att[part][...] = (
                nt(wo_own[rows, :], low[:, own]) + nt(wo_other[rows, :], low[:, other])
            ).astype(bf16)


def middle(place, att, x, cot, wo, fc, dn, b_out, b_fc, b_down, gain, shift):
    parts, half, ffw = fc[0].shape
    sub, width = x.shape
    cols = wo[0].shape[0] // parts
    whole = lambda *dims: pl.BlockSpec(dims, lambda i: (0,) * len(dims))
    each = lambda *dims: pl.BlockSpec((1,) + dims, lambda i: (i, 0, 0))
    once = lambda a: whole(*a.shape)
    return pl.pallas_call(
        functools.partial(middle_kernel, len(att), parts),
        grid=(parts,),
        in_specs=[SM]
        + [once(a) for a in att]
        + [once(x), once(cot), once(wo[0]), once(wo[1])]
        + [each(half, ffw)] * 2
        + [each(ffw, half)] * 2
        + [once(b_out), each(1, ffw), once(b_down), once(gain), once(shift)],
        out_specs=[whole(sub, width), whole(sub, width), whole(4, width), each(1, ffw)]
        + [whole(cols, sub)] * parts
        + [each(half, 2 * ffw)] * 2
        + [whole(half, parts * cols)] * 2,
        out_shape=[
            shape((sub, width)),
            shape((sub, width), f32),
            shape((4, width), f32),
            shape((parts, 1, ffw), f32),
        ]
        + [shape((cols, sub))] * parts
        + [shape((parts, half, 2 * ffw))] * 2
        + [shape((half, parts * cols))] * 2,
        scratch_shapes=[
            pltpu.VMEM((sub, width), f32),
            pltpu.VMEM((parts * cols, sub), bf16),
            pltpu.VMEM((sub, width), bf16),
            pltpu.VMEM((width, sub), bf16),
            pltpu.VMEM((width, sub), bf16),
            pltpu.VMEM((sub, width), f32),
            pltpu.VMEM((sub, width), f32),
        ],
        compiler_params=params(),
        name="middle",
    )(place, *att, x, cot, wo[0], wo[1], fc[0], fc[1], dn[0], dn[1], b_out, b_fc, b_down, gain, shift)


def last_kernel(parts, pieces, sc, *refs):
    grads, refs = refs[: parts * pieces], refs[parts * pieces :]
    w_own, w_other, x, grad_mid, gain, out, sums, back_t, stacked = refs
    half = w_own.shape[1]
    own_rows = pl.ds(pl.multiple_of(sc[2] * half, half), half)
    other_rows = pl.ds(pl.multiple_of((1 - sc[2]) * half, half), half)
    for part in range(parts):
        row = 0
        for n in range(pieces):
            piece = grads[part * pieces + n]
            stacked[row : row + piece.shape[0], :] = piece[...]
            row += piece.shape[0]
        mine, theirs = nn(w_own[part], stacked[...]), nn(w_other[part], stacked[...])
        if part == 0:
            back_t[own_rows, :], back_t[other_rows, :] = mine, theirs
        else:
            back_t[own_rows, :] += mine
            back_t[other_rows, :] += theirs
    back = back_t[...].T
    normed, inverse = norm(x[...].astype(f32))
    out[...] = (grad_mid[...] + norm_gradient(back, normed, inverse, gain[...])).astype(bf16)
    sums[0:1, :] = jnp.sum(back * normed, axis=0, keepdims=True)
    sums[1:2, :] = jnp.sum(back, axis=0, keepdims=True)


def last(place, grads, pieces, w, x, grad_mid, gain):
    parts = w[0].shape[0]
    sub, width = x.shape
    return pl.pallas_call(
        functools.partial(last_kernel, parts, pieces),
        in_specs=[SM] + [VM] * (len(grads) + 5),
        out_specs=[VM, VM],
        out_shape=[shape((sub, width)), shape((2, width), f32)],
        scratch_shapes=[pltpu.VMEM((width, sub), f32), pltpu.VMEM((w[0].shape[2], sub), bf16)],
        compiler_params=params(),
        name="last",
    )(place, *grads, w[0], w[1], x, grad_mid, gain)


def body(
    n_shard,
    n_context,
    n_tensor,
    inputs,
    segments,
    w_qkv,
    w_out,
    w_fc,
    w_down,
    b_qv,
    b_out,
    b_fc,
    b_down,
    first_norm_gain,
    first_norm_bias,
    second_norm_gain,
    second_norm_bias,
    cotangent,
):
    _, tok, width = inputs.shape
    length = segments.shape[1]
    half, _, cols = w_qkv.shape
    heads = cols // HD
    ffw = w_fc.shape[1]
    sub = tok // n_tensor
    context = lax.axis_index("context")
    tensor = lax.axis_index("tensor")
    core = lax.axis_index("shard")
    first = context * tok
    place = jnp.stack([first, context, core, tensor]).astype(jnp.int32)
    grouped = n_context == 4
    x = inputs[0]
    cot = cotangent[0]
    row = lambda v: v[None, :]

    swap = lambda v: lax.ppermute(v, "shard", [(0, 1), (1, 0)])
    along_x = lambda v: lax.ppermute(v, "context", [(0, 1), (1, 0), (2, 3), (3, 2)])
    along_y = lambda v: lax.ppermute(v, "context", [(0, 2), (2, 0), (1, 3), (3, 1)])
    shift_by = lambda v, d: lax.ppermute(
        v, "tensor", [(s, (s + d) % n_tensor) for s in range(n_tensor)]
    )

    def gather_line(v):
        right, left = [v], [v]
        for s in range(1, n_tensor):
            right.append(
                lax.ppermute(
                    right[-1], "tensor", [(d, d + 1) for d in range(s - 1, n_tensor - 1)]
                )
            )
            left.append(
                lax.ppermute(left[-1], "tensor", [(d, d - 1) for d in range(1, n_tensor - s + 1)])
            )
        return [v] + [right[d] + left[n_tensor - d] for d in range(1, n_tensor)]

    def scatter_line(pieces):
        right = left = None
        for s in range(1, n_tensor):
            r, l = pieces[s], pieces[n_tensor - s]
            if s > 1:
                r = (r.astype(f32) + right.astype(f32)).astype(bf16)
                l = (l.astype(f32) + left.astype(f32)).astype(bf16)
            right = lax.ppermute(r, "tensor", [(d, d + 1) for d in range(s)])
            left = lax.ppermute(
                l, "tensor", [(n_tensor - 1 - d, n_tensor - 2 - d) for d in range(s)]
            )
        return pieces[0].astype(f32) + right.astype(f32) + left.astype(f32)

    def scatter_context(v):
        if not grouped:
            return lax.psum_scatter(v, "context", scatter_dimension=1, tiled=True)
        size = v.shape[1] // 4
        block = lambda n: lax.dynamic_slice_in_dim(v, (context ^ n) * size, size, 1)
        own, by_x, by_y, by_both = (block(n) for n in range(4))
        cut = (v.shape[2] // 256) * 128
        lo = lambda a: a[:, :, :cut]
        hi = lambda a: a[:, :, cut:]
        r = along_x(jnp.stack([lo(by_x), lo(by_both)])).astype(f32)
        s = along_y(jnp.stack([hi(by_y), hi(by_both)])).astype(f32)
        r2 = along_y((lo(by_y).astype(f32) + r[1]).astype(bf16)).astype(f32)
        s2 = along_x((hi(by_x).astype(f32) + s[1]).astype(bf16)).astype(f32)
        return jnp.concatenate(
            [lo(own).astype(f32) + r[0] + r2, hi(own).astype(f32) + s[0] + s2], axis=2
        )

    def scatter_weights(mine, theirs):
        both = (mine.astype(f32) + swap(theirs).astype(f32)).astype(bf16)
        return scatter_context(both)

    bounds = [jnp.sum((segments[0] < d).astype(jnp.int32)) for d in range(1, 5)]
    seg = lax.dynamic_slice_in_dim(segments[0], first, tok, 0)
    starts = jnp.zeros_like(seg)
    for d in range(1, 5):
        starts = jnp.where(seg == d, bounds[d - 1], starts)

    def scalars(bk, bq):
        count = tok // bq
        begin = starts.reshape(count, bq)
        base = first + jnp.arange(count, dtype=jnp.int32) * bq
        lo = begin[:, 0] // bk
        diag = base // bk
        end = (base + bq + bk - 1) // bk
        full = jnp.minimum(jnp.maximum((begin[:, -1] + bk - 1) // bk, lo), diag)
        table = jnp.stack([lo, full, diag, end], axis=1).reshape(-1)
        return jnp.concatenate([place, table.astype(jnp.int32)])

    qkv_own = w_qkv.reshape(half, 3 * cols)
    low_one, qt, kt, vt = project(
        place,
        x,
        qkv_own,
        swap(qkv_own),
        b_qv,
        row(first_norm_gain),
        row(first_norm_bias),
    )

    kv = []
    head = 0
    for g in GROUPS:
        rows = slice(head * HD, (head + g) * HD)
        head += g
        k, v = kt[rows], vt[rows]
        if grouped:
            kx, vy, ky, vx = along_x(k), along_y(v), along_y(k), along_x(v)
            kv.append([k, kx, ky, along_y(kx), v, vx, vy, along_x(vy)])
        else:
            kv.append([lax.all_gather(jnp.concatenate([k, v], axis=0), "context", axis=0)])

    def gather_weights(w):
        own = jnp.stack(gather_line(w))
        return own, swap(own)

    wo = tuple(w.reshape(n_tensor * cols, half) for w in gather_weights(w_out))
    fc = gather_weights(w_fc)
    dn = gather_weights(w_down)

    saved = []
    att = [[] for _ in range(n_tensor)]
    head = 0
    for g, held in zip(GROUPS, kv):
        lse, ot, *out = attend(scalars, row(starts), qt, held, head, g, BK_F, BQ_F, n_tensor)
        saved.append((lse, ot))
        att[0].append(out[0])
        for d in range(1, n_tensor):
            att[d].append(shift_by(out[d], d))
        head += g

    x_sub = lax.dynamic_slice_in_dim(x, tensor * sub, sub, 0)
    cot_sub = lax.dynamic_slice_in_dim(cot, tensor * sub, sub, 0)
    qkv = gather_weights(qkv_own)
    fc_bias = [row(b_fc)[None]]
    fc_bias = jnp.concatenate(gather_line(row(b_fc)[None]), axis=0)
    outputs_sub, grad_mid, sums, fc_sums, *rest = middle(
        place,
        [piece for part in att for piece in part],
        x_sub,
        cot_sub,
        wo,
        fc,
        dn,
        row(b_out),
        fc_bias,
        row(b_down),
        row(second_norm_gain),
        row(second_norm_bias),
    )
    d_att, (g_own, g_other, go_own, go_other) = rest[:n_tensor], rest[n_tensor:]
    do_parts = [d_att[0]] + [
        shift_by(d_att[d], -d) for d in range(1, n_tensor)
    ]

    def spread(v):
        pieces = gather_line(v)
        whole = jnp.zeros((tok, width), f32)
        for d in range(n_tensor):
            at = lax.rem(tensor - d + n_tensor, n_tensor) * sub
            whole = lax.dynamic_update_slice_in_dim(whole, pieces[d].astype(f32), at, 0)
        return whole[None]

    ff_grads = scatter_weights(g_own, g_other)
    out_split = lambda v: jnp.stack(jnp.split(v, n_tensor, axis=1))
    out_grads = scatter_weights(out_split(go_own), out_split(go_other))
    ff_grads = scatter_line([ff_grads[d].astype(bf16) for d in range(n_tensor)])
    out_grads = scatter_line([out_grads[d].astype(bf16) for d in range(n_tensor)])
    outputs = spread(outputs_sub)

    dq_pieces, dkv_pieces, dqkv = [], [], []
    head = 0
    queries, keys, values = [], [], []
    sent = [[] for _ in range(n_tensor)]
    for g, held, (lse, ot) in zip(GROUPS, kv, saved):
        out = attend_back(
            scalars, row(starts), qt, lse, ot, do_parts, held, head, g, BK_B, BQ_B
        )
        dq, dkv = out[:n_tensor], out[n_tensor:]
        if grouped:
            dk_keep, dk_send, dv_keep, dv_send = dkv
            r = along_x(dk_send).astype(f32)
            s = along_y(dv_send).astype(f32)
            r2 = along_y((dk_keep[1].astype(f32) + r[1]).astype(bf16)).astype(f32)
            s2 = along_x((dv_keep[1].astype(f32) + s[1]).astype(bf16)).astype(f32)
            dk = (dk_keep[0].astype(f32) + r[0] + r2).astype(bf16)
            dv = (dv_keep[0].astype(f32) + s[0] + s2).astype(bf16)
        else:
            both = lax.psum_scatter(dkv[0], "context", scatter_dimension=0, tiled=True)[0]
            dk, dv = both[: g * HD], both[g * HD :]
        queries.append(dq)
        keys.append(dk)
        values.append(dv)
        head += g

    def part_of(v, d):
        at = lax.rem(tensor + d, n_tensor) * sub
        return lax.dynamic_slice_in_dim(v, at, sub, 1)

    grads = []
    for d in range(n_tensor):
        pieces = [q[d] for q in queries]
        pieces += [part_of(k, d) for k in keys] + [part_of(v, d) for v in values]
        grads += pieces if d == 0 else [shift_by(p, d) for p in pieces]
    pieces = 3 * len(GROUPS)

    dq_whole = []
    for q in queries:
        whole = jnp.zeros((q[0].shape[0], tok), bf16)
        for d in range(n_tensor):
            at = lax.rem(tensor + d, n_tensor) * sub
            whole = lax.dynamic_update_slice_in_dim(whole, q[d], at, 1)
        dq_whole.append(whole)
    stacked = jnp.concatenate(dq_whole + keys + values, axis=0)
    qkv_grad = jnp.einsum("td,ct->dc", low_one, stacked, preferred_element_type=f32).astype(bf16)
    qv_sums = jnp.sum(stacked.astype(f32), axis=1).reshape(3, cols)
    qkv_mine = lax.dynamic_slice_in_dim(qkv_grad, core * half, half, 0)
    qkv_theirs = lax.dynamic_slice_in_dim(qkv_grad, (1 - core) * half, half, 0)

    input_sub, first_sums = last(
        place, grads, pieces, qkv, x_sub, grad_mid, row(first_norm_gain)
    )
    input_gradient = spread(input_sub)
    qkv_grads = scatter_weights(qkv_mine[None], qkv_theirs[None])[0]

    zero_fc = jnp.zeros((n_tensor, ffw), f32)
    for d in range(n_tensor):
        at = lax.rem(tensor - d + n_tensor, n_tensor)
        zero_fc = lax.dynamic_update_slice_in_dim(zero_fc, fc_sums[d], at, 0)
    zero_qv = lax.dynamic_update_slice_in_dim(
        jnp.zeros((n_tensor, 2 * cols), f32),
        jnp.concatenate([qv_sums[0], qv_sums[2]])[None],
        tensor,
        0,
    )
    small = lax.psum(
        jnp.concatenate(
            [sums.reshape(-1), first_sums.reshape(-1), zero_fc.reshape(-1), zero_qv.reshape(-1)]
        ),
        ("shard", "context", "tensor"),
    )
    table = small[: 6 * width].reshape(6, width)
    fc_total = lax.dynamic_slice_in_dim(small, 6 * width + tensor * ffw, ffw, 0)
    qv_total = lax.dynamic_slice_in_dim(
        small, 6 * width + n_tensor * ffw + tensor * 2 * cols, 2 * cols, 0
    ).reshape(2, cols)
    return (
        outputs,
        input_gradient,
        qkv_grads.astype(f32).reshape(-1, 3, cols),
        out_grads.T,
        ff_grads[:, :ffw],
        ff_grads[:, ffw:].T,
        qv_total,
        table[0],
        fc_total,
        table[1],
        table[4],
        table[5],
        table[2],
        table[3],
    )


def solution(mesh):
    sizes = dict(mesh.shape)
    placed = (
        P("shard", "context", None),
        P("shard", None),
        P("shard", None, "tensor"),
        P("tensor", "shard"),
        P("shard", "tensor"),
        P("tensor", "shard"),
        P(None, "tensor"),
        P(),
        P("tensor"),
        P(),
        P(),
        P(),
        P(),
        P(),
        P("shard", "context", None),
    )
    return jax.shard_map(
        functools.partial(body, sizes["shard"], sizes["context"], sizes["tensor"]),
        mesh=mesh,
        in_specs=placed,
        out_specs=(
            P("shard", "context", None),
            P("shard", "context", None),
            P(("shard", "context"), None, "tensor"),
            P("tensor", ("shard", "context")),
            P(("shard", "context"), "tensor"),
            P("tensor", ("shard", "context")),
            P(None, "tensor"),
            P(),
            P("tensor"),
            P(),
            P(),
            P(),
            P(),
            P(),
        ),
        check_vma=False,
    )
```

```python
import functools

import jax
import jax.numpy as jnp
from jax import lax
from jax.experimental import pallas as pl
from jax.experimental.pallas import tpu as pltpu
from jax.sharding import PartitionSpec as P

HD = 64
EPS = 1e-05
NEG = -1e30
SCALE = float(HD) ** -0.5
VMEM_LIMIT = 56 * 1024 * 1024
GROUPS = (3,)
BK_F, BQ_F = 512, 512
BK_B, BQ_B = 512, 512
f32 = jnp.float32
bf16 = jnp.bfloat16
VM = pl.BlockSpec(memory_space=pltpu.VMEM)
SM = pl.BlockSpec(memory_space=pltpu.SMEM)
HBM = pl.BlockSpec(memory_space=pl.ANY)


def nn(a, b):
    return lax.dot_general(a, b, (((1,), (0,)), ((), ())), preferred_element_type=f32)


def tn(a, b):
    return lax.dot_general(a, b, (((0,), (0,)), ((), ())), preferred_element_type=f32)


def nt(a, b):
    return lax.dot_general(a, b, (((1,), (1,)), ((), ())), preferred_element_type=f32)


def params():
    return pltpu.CompilerParams(vmem_limit_bytes=VMEM_LIMIT)


def cost(microseconds):
    return pl.CostEstimate(
        flops=int(microseconds * 1.15e9), bytes_accessed=1 << 20, transcendentals=0
    )


def shape(dims, kind=bf16):
    return jax.ShapeDtypeStruct(dims, kind)


def halves(core, width):
    half = width // 2
    own = pl.ds(pl.multiple_of(core * half, 128), half)
    other = pl.ds(pl.multiple_of((1 - core) * half, 128), half)
    return own, other


def norm(value):
    centred = value - jnp.mean(value, axis=-1, keepdims=True)
    inverse = lax.rsqrt(jnp.mean(centred * centred, axis=-1, keepdims=True) + EPS)
    return centred * inverse, inverse


def norm_gradient(grad, normed, inverse, gain):
    scaled = grad * gain
    return inverse * (
        scaled
        - jnp.mean(scaled, axis=-1, keepdims=True)
        - normed * jnp.mean(scaled * normed, axis=-1, keepdims=True)
    )


def project_kernel(sc, x, w_own, w_other, b_qv, rows, low, qt, kt, vt):
    own, other = halves(sc[2], x.shape[1])
    cols = qt.shape[0]
    normed, _ = norm(x[...].astype(f32))
    low[...] = (normed * rows[0:1, :] + rows[1:2, :]).astype(bf16)
    projected = nn(low[:, own], w_own[...]) + nn(low[:, other], w_other[...])
    qt[...] = ((projected[:, :cols] + b_qv[0:1, :]) * SCALE).T.astype(bf16)
    kt[...] = projected[:, cols : 2 * cols].T.astype(bf16)
    vt[...] = (projected[:, 2 * cols :] + b_qv[1:2, :]).T.astype(bf16)


def project(place, x, w_own, w_other, b_qv, table):
    tok, width = x.shape
    cols = b_qv.shape[1]
    rows = min(256, tok)
    fixed = lambda a: pl.BlockSpec(a.shape, lambda i: (0,) * a.ndim)
    across = pl.BlockSpec((cols, rows), lambda i: (0, i))
    return pl.pallas_call(
        project_kernel,
        grid=(tok // rows,),
        in_specs=[SM, pl.BlockSpec((rows, width), lambda i: (i, 0))]
        + [fixed(a) for a in (w_own, w_other, b_qv, table)],
        out_specs=[pl.BlockSpec((rows, width), lambda i: (i, 0)), across, across, across],
        out_shape=[shape((tok, width))] + [shape((cols, tok))] * 3,
        compiler_params=params(),
        cost_estimate=cost(7),
        name="project",
    )(place, x, w_own, w_other, b_qv, table)


def key_loop(sc, i, step, carry):
    lo, full, diag, end = sc[4 * i + 4], sc[4 * i + 5], sc[4 * i + 6], sc[4 * i + 7]
    carry = lax.fori_loop(lo, full, functools.partial(step, True), carry)
    carry = lax.fori_loop(full, diag, functools.partial(step, False), carry)
    return lax.fori_loop(diag, end, functools.partial(step, True), carry)


def tile_mask(j, bk, bq, start, qpos):
    kpos = j * bk + lax.broadcasted_iota(jnp.int32, (bk, bq), 0)
    return (kpos >= start) & (kpos <= qpos)


def load_keys(sc, kv, held, sems):
    if len(kv) == 1:
        copies = [pltpu.make_async_copy(kv[0], held, sems.at[0])]
    else:
        k, k_x, k_yd, v, v_y, v_xd = kv
        rows = k.shape[0]
        pieces = [(k, 0, 0), (k_x, 0, 1), (k_yd.at[0], 0, 2), (k_yd.at[1], 0, 3)]
        pieces += [(v, 1, 0), (v_y, 1, 2), (v_xd.at[0], 1, 1), (v_xd.at[1], 1, 3)]
        copies = [
            pltpu.make_async_copy(
                piece, held.at[sc[1] ^ run, pl.ds(which * rows, rows), :], sems.at[n]
            )
            for n, (piece, which, run) in enumerate(pieces)
        ]
    for copy in copies:
        copy.start()
    for copy in copies:
        copy.wait()


def attend_kernel(first_head, heads, bk, bq, parts, n_kv, sc, qt, st, *refs):
    kv, refs = refs[:n_kv], refs[n_kv:]
    lse, ot, out, (held, acc, sems) = refs[0], refs[1], refs[2 : 2 + parts], refs[2 + parts :]
    i = pl.program_id(0)
    per = held.shape[2] // bk
    cols = heads * HD
    start = st[...]
    qpos = sc[0] + i * bq + lax.broadcasted_iota(jnp.int32, (1, bq), 1)

    @pl.when(i == 0)
    def _():
        load_keys(sc, kv, held, sems)

    acc[...] = jnp.zeros_like(acc)

    def step(masked, j, carry):
        r = j // per
        off = pl.multiple_of((j % per) * bk, bk)
        new = []
        if masked:
            ok = tile_mask(j, bk, bq, start, qpos)
        for h in range(heads):
            m, l = carry[h]
            hs = slice(h * HD, (h + 1) * HD)
            s = tn(
                held[r, hs, pl.ds(off, bk)],
                qt[(first_head + h) * HD : (first_head + h + 1) * HD, :],
            )
            if masked:
                s = jnp.where(ok, s, NEG)
            m2 = jnp.maximum(m, jnp.max(s, axis=0, keepdims=True))
            p = jnp.exp(s - m2)
            al = jnp.exp(m - m2)
            l = l * al + jnp.sum(p, axis=0, keepdims=True)
            v = held[r, cols + h * HD : cols + (h + 1) * HD, pl.ds(off, bk)]
            acc[hs, :] = acc[hs, :] * al + nn(v, p.astype(bf16))
            new.append((m2, l))
        return tuple(new)

    one = (jnp.full((1, bq), NEG, f32), jnp.zeros((1, bq), f32))
    res = key_loop(sc, i, step, (one,) * heads)
    here = pl.ds(pl.multiple_of(i * bq, bq), bq)
    for h in range(heads):
        m, l = res[h]
        ot[h * HD : (h + 1) * HD, here] = (acc[h * HD : (h + 1) * HD, :] / l).astype(bf16)
        lse[h : h + 1, :] = m + jnp.log(l)

    @pl.when(i == pl.num_programs(0) - 1)
    def _():
        send_parts(sc[3], ot, out)


def send_parts(me, source, out):
    parts, size = len(out), out[0].shape[1]
    for d in range(parts):
        if size % 128 == 0:
            at = pl.multiple_of(lax.rem(me + d, parts) * size, 128)
            out[d][...] = source[:, pl.ds(at, size)].astype(out[d].dtype)
        else:
            for n in range(parts):

                @pl.when(lax.rem(me + d, parts) == n)
                def _():
                    out[d][...] = source[:, n * size : (n + 1) * size].astype(out[d].dtype)


def take_parts(me, rows, parts, target):
    size = parts[0].shape[1]
    for d in range(len(parts)):
        if size % 128 == 0:
            at = pl.multiple_of(lax.rem(me + d, len(parts)) * size, 128)
            target[:, pl.ds(at, size)] = parts[d][rows, :]
        else:
            for n in range(len(parts)):

                @pl.when(lax.rem(me + d, len(parts)) == n)
                def _():
                    target[:, n * size : (n + 1) * size] = parts[d][rows, :]


def attend(scalars, starts, qt, kv, first_head, heads, bk, bq, parts):
    tok = qt.shape[1]
    cols = heads * HD
    runs = kv[0].shape[0] if len(kv) == 1 else 4
    bk, bq = min(bk, tok), min(bq, tok)
    whole = lambda a, b: pl.BlockSpec((a, b), lambda i: (0, 0))
    return pl.pallas_call(
        functools.partial(attend_kernel, first_head, heads, bk, bq, parts, len(kv)),
        grid=(tok // bq,),
        in_specs=[
            SM,
            pl.BlockSpec((qt.shape[0], bq), lambda i: (0, i)),
            pl.BlockSpec((1, bq), lambda i: (0, i)),
        ]
        + [HBM] * len(kv),
        out_specs=[pl.BlockSpec((heads, bq), lambda i: (0, i)), whole(cols, tok)]
        + [whole(cols, tok // parts)] * parts,
        scratch_shapes=[
            pltpu.VMEM((runs, 2 * cols, tok), bf16),
            pltpu.VMEM((cols, bq), f32),
            pltpu.SemaphoreType.DMA((8,)),
        ],
        out_shape=[shape((heads, tok), f32), shape((cols, tok))]
        + [shape((cols, tok // parts))] * parts,
        compiler_params=params(),
        cost_estimate=cost(20),
        name="attend",
    )(scalars(bk, bq), qt, starts, *kv)


def attend_back_kernel(first_head, heads, bk, bq, parts, n_kv, sc, qt, st, lse, ot, *refs):
    do_parts, refs = refs[:parts], refs[parts:]
    kv, refs = refs[:n_kv], refs[n_kv:]
    n_out = 1 if n_kv == 1 else 4
    dq, dkv, (held, acc, dqa, do_all, sems) = (
        refs[:parts],
        refs[parts : parts + n_out],
        refs[parts + n_out :],
    )
    i = pl.program_id(0)
    per = held.shape[2] // bk
    cols = heads * HD
    start = st[...]
    qpos = sc[0] + i * bq + lax.broadcasted_iota(jnp.int32, (1, bq), 1)
    here = pl.ds(pl.multiple_of(i * bq, bq), bq)

    @pl.when(i == 0)
    def _():
        acc[...] = jnp.zeros_like(acc)
        dqa[...] = jnp.zeros_like(dqa)
        take_parts(sc[3], slice(first_head * HD, (first_head + heads) * HD), do_parts, do_all)
        load_keys(sc, kv, held, sems)

    delta = [
        jnp.sum(
            do_all[h * HD : (h + 1) * HD, here].astype(f32)
            * ot[h * HD : (h + 1) * HD, :].astype(f32),
            axis=0,
            keepdims=True,
        )
        for h in range(heads)
    ]

    def step(masked, j, carry):
        r = j // per
        off = pl.multiple_of((j % per) * bk, bk)
        if masked:
            ok = tile_mask(j, bk, bq, start, qpos)
        for h in range(heads):
            hs = slice(h * HD, (h + 1) * HD)
            vs = slice(cols + h * HD, cols + (h + 1) * HD)
            k = held[r, hs, pl.ds(off, bk)]
            v = held[r, vs, pl.ds(off, bk)]
            q = qt[(first_head + h) * HD : (first_head + h + 1) * HD, :]
            do = do_all[hs, here]
            s = tn(k, q) - lse[h : h + 1, :]
            if masked:
                s = jnp.where(ok, s, NEG)
            p = jnp.exp(s)
            ds = (p * (tn(v, do) - delta[h])).astype(bf16)
            acc[r, vs, pl.ds(off, bk)] += nt(do, p.astype(bf16))
            acc[r, hs, pl.ds(off, bk)] += nt(q, ds)
            dqa[hs, here] += nn(k, ds)
        return carry

    key_loop(sc, i, step, 0)

    @pl.when(i == pl.num_programs(0) - 1)
    def _():
        dqa[...] = dqa[...] * SCALE
        send_parts(sc[3], dqa, dq)
        if n_out == 1:
            dkv[0][...] = acc[...].astype(bf16)
        else:
            for target, pair, rows in (
                (0, (0, 2), slice(0, cols)),
                (1, (1, 3), slice(0, cols)),
                (2, (0, 1), slice(cols, 2 * cols)),
                (3, (2, 3), slice(cols, 2 * cols)),
            ):
                for n in range(2):
                    dkv[target][n] = acc[sc[1] ^ pair[n], rows, :].astype(bf16)


def attend_back(scalars, starts, qt, lse, ot, do_parts, kv, first_head, heads, bk, bq):
    tok = qt.shape[1]
    cols = heads * HD
    parts = len(do_parts)
    runs = kv[0].shape[0] if len(kv) == 1 else 4
    bk, bq = min(bk, tok), min(bq, tok)
    whole = lambda *dims: pl.BlockSpec(dims, lambda i: (0,) * len(dims))
    out_kv = [(runs, 2 * cols, tok)] if len(kv) == 1 else [(2, cols, tok)] * 4
    return pl.pallas_call(
        functools.partial(attend_back_kernel, first_head, heads, bk, bq, parts, len(kv)),
        grid=(tok // bq,),
        in_specs=[
            SM,
            pl.BlockSpec((qt.shape[0], bq), lambda i: (0, i)),
            pl.BlockSpec((1, bq), lambda i: (0, i)),
            pl.BlockSpec((heads, bq), lambda i: (0, i)),
            pl.BlockSpec((cols, bq), lambda i: (0, i)),
        ]
        + [whole(*d.shape) for d in do_parts]
        + [HBM] * len(kv),
        out_specs=[whole(cols, tok // parts)] * parts + [whole(*d) for d in out_kv],
        scratch_shapes=[
            pltpu.VMEM((runs, 2 * cols, tok), bf16),
            pltpu.VMEM((runs, 2 * cols, tok), f32),
            pltpu.VMEM((cols, tok), f32),
            pltpu.VMEM((cols, tok), bf16),
            pltpu.SemaphoreType.DMA((8,)),
        ],
        out_shape=[shape((cols, tok // parts))] * parts + [shape(d) for d in out_kv],
        compiler_params=params(),
        cost_estimate=cost(26),
        name="attend_back",
    )(scalars(bk, bq), qt, starts, lse, ot, *do_parts, *kv)


ROOT = 0.7978845608028654


def middle_kernel(n_att, parts, sc, *refs):
    att, refs = refs[:n_att], refs[n_att:]
    x, cot, od_own, od_other, fc_own, fc_other, b_fc, rows = refs[:8]
    refs = refs[8:]
    outputs, grad_mid, sums, fc_sums = refs[:4]
    d_att, (g_own, g_other) = refs[4 : 4 + parts], refs[4 + parts : 6 + parts]
    mid, att_t, low, low_t, cot_t, mlp, back = refs[6 + parts :]
    d = pl.program_id(0)
    width = x.shape[1]
    own, other = halves(sc[2], width)
    half = width // 2
    ffw = fc_own.shape[2]
    cols = att_t.shape[0] // parts
    b_out, b_down, gain, shift = (rows[n : n + 1, :] for n in range(2, 6))

    @pl.when(d == 0)
    def _():
        group = n_att // parts
        row = 0
        for part in range(parts):
            for g in range(group):
                piece = att[part * group + g]
                att_t[row : row + piece.shape[0], :] = piece[...]
                row += piece.shape[0]
        att_low = att_t[...].T
        mine = theirs = 0.0
        for part in range(parts):
            piece = att_low[:, part * cols : (part + 1) * cols]
            mine += nn(piece, od_own[part, :cols, :])
            theirs += nn(piece, od_other[part, :cols, :])
        mid[:, own] = mine
        mid[:, other] = theirs
        mid[...] = x[...].astype(f32) + mid[...] + b_out
        normed, _ = norm(mid[...])
        low[...] = (normed * gain + shift).astype(bf16)
        low_t[...] = low[...].T
        cot_t[...] = cot[...].T
        mlp[...] = jnp.zeros_like(mlp)
        back[...] = jnp.zeros_like(back)

    own_rows = pl.ds(pl.multiple_of(sc[2] * half, half), half)
    other_rows = pl.ds(pl.multiple_of((1 - sc[2]) * half, half), half)
    dn_own, dn_other = od_own[d, cols:, :], od_other[d, cols:, :]
    u = nn(low[:, own], fc_own[0]) + nn(low[:, other], fc_other[0]) + b_fc[0]
    t = jnp.tanh(ROOT * (u + 0.044715 * (u * u * u)))
    act = (0.5 * u * (1.0 + t)).astype(bf16)
    slope = 0.5 * (1.0 + t) + (0.5 * ROOT) * u * (1.0 - t * t) * (1.0 + 0.134145 * (u * u))
    d_act = nt(cot[:, own], dn_own) + nt(cot[:, other], dn_other)
    dh = (d_act * slope).astype(bf16)
    mlp[:, own] += nn(act, dn_own)
    mlp[:, other] += nn(act, dn_other)
    back[:, own] += nt(dh, fc_own[0])
    back[:, other] += nt(dh, fc_other[0])
    g_own[d, :, :ffw] = nn(low_t[own_rows, :], dh).astype(bf16)
    g_other[d, :, :ffw] = nn(low_t[other_rows, :], dh).astype(bf16)
    g_own[d, :, ffw : 2 * ffw] = nn(cot_t[own_rows, :], act).astype(bf16)
    g_other[d, :, ffw : 2 * ffw] = nn(cot_t[other_rows, :], act).astype(bf16)
    fc_sums[lax.rem(sc[3] - d + parts, parts)] = jnp.sum(dh.astype(f32), axis=0, keepdims=True)

    @pl.when(d == parts - 1)
    def _():
        normed, inverse = norm(mid[...])
        outputs[...] = (mid[...] + mlp[...] + b_down).astype(bf16)
        upper = cot[...].astype(f32)
        grad = back[...]
        down = upper + norm_gradient(grad, normed, inverse, gain)
        grad_mid[...] = down
        sums[0:1, :] = jnp.sum(down, axis=0, keepdims=True)
        sums[1:2, :] = jnp.sum(upper, axis=0, keepdims=True)
        sums[2:3, :] = jnp.sum(grad * normed, axis=0, keepdims=True)
        sums[3:4, :] = jnp.sum(grad, axis=0, keepdims=True)
        low[...] = down.astype(bf16)
        low_t[...] = low[...].T
        for part in range(parts):
            at = slice(part * cols, (part + 1) * cols)
            g_own[part, :, 2 * ffw :] = nt(low_t[own_rows, :], att_t[at, :]).astype(bf16)
            g_other[part, :, 2 * ffw :] = nt(low_t[other_rows, :], att_t[at, :]).astype(bf16)
            d_att[part][...] = (
                nt(od_own[part, :cols, :], low[:, own]) + nt(od_other[part, :cols, :], low[:, other])
            ).astype(bf16)


def middle(place, att, x, cot, od, fc, b_fc, table):
    parts, half, ffw = fc[0].shape
    sub, width = x.shape
    cols = od[0].shape[1] - ffw
    whole = lambda *dims: pl.BlockSpec(
        dims, lambda i: (0,) * len(dims), pipeline_mode=pl.Buffered(1)
    )
    each = lambda *dims: pl.BlockSpec((1,) + dims, lambda i: (i, 0, 0))
    once = lambda a: whole(*a.shape)
    grads = (parts, half, 2 * ffw + cols)
    return pl.pallas_call(
        functools.partial(middle_kernel, len(att), parts),
        grid=(parts,),
        in_specs=[SM]
        + [once(a) for a in att]
        + [once(x), once(cot), once(od[0]), once(od[1])]
        + [each(half, ffw)] * 2
        + [each(1, ffw), once(table)],
        out_specs=[whole(sub, width), whole(sub, width), whole(4, width), whole(parts, 1, ffw)]
        + [whole(cols, sub)] * parts
        + [whole(*grads)] * 2,
        out_shape=[
            shape((sub, width)),
            shape((sub, width), f32),
            shape((4, width), f32),
            shape((parts, 1, ffw), f32),
        ]
        + [shape((cols, sub))] * parts
        + [shape(grads)] * 2,
        scratch_shapes=[
            pltpu.VMEM((sub, width), f32),
            pltpu.VMEM((parts * cols, sub), bf16),
            pltpu.VMEM((sub, width), bf16),
            pltpu.VMEM((width, sub), bf16),
            pltpu.VMEM((width, sub), bf16),
            pltpu.VMEM((sub, width), f32),
            pltpu.VMEM((sub, width), f32),
        ],
        compiler_params=params(),
        cost_estimate=cost(19),
        name="middle",
    )(place, *att, x, cot, od[0], od[1], fc[0], fc[1], b_fc, table)


def last_kernel(parts, pieces, sc, *refs):
    grads, refs = refs[: parts * pieces], refs[parts * pieces :]
    w_own, w_other, x, grad_mid, rows, mid_sums, fc_sums, out, sums, back_t, stacked = refs
    half = w_own.shape[1]
    wide = w_own.shape[2]
    own_rows = pl.ds(pl.multiple_of(sc[2] * half, half), half)
    other_rows = pl.ds(pl.multiple_of((1 - sc[2]) * half, half), half)
    ones = jnp.ones((8, x.shape[0]), bf16)
    sums[...] = jnp.zeros_like(sums)
    for part in range(parts):
        row = 0
        for n in range(pieces):
            piece = grads[part * pieces + n]
            stacked[row : row + piece.shape[0], :] = piece[...]
            row += piece.shape[0]
        mine, theirs = nn(w_own[part], stacked[...]), nn(w_other[part], stacked[...])
        if part == 0:
            back_t[own_rows, :], back_t[other_rows, :] = mine, theirs
        else:
            back_t[own_rows, :] += mine
            back_t[other_rows, :] += theirs
        at = lax.rem(sc[3] - part + parts, parts)
        sums[pl.ds(6 + parts + at, 1), :wide] = nt(ones, stacked[...])[0:1, :]
    back = back_t[...].T
    normed, inverse = norm(x[...].astype(f32))
    out[...] = (grad_mid[...] + norm_gradient(back, normed, inverse, rows[0:1, :])).astype(bf16)
    sums[0:4, :] = mid_sums[...]
    sums[4:5, :] = jnp.sum(back * normed, axis=0, keepdims=True)
    sums[5:6, :] = jnp.sum(back, axis=0, keepdims=True)
    for part in range(parts):
        sums[6 + part : 7 + part, :] = fc_sums[part]


def last(place, grads, pieces, w, x, grad_mid, table, mid_sums, fc_sums):
    parts = w[0].shape[0]
    sub, width = x.shape
    rows = 8 * ((6 + 2 * parts + 7) // 8)
    return pl.pallas_call(
        functools.partial(last_kernel, parts, pieces),
        in_specs=[SM] + [VM] * (len(grads) + 7),
        out_specs=[VM, VM],
        out_shape=[shape((sub, width)), shape((rows, width), f32)],
        scratch_shapes=[pltpu.VMEM((width, sub), f32), pltpu.VMEM((w[0].shape[2], sub), bf16)],
        compiler_params=params(),
        cost_estimate=cost(6),
        name="last",
    )(place, *grads, w[0], w[1], x, grad_mid, table, mid_sums, fc_sums)


def body(
    n_shard,
    n_context,
    n_tensor,
    inputs,
    segments,
    w_qkv,
    w_out,
    w_fc,
    w_down,
    b_qv,
    b_out,
    b_fc,
    b_down,
    first_norm_gain,
    first_norm_bias,
    second_norm_gain,
    second_norm_bias,
    cotangent,
):
    _, tok, width = inputs.shape
    length = segments.shape[1]
    half, _, cols = w_qkv.shape
    heads = cols // HD
    ffw = w_fc.shape[1]
    sub = tok // n_tensor
    context = lax.axis_index("context")
    tensor = lax.axis_index("tensor")
    core = lax.axis_index("shard")
    first = context * tok
    place = jnp.stack([first, context, core, tensor]).astype(jnp.int32)
    grouped = n_context == 4
    x = inputs[0]
    cot = cotangent[0]
    row = lambda v: v[None, :]
    zero = jnp.zeros_like(b_out)
    table = jnp.stack(
        [
            first_norm_gain,
            first_norm_bias,
            b_out,
            b_down,
            second_norm_gain,
            second_norm_bias,
            zero,
            zero,
        ]
    )
    after = lambda v, dep: lax.optimization_barrier((v, dep))[0]

    swap = lambda v: lax.ppermute(v, "shard", [(0, 1), (1, 0)])
    along_x = lambda v: lax.ppermute(v, "context", [(0, 1), (1, 0), (2, 3), (3, 2)])
    along_y = lambda v: lax.ppermute(v, "context", [(0, 2), (2, 0), (1, 3), (3, 1)])
    shift_by = lambda v, d: lax.ppermute(
        v, "tensor", [(s, (s + d) % n_tensor) for s in range(n_tensor)]
    )

    def gather_direct(v):
        return [v] + [shift_by(v, d) for d in range(1, n_tensor)]

    def gather_line(v):
        if n_tensor != 4:
            return gather_direct(v)
        move = lambda a, perm: lax.ppermute(a, "tensor", perm)
        two = move(v, [(0, 2), (1, 3), (2, 0), (3, 1)])
        right = move(v, [(0, 1), (1, 2), (2, 3)])
        left = move(v, [(3, 2), (2, 1), (1, 0)])
        far = move(two, [(2, 3), (1, 0)])
        return [
            v,
            jnp.where(tensor == 0, far, right),
            two,
            jnp.where(tensor == 3, far, left),
        ]

    def scatter_direct(pieces):
        total = pieces[0].astype(f32)
        for d in range(1, n_tensor):
            total += shift_by(pieces[d].astype(bf16), -d).astype(f32)
        return total

    def scatter_context(v):
        if not grouped:
            return lax.psum_scatter(v, "context", scatter_dimension=1, tiled=True)
        size = v.shape[1] // 4
        block = lambda n: lax.dynamic_slice_in_dim(v, (context ^ n) * size, size, 1)
        own, by_x, by_y, by_both = (block(n) for n in range(4))
        cut = (v.shape[2] // 256) * 128
        lo = lambda a: a[:, :, :cut]
        hi = lambda a: a[:, :, cut:]
        r = along_x(jnp.stack([lo(by_x), lo(by_both)])).astype(f32)
        s = along_y(jnp.stack([hi(by_y), hi(by_both)])).astype(f32)
        r2 = along_y((lo(by_y).astype(f32) + r[1]).astype(bf16)).astype(f32)
        s2 = along_x((hi(by_x).astype(f32) + s[1]).astype(bf16)).astype(f32)
        return jnp.concatenate(
            [lo(own).astype(f32) + r[0] + r2, hi(own).astype(f32) + s[0] + s2], axis=2
        )

    def scatter_weights(mine, theirs):
        both = (mine.astype(f32) + swap(theirs).astype(f32)).astype(bf16)
        return scatter_context(both)

    bounds = [jnp.sum((segments[0] < d).astype(jnp.int32)) for d in range(1, 5)]
    seg = lax.dynamic_slice_in_dim(segments[0], first, tok, 0)
    starts = jnp.zeros_like(seg)
    for d in range(1, 5):
        starts = jnp.where(seg == d, bounds[d - 1], starts)

    def scalars(bk, bq):
        count = tok // bq
        begin = starts.reshape(count, bq)
        base = first + jnp.arange(count, dtype=jnp.int32) * bq
        lo = begin[:, 0] // bk
        diag = base // bk
        end = (base + bq + bk - 1) // bk
        full = jnp.minimum(jnp.maximum((begin[:, -1] + bk - 1) // bk, lo), diag)
        table = jnp.stack([lo, full, diag, end], axis=1).reshape(-1)
        return jnp.concatenate([place, table.astype(jnp.int32)])

    qkv_own = w_qkv.reshape(half, 3 * cols)
    low_one, qt, kt, vt = project(
        place,
        x,
        qkv_own,
        swap(qkv_own),
        b_qv,
        table,
    )

    kv = []
    head = 0
    for g in GROUPS:
        rows = slice(head * HD, (head + g) * HD)
        head += g
        k, v = kt[rows], vt[rows]
        if grouped:
            kx, vy = along_x(k), along_y(v)
            kv.append([k, kx, along_y(jnp.stack([k, kx])), v, vy, along_x(jnp.stack([v, vy]))])
        else:
            kv.append([lax.all_gather(jnp.concatenate([k, v], axis=0), "context", axis=0)])

    def gather_weights(w, gather):
        own = jnp.stack(gather(w))
        return own, swap(own)

    od = gather_weights(jnp.concatenate([w_out, w_down], axis=0), gather_line)
    fc = gather_weights(w_fc, gather_line)

    saved = []
    att = [[] for _ in range(n_tensor)]
    head = 0
    for g, held in zip(GROUPS, kv):
        lse, ot, *out = attend(scalars, row(starts), qt, held, head, g, BK_F, BQ_F, n_tensor)
        saved.append((lse, ot))
        att[0].append(out[0])
        for d in range(1, n_tensor):
            att[d].append(shift_by(out[d], d))
        head += g

    x_sub = lax.dynamic_slice_in_dim(x, tensor * sub, sub, 0)
    cot_sub = lax.dynamic_slice_in_dim(cot, tensor * sub, sub, 0)
    qkv = gather_weights(after(qkv_own, saved[-1][1]), gather_direct)
    all_bias = lax.all_gather(row(b_fc), "tensor", axis=0)
    fc_bias = jnp.stack(
        [
            lax.dynamic_index_in_dim(
                all_bias, lax.rem(tensor - d + n_tensor, n_tensor), 0, keepdims=False
            )
            for d in range(n_tensor)
        ]
    )
    outputs_sub, grad_mid, mid_sums, fc_sums, *rest = middle(
        place,
        [piece for part in att for piece in part],
        x_sub,
        cot_sub,
        od,
        fc,
        fc_bias,
        table,
    )
    d_att, (g_own, g_other) = rest[:n_tensor], rest[n_tensor:]
    do_parts = [d_att[0]] + [
        shift_by(d_att[d], -d) for d in range(1, n_tensor)
    ]

    def spread(v):
        pieces = gather_direct(v)
        whole = jnp.zeros((tok, width), f32)
        for d in range(n_tensor):
            at = lax.rem(tensor - d + n_tensor, n_tensor) * sub
            whole = lax.dynamic_update_slice_in_dim(whole, pieces[d].astype(f32), at, 0)
        return whole[None]

    wide_grads = scatter_weights(g_own, g_other)
    wide_grads = scatter_direct([wide_grads[d] for d in range(n_tensor)])
    outputs = spread(outputs_sub)

    dq_pieces, dkv_pieces, dqkv = [], [], []
    head = 0
    queries, keys, values = [], [], []
    sent = [[] for _ in range(n_tensor)]
    for g, held, (lse, ot) in zip(GROUPS, kv, saved):
        out = attend_back(
            scalars, row(starts), qt, lse, ot, do_parts, held, head, g, BK_B, BQ_B
        )
        dq, dkv = out[:n_tensor], out[n_tensor:]
        if grouped:
            dk_keep, dk_send, dv_keep, dv_send = dkv
            r = along_x(dk_send).astype(f32)
            s = along_y(dv_send).astype(f32)
            r2 = along_y((dk_keep[1].astype(f32) + r[1]).astype(bf16)).astype(f32)
            s2 = along_x((dv_keep[1].astype(f32) + s[1]).astype(bf16)).astype(f32)
            dk = (dk_keep[0].astype(f32) + r[0] + r2).astype(bf16)
            dv = (dv_keep[0].astype(f32) + s[0] + s2).astype(bf16)
        else:
            both = lax.psum_scatter(dkv[0], "context", scatter_dimension=0, tiled=True)[0]
            dk, dv = both[: g * HD], both[g * HD :]
        queries.append(dq)
        keys.append(dk)
        values.append(dv)
        head += g

    def part_of(v, d):
        at = lax.rem(tensor + d, n_tensor) * sub
        return lax.dynamic_slice_in_dim(v, at, sub, 1)

    grads = []
    both = jnp.concatenate(keys + values, axis=0)
    for d in range(n_tensor):
        pieces = [q[d] for q in queries] + [part_of(both, d)]
        grads += pieces if d == 0 else [shift_by(p, d) for p in pieces]
    pieces = len(GROUPS) + 1

    dq_whole = []
    for q in queries:
        whole = jnp.zeros((q[0].shape[0], tok), bf16)
        for d in range(n_tensor):
            at = lax.rem(tensor + d, n_tensor) * sub
            whole = lax.dynamic_update_slice_in_dim(whole, q[d], at, 1)
        dq_whole.append(whole)
    stacked = jnp.concatenate(dq_whole + [both], axis=0)
    qkv_grad = jnp.einsum("td,ct->dc", low_one, stacked, preferred_element_type=f32).astype(bf16)
    qkv_mine = lax.dynamic_slice_in_dim(qkv_grad, core * half, half, 0)
    qkv_theirs = lax.dynamic_slice_in_dim(qkv_grad, (1 - core) * half, half, 0)

    input_sub, small = last(
        place, grads, pieces, qkv, x_sub, grad_mid, table, mid_sums, fc_sums
    )
    input_gradient = spread(input_sub)
    qkv_grads = scatter_weights(qkv_mine[None], qkv_theirs[None])[0]

    if grouped and n_tensor == 4 and n_shard == 2:
        small += swap(small)
        small += along_x(small)
        small += along_y(small)
        small += lax.ppermute(small, "tensor", [(0, 1), (1, 0), (2, 3), (3, 2)])
        small += lax.ppermute(small, "tensor", [(0, 2), (2, 0), (1, 3), (3, 1)])
    else:
        small = lax.psum(small, ("shard", "context", "tensor"))
    fc_total = lax.dynamic_index_in_dim(small, 6 + tensor, 0, keepdims=False)
    qv_total = lax.dynamic_index_in_dim(small, 6 + n_tensor + tensor, 0, keepdims=False)
    qv_total = jnp.stack([qv_total[:cols], qv_total[2 * cols : 3 * cols]])
    return (
        outputs,
        input_gradient,
        qkv_grads.astype(f32).reshape(-1, 3, cols),
        wide_grads[:, 2 * ffw :].T,
        wide_grads[:, :ffw],
        wide_grads[:, ffw : 2 * ffw].T,
        qv_total,
        small[0],
        fc_total,
        small[1],
        small[4],
        small[5],
        small[2],
        small[3],
    )


def solution(mesh):
    sizes = dict(mesh.shape)
    placed = (
        P("shard", "context", None),
        P("shard", None),
        P("shard", None, "tensor"),
        P("tensor", "shard"),
        P("shard", "tensor"),
        P("tensor", "shard"),
        P(None, "tensor"),
        P(),
        P("tensor"),
        P(),
        P(),
        P(),
        P(),
        P(),
        P("shard", "context", None),
    )
    return jax.shard_map(
        functools.partial(body, sizes["shard"], sizes["context"], sizes["tensor"]),
        mesh=mesh,
        in_specs=placed,
        out_specs=(
            P("shard", "context", None),
            P("shard", "context", None),
            P(("shard", "context"), None, "tensor"),
            P("tensor", ("shard", "context")),
            P(("shard", "context"), "tensor"),
            P("tensor", ("shard", "context")),
            P(None, "tensor"),
            P(),
            P("tensor"),
            P(),
            P(),
            P(),
            P(),
            P(),
        ),
        check_vma=False,
    )
```

```python
import functools

import jax
import jax.numpy as jnp
from jax import lax
from jax.experimental import pallas as pl
from jax.experimental.pallas import tpu as pltpu
from jax.sharding import PartitionSpec as P

HD = 64
EPS = 1e-05
NEG = -1e30
SCALE = float(HD) ** -0.5
VMEM_LIMIT = 56 * 1024 * 1024
GROUPS = (3,)
BK_F, BQ_F = 512, 512
BK_B, BQ_B = 512, 512
f32 = jnp.float32
bf16 = jnp.bfloat16
VM = pl.BlockSpec(memory_space=pltpu.VMEM)
SM = pl.BlockSpec(memory_space=pltpu.SMEM)
HBM = pl.BlockSpec(memory_space=pl.ANY)


def nn(a, b):
    return lax.dot_general(a, b, (((1,), (0,)), ((), ())), preferred_element_type=f32)


def tn(a, b):
    return lax.dot_general(a, b, (((0,), (0,)), ((), ())), preferred_element_type=f32)


def nt(a, b):
    return lax.dot_general(a, b, (((1,), (1,)), ((), ())), preferred_element_type=f32)


def params():
    return pltpu.CompilerParams(vmem_limit_bytes=VMEM_LIMIT)


def cost(microseconds):
    return pl.CostEstimate(
        flops=int(microseconds * 1.15e9), bytes_accessed=1 << 20, transcendentals=0
    )


def shape(dims, kind=bf16):
    return jax.ShapeDtypeStruct(dims, kind)


def halves(core, width):
    half = width // 2
    own = pl.ds(pl.multiple_of(core * half, 128), half)
    other = pl.ds(pl.multiple_of((1 - core) * half, 128), half)
    return own, other


def norm(value):
    centred = value - jnp.mean(value, axis=-1, keepdims=True)
    inverse = lax.rsqrt(jnp.mean(centred * centred, axis=-1, keepdims=True) + EPS)
    return centred * inverse, inverse


def norm_gradient(grad, normed, inverse, gain):
    scaled = grad * gain
    return inverse * (
        scaled
        - jnp.mean(scaled, axis=-1, keepdims=True)
        - normed * jnp.mean(scaled * normed, axis=-1, keepdims=True)
    )


def project_kernel(sc, x, w_own, w_other, b_qv, rows, low, qt, kt, vt):
    own, other = halves(sc[2], x.shape[1])
    cols = qt.shape[0]
    normed, _ = norm(x[...].astype(f32))
    low[...] = (normed * rows[0:1, :] + rows[1:2, :]).astype(bf16)
    projected = nn(low[:, own], w_own[...]) + nn(low[:, other], w_other[...])
    qt[...] = ((projected[:, :cols] + b_qv[0:1, :]) * SCALE).T.astype(bf16)
    kt[...] = projected[:, cols : 2 * cols].T.astype(bf16)
    vt[...] = (projected[:, 2 * cols :] + b_qv[1:2, :]).T.astype(bf16)


def project(place, x, w_own, w_other, b_qv, table):
    tok, width = x.shape
    cols = b_qv.shape[1]
    rows = min(256, tok)
    fixed = lambda a: pl.BlockSpec(a.shape, lambda i: (0,) * a.ndim)
    across = pl.BlockSpec((cols, rows), lambda i: (0, i))
    return pl.pallas_call(
        project_kernel,
        grid=(tok // rows,),
        in_specs=[SM, pl.BlockSpec((rows, width), lambda i: (i, 0))]
        + [fixed(a) for a in (w_own, w_other, b_qv, table)],
        out_specs=[pl.BlockSpec((rows, width), lambda i: (i, 0)), across, across, across],
        out_shape=[shape((tok, width))] + [shape((cols, tok))] * 3,
        compiler_params=params(),
        cost_estimate=cost(7),
        name="project",
    )(place, x, w_own, w_other, b_qv, table)


def key_loop(sc, i, step, carry):
    lo, full, diag, end = sc[4 * i + 4], sc[4 * i + 5], sc[4 * i + 6], sc[4 * i + 7]
    carry = lax.fori_loop(lo, full, functools.partial(step, True), carry)
    carry = lax.fori_loop(full, diag, functools.partial(step, False), carry)
    return lax.fori_loop(diag, end, functools.partial(step, True), carry)


def tile_mask(j, bk, bq, start, qpos):
    kpos = j * bk + lax.broadcasted_iota(jnp.int32, (bk, bq), 0)
    return (kpos >= start) & (kpos <= qpos)


def load_keys(sc, kv, held, sems):
    if len(kv) == 1:
        copies = [pltpu.make_async_copy(kv[0], held, sems.at[0])]
    else:
        k, k_x, k_yd, v, v_y, v_xd = kv
        rows = k.shape[0]
        pieces = [(k, 0, 0), (k_x, 0, 1), (k_yd.at[0], 0, 2), (k_yd.at[1], 0, 3)]
        pieces += [(v, 1, 0), (v_y, 1, 2), (v_xd.at[0], 1, 1), (v_xd.at[1], 1, 3)]
        copies = [
            pltpu.make_async_copy(
                piece, held.at[sc[1] ^ run, pl.ds(which * rows, rows), :], sems.at[n]
            )
            for n, (piece, which, run) in enumerate(pieces)
        ]
    for copy in copies:
        copy.start()
    for copy in copies:
        copy.wait()


def attend_kernel(first_head, heads, bk, bq, parts, n_kv, sc, qt, st, *refs):
    kv, refs = refs[:n_kv], refs[n_kv:]
    lse, ot, out, (held, acc, sems) = refs[0], refs[1], refs[2 : 2 + parts], refs[2 + parts :]
    i = pl.program_id(0)
    per = held.shape[2] // bk
    cols = heads * HD
    start = st[...]
    qpos = sc[0] + i * bq + lax.broadcasted_iota(jnp.int32, (1, bq), 1)

    @pl.when(i == 0)
    def _():
        load_keys(sc, kv, held, sems)

    acc[...] = jnp.zeros_like(acc)

    def step(masked, j, carry):
        r = j // per
        off = pl.multiple_of((j % per) * bk, bk)
        new = []
        if masked:
            ok = tile_mask(j, bk, bq, start, qpos)
        for h in range(heads):
            m, l = carry[h]
            hs = slice(h * HD, (h + 1) * HD)
            s = tn(
                held[r, hs, pl.ds(off, bk)],
                qt[(first_head + h) * HD : (first_head + h + 1) * HD, :],
            )
            if masked:
                s = jnp.where(ok, s, NEG)
            m2 = jnp.maximum(m, jnp.max(s, axis=0, keepdims=True))
            p = jnp.exp(s - m2)
            al = jnp.exp(m - m2)
            l = l * al + jnp.sum(p, axis=0, keepdims=True)
            v = held[r, cols + h * HD : cols + (h + 1) * HD, pl.ds(off, bk)]
            acc[hs, :] = acc[hs, :] * al + nn(v, p.astype(bf16))
            new.append((m2, l))
        return tuple(new)

    one = (jnp.full((1, bq), NEG, f32), jnp.zeros((1, bq), f32))
    res = key_loop(sc, i, step, (one,) * heads)
    here = pl.ds(pl.multiple_of(i * bq, bq), bq)
    for h in range(heads):
        m, l = res[h]
        ot[h * HD : (h + 1) * HD, here] = (acc[h * HD : (h + 1) * HD, :] / l).astype(bf16)
        lse[h : h + 1, :] = m + jnp.log(l)

    @pl.when(i == pl.num_programs(0) - 1)
    def _():
        send_parts(sc[3], ot, out)


def send_parts(me, source, out):
    parts, size = len(out), out[0].shape[1]
    for d in range(parts):
        if size % 128 == 0:
            at = pl.multiple_of(lax.rem(me + d, parts) * size, 128)
            out[d][...] = source[:, pl.ds(at, size)].astype(out[d].dtype)
        else:
            for n in range(parts):

                @pl.when(lax.rem(me + d, parts) == n)
                def _():
                    out[d][...] = source[:, n * size : (n + 1) * size].astype(out[d].dtype)


def take_parts(me, rows, parts, target):
    size = parts[0].shape[1]
    for d in range(len(parts)):
        if size % 128 == 0:
            at = pl.multiple_of(lax.rem(me + d, len(parts)) * size, 128)
            target[:, pl.ds(at, size)] = parts[d][rows, :]
        else:
            for n in range(len(parts)):

                @pl.when(lax.rem(me + d, len(parts)) == n)
                def _():
                    target[:, n * size : (n + 1) * size] = parts[d][rows, :]


def attend(scalars, starts, qt, kv, first_head, heads, bk, bq, parts):
    tok = qt.shape[1]
    cols = heads * HD
    runs = kv[0].shape[0] if len(kv) == 1 else 4
    bk, bq = min(bk, tok), min(bq, tok)
    whole = lambda a, b: pl.BlockSpec((a, b), lambda i: (0, 0))
    return pl.pallas_call(
        functools.partial(attend_kernel, first_head, heads, bk, bq, parts, len(kv)),
        grid=(tok // bq,),
        in_specs=[
            SM,
            pl.BlockSpec((qt.shape[0], bq), lambda i: (0, i)),
            pl.BlockSpec((1, bq), lambda i: (0, i)),
        ]
        + [HBM] * len(kv),
        out_specs=[pl.BlockSpec((heads, bq), lambda i: (0, i)), whole(cols, tok)]
        + [whole(cols, tok // parts)] * parts,
        scratch_shapes=[
            pltpu.VMEM((runs, 2 * cols, tok), bf16),
            pltpu.VMEM((cols, bq), f32),
            pltpu.SemaphoreType.DMA((8,)),
        ],
        out_shape=[shape((heads, tok), f32), shape((cols, tok))]
        + [shape((cols, tok // parts))] * parts,
        compiler_params=params(),
        cost_estimate=cost(20),
        name="attend",
    )(scalars(bk, bq), qt, starts, *kv)


def attend_back_kernel(first_head, heads, bk, bq, parts, n_kv, sc, qt, st, lse, ot, *refs):
    do_parts, refs = refs[:parts], refs[parts:]
    kv, refs = refs[:n_kv], refs[n_kv:]
    n_out = 1 if n_kv == 1 else 4
    dq, dkv, (held, acc, dqa, do_all, sems) = (
        refs[:parts],
        refs[parts : parts + n_out],
        refs[parts + n_out :],
    )
    i = pl.program_id(0)
    per = held.shape[2] // bk
    cols = heads * HD
    start = st[...]
    qpos = sc[0] + i * bq + lax.broadcasted_iota(jnp.int32, (1, bq), 1)
    here = pl.ds(pl.multiple_of(i * bq, bq), bq)

    @pl.when(i == 0)
    def _():
        acc[...] = jnp.zeros_like(acc)
        dqa[...] = jnp.zeros_like(dqa)
        take_parts(sc[3], slice(first_head * HD, (first_head + heads) * HD), do_parts, do_all)
        load_keys(sc, kv, held, sems)

    delta = [
        jnp.sum(
            do_all[h * HD : (h + 1) * HD, here].astype(f32)
            * ot[h * HD : (h + 1) * HD, :].astype(f32),
            axis=0,
            keepdims=True,
        )
        for h in range(heads)
    ]

    def step(masked, j, carry):
        r = j // per
        off = pl.multiple_of((j % per) * bk, bk)
        if masked:
            ok = tile_mask(j, bk, bq, start, qpos)
        for h in range(heads):
            hs = slice(h * HD, (h + 1) * HD)
            vs = slice(cols + h * HD, cols + (h + 1) * HD)
            k = held[r, hs, pl.ds(off, bk)]
            v = held[r, vs, pl.ds(off, bk)]
            q = qt[(first_head + h) * HD : (first_head + h + 1) * HD, :]
            do = do_all[hs, here]
            s = tn(k, q) - lse[h : h + 1, :]
            if masked:
                s = jnp.where(ok, s, NEG)
            p = jnp.exp(s)
            ds = (p * (tn(v, do) - delta[h])).astype(bf16)
            acc[r, vs, pl.ds(off, bk)] += nt(do, p.astype(bf16))
            acc[r, hs, pl.ds(off, bk)] += nt(q, ds)
            dqa[hs, here] += nn(k, ds)
        return carry

    key_loop(sc, i, step, 0)

    @pl.when(i == pl.num_programs(0) - 1)
    def _():
        dqa[...] = dqa[...] * SCALE
        send_parts(sc[3], dqa, dq)
        if n_out == 1:
            dkv[0][...] = acc[...].astype(bf16)
        else:
            for target, pair, rows in (
                (0, (0, 2), slice(0, cols)),
                (1, (1, 3), slice(0, cols)),
                (2, (0, 1), slice(cols, 2 * cols)),
                (3, (2, 3), slice(cols, 2 * cols)),
            ):
                for n in range(2):
                    dkv[target][n] = acc[sc[1] ^ pair[n], rows, :].astype(bf16)


def attend_back(scalars, starts, qt, lse, ot, do_parts, kv, first_head, heads, bk, bq):
    tok = qt.shape[1]
    cols = heads * HD
    parts = len(do_parts)
    runs = kv[0].shape[0] if len(kv) == 1 else 4
    bk, bq = min(bk, tok), min(bq, tok)
    whole = lambda *dims: pl.BlockSpec(dims, lambda i: (0,) * len(dims))
    out_kv = [(runs, 2 * cols, tok)] if len(kv) == 1 else [(2, cols, tok)] * 4
    return pl.pallas_call(
        functools.partial(attend_back_kernel, first_head, heads, bk, bq, parts, len(kv)),
        grid=(tok // bq,),
        in_specs=[
            SM,
            pl.BlockSpec((qt.shape[0], bq), lambda i: (0, i)),
            pl.BlockSpec((1, bq), lambda i: (0, i)),
            pl.BlockSpec((heads, bq), lambda i: (0, i)),
            pl.BlockSpec((cols, bq), lambda i: (0, i)),
        ]
        + [whole(*d.shape) for d in do_parts]
        + [HBM] * len(kv),
        out_specs=[whole(cols, tok // parts)] * parts + [whole(*d) for d in out_kv],
        scratch_shapes=[
            pltpu.VMEM((runs, 2 * cols, tok), bf16),
            pltpu.VMEM((runs, 2 * cols, tok), f32),
            pltpu.VMEM((cols, tok), f32),
            pltpu.VMEM((cols, tok), bf16),
            pltpu.SemaphoreType.DMA((8,)),
        ],
        out_shape=[shape((cols, tok // parts))] * parts + [shape(d) for d in out_kv],
        compiler_params=params(),
        cost_estimate=cost(26),
        name="attend_back",
    )(scalars(bk, bq), qt, starts, lse, ot, *do_parts, *kv)


ROOT = 0.7978845608028654


def middle_kernel(n_att, parts, sc, *refs):
    att, refs = refs[:n_att], refs[n_att:]
    x, cot, of_own, of_other, dn_own, dn_other, rows = refs[:7]
    refs = refs[7:]
    outputs, grad_mid, sums, fc_sums = refs[:4]
    d_att, (g_own, g_other) = refs[4 : 4 + parts], refs[4 + parts : 6 + parts]
    mid, att_t, low, low_t, cot_t, mlp, back = refs[6 + parts :]
    d = pl.program_id(0)
    width = x.shape[1]
    own, other = halves(sc[2], width)
    half = width // 2
    ffw = dn_own.shape[1]
    count = ffw // half
    cols = att_t.shape[0] // parts
    b_out, b_down, gain, shift = (rows[n : n + 1, :] for n in range(2, 6))

    @pl.when(d == 0)
    def _():
        group = n_att // parts
        row = 0
        for part in range(parts):
            for g in range(group):
                piece = att[part * group + g]
                att_t[row : row + piece.shape[0], :] = piece[...]
                row += piece.shape[0]
        att_low = att_t[...].T
        mine = theirs = 0.0
        for part in range(parts):
            piece = att_low[:, part * cols : (part + 1) * cols]
            mine += nn(piece, of_own[part, :cols, :])
            theirs += nn(piece, of_other[part, :cols, :])
        mid[:, own] = mine
        mid[:, other] = theirs
        mid[...] = x[...].astype(f32) + mid[...] + b_out
        normed, _ = norm(mid[...])
        low[...] = (normed * gain + shift).astype(bf16)
        low_t[...] = low[...].T
        cot_t[...] = cot[...].T
        mlp[...] = jnp.zeros_like(mlp)
        back[...] = jnp.zeros_like(back)

    own_rows = pl.ds(pl.multiple_of(sc[2] * half, half), half)
    other_rows = pl.ds(pl.multiple_of((1 - sc[2]) * half, half), half)
    terms = of_own[d, cols : cols + 16, :].astype(f32)
    pieces = [slice(cols + 16 + n * half, cols + 16 + (n + 1) * half) for n in range(count)]
    u = [
        nn(low[:, own], of_own[d, at, :])
        + nn(low[:, other], of_other[d, at, :])
        + sum(terms[t * count + n : t * count + n + 1, :] for t in range(3))
        for n, at in enumerate(pieces)
    ]
    u = jnp.concatenate(u, axis=1)
    t = jnp.tanh(ROOT * (u + 0.044715 * (u * u * u)))
    act = (0.5 * u * (1.0 + t)).astype(bf16)
    slope = 0.5 * (1.0 + t) + (0.5 * ROOT) * u * (1.0 - t * t) * (1.0 + 0.134145 * (u * u))
    d_act = nt(cot[:, own], dn_own[0]) + nt(cot[:, other], dn_other[0])
    dh = (d_act * slope).astype(bf16)
    mlp[:, own] += nn(act, dn_own[0])
    mlp[:, other] += nn(act, dn_other[0])
    for n, at in enumerate(pieces):
        dh_n = dh[:, n * half : (n + 1) * half]
        back[:, own] += nt(dh_n, of_own[d, at, :])
        back[:, other] += nt(dh_n, of_other[d, at, :])
    g_own[d, :, :ffw] = nn(low_t[own_rows, :], dh).astype(bf16)
    g_other[d, :, :ffw] = nn(low_t[other_rows, :], dh).astype(bf16)
    g_own[d, :, ffw : 2 * ffw] = nn(cot_t[own_rows, :], act).astype(bf16)
    g_other[d, :, ffw : 2 * ffw] = nn(cot_t[other_rows, :], act).astype(bf16)
    fc_sums[lax.rem(sc[3] - d + parts, parts)] = jnp.sum(dh.astype(f32), axis=0, keepdims=True)

    @pl.when(d == parts - 1)
    def _():
        normed, inverse = norm(mid[...])
        outputs[...] = (mid[...] + mlp[...] + b_down).astype(bf16)
        upper = cot[...].astype(f32)
        grad = back[...]
        down = upper + norm_gradient(grad, normed, inverse, gain)
        grad_mid[...] = down
        sums[0:1, :] = jnp.sum(down, axis=0, keepdims=True)
        sums[1:2, :] = jnp.sum(upper, axis=0, keepdims=True)
        sums[2:3, :] = jnp.sum(grad * normed, axis=0, keepdims=True)
        sums[3:4, :] = jnp.sum(grad, axis=0, keepdims=True)
        low[...] = down.astype(bf16)
        low_t[...] = low[...].T
        g_own[:, :, 2 * ffw + cols :] = jnp.zeros_like(g_own[:, :, 2 * ffw + cols :])
        g_other[:, :, 2 * ffw + cols :] = jnp.zeros_like(g_other[:, :, 2 * ffw + cols :])
        for part in range(parts):
            at = slice(part * cols, (part + 1) * cols)
            g_own[part, :, 2 * ffw : 2 * ffw + cols] = nt(low_t[own_rows, :], att_t[at, :]).astype(bf16)
            g_other[part, :, 2 * ffw : 2 * ffw + cols] = nt(low_t[other_rows, :], att_t[at, :]).astype(bf16)
            d_att[part][...] = (
                nt(of_own[part, :cols, :], low[:, own]) + nt(of_other[part, :cols, :], low[:, other])
            ).astype(bf16)


def middle(place, att, x, cot, of, dn, cols, table):
    parts, ffw, half = dn[0].shape
    sub, width = x.shape
    whole = lambda *dims: pl.BlockSpec(
        dims, lambda i, sc: (0,) * len(dims), pipeline_mode=pl.Buffered(1)
    )
    placed = pl.BlockSpec(
        (1, ffw, half), lambda i, sc: (lax.rem(sc[3] - i + parts, parts), 0, 0)
    )
    once = lambda a: whole(*a.shape)
    grads = (parts, half, 128 * ((2 * ffw + cols + 127) // 128))
    return pl.pallas_call(
        functools.partial(middle_kernel, len(att), parts),
        grid_spec=pltpu.PrefetchScalarGridSpec(
            num_scalar_prefetch=1,
            grid=(parts,),
            in_specs=[once(a) for a in att]
            + [once(x), once(cot), once(of[0]), once(of[1]), placed, placed, once(table)],
            out_specs=[whole(sub, width), whole(sub, width), whole(4, width), whole(parts, 1, ffw)]
            + [whole(cols, sub)] * parts
            + [whole(*grads)] * 2,
            scratch_shapes=[
                pltpu.VMEM((sub, width), f32),
                pltpu.VMEM((parts * cols, sub), bf16),
                pltpu.VMEM((sub, width), bf16),
                pltpu.VMEM((width, sub), bf16),
                pltpu.VMEM((width, sub), bf16),
                pltpu.VMEM((sub, width), f32),
                pltpu.VMEM((sub, width), f32),
            ],
        ),
        out_shape=[
            shape((sub, width)),
            shape((sub, width), f32),
            shape((4, width), f32),
            shape((parts, 1, ffw), f32),
        ]
        + [shape((cols, sub))] * parts
        + [shape(grads)] * 2,
        compiler_params=params(),
        cost_estimate=cost(19),
        name="middle",
    )(place, *att, x, cot, of[0], of[1], dn[0], dn[1], table)


def last_kernel(parts, pieces, sc, *refs):
    grads, refs = refs[: parts * pieces], refs[parts * pieces :]
    w_own, w_other, x, grad_mid, rows, mid_sums, fc_sums, out, sums, back_t, stacked = refs
    half = w_own.shape[1]
    wide = w_own.shape[2]
    own_rows = pl.ds(pl.multiple_of(sc[2] * half, half), half)
    other_rows = pl.ds(pl.multiple_of((1 - sc[2]) * half, half), half)
    ones = jnp.ones((8, x.shape[0]), bf16)
    sums[...] = jnp.zeros_like(sums)
    stacked[...] = jnp.zeros_like(stacked)
    for part in range(parts):
        row = 0
        for n in range(pieces):
            piece = grads[part * pieces + n]
            stacked[row : row + piece.shape[0], :] = piece[...]
            row += piece.shape[0]
        at = lax.rem(sc[3] - part + parts, parts)
        mine, theirs = nn(w_own[at], stacked[...]), nn(w_other[at], stacked[...])
        if part == 0:
            back_t[own_rows, :], back_t[other_rows, :] = mine, theirs
        else:
            back_t[own_rows, :] += mine
            back_t[other_rows, :] += theirs
        sums[pl.ds(6 + parts + at, 1), :wide] = nt(ones, stacked[...])[0:1, :]
    back = back_t[...].T
    normed, inverse = norm(x[...].astype(f32))
    out[...] = (grad_mid[...] + norm_gradient(back, normed, inverse, rows[0:1, :])).astype(bf16)
    sums[0:4, :] = mid_sums[...]
    sums[4:5, :] = jnp.sum(back * normed, axis=0, keepdims=True)
    sums[5:6, :] = jnp.sum(back, axis=0, keepdims=True)
    for part in range(parts):
        sums[6 + part : 7 + part, :] = fc_sums[part]


def last(place, grads, pieces, w, x, grad_mid, table, mid_sums, fc_sums):
    parts = w[0].shape[0]
    sub, width = x.shape
    rows = 8 * ((6 + 2 * parts + 7) // 8)
    return pl.pallas_call(
        functools.partial(last_kernel, parts, pieces),
        in_specs=[SM] + [VM] * (len(grads) + 7),
        out_specs=[VM, VM],
        out_shape=[shape((sub, width)), shape((rows, width), f32)],
        scratch_shapes=[pltpu.VMEM((width, sub), f32), pltpu.VMEM((w[0].shape[2], sub), bf16)],
        compiler_params=params(),
        cost_estimate=cost(6),
        name="last",
    )(place, *grads, w[0], w[1], x, grad_mid, table, mid_sums, fc_sums)


def fold_kernel(cut, sc, mine, theirs, lo_send, lo_keep, hi_send, hi_keep):
    i = pl.program_id(0)
    total = (mine[...].astype(f32) + theirs[...].astype(f32)).astype(bf16)
    lo, hi = total[None, :, :, :cut], total[None, :, :, cut:]

    @pl.when(i < 2)
    def _():
        lo_send[...] = lo

    @pl.when(i >= 2)
    def _():
        lo_keep[...] = lo

    @pl.when((i == 1) | (i == 2))
    def _():
        hi_send[...] = hi

    @pl.when((i == 0) | (i == 3))
    def _():
        hi_keep[...] = hi


def fold(place, mine, theirs):
    parts, rows, wide = mine.shape
    size = rows // 4
    cut = (wide // 256) * 128 if wide % 256 == 0 else (wide // 256 + 1) * 128
    block = pl.BlockSpec(
        (parts, size, wide),
        lambda i, sc: (
            0,
            sc[1] ^ jnp.where(i == 0, 1, jnp.where(i == 1, 3, jnp.where(i == 2, 2, 0))),
            0,
        ),
    )
    out = lambda width, index: pl.BlockSpec(
        (1, parts, size, width), lambda i, sc: (index(i), 0, 0, 0)
    )
    lo, hi = cut, wide - cut
    return pl.pallas_call(
        functools.partial(fold_kernel, cut),
        grid_spec=pltpu.PrefetchScalarGridSpec(
            num_scalar_prefetch=1,
            grid=(4,),
            in_specs=[block, block],
            out_specs=[
                out(lo, lambda i: jnp.minimum(i, 1)),
                out(lo, lambda i: jnp.where(i == 3, 0, 1)),
                out(hi, lambda i: jnp.where(i < 2, 1, 0)),
                out(hi, lambda i: jnp.where(i == 3, 0, 1)),
            ],
        ),
        out_shape=[
            shape((2, parts, size, lo)),
            shape((2, parts, size, lo)),
            shape((2, parts, size, hi)),
            shape((2, parts, size, hi)),
        ],
        compiler_params=params(),
        cost_estimate=cost(1 + 6 * parts / 4),
        name="fold",
    )(place, mine, theirs)


def body(
    n_shard,
    n_context,
    n_tensor,
    inputs,
    segments,
    w_qkv,
    w_out,
    w_fc,
    w_down,
    b_qv,
    b_out,
    b_fc,
    b_down,
    first_norm_gain,
    first_norm_bias,
    second_norm_gain,
    second_norm_bias,
    cotangent,
):
    _, tok, width = inputs.shape
    length = segments.shape[1]
    half, _, cols = w_qkv.shape
    heads = cols // HD
    ffw = w_fc.shape[1]
    sub = tok // n_tensor
    context = lax.axis_index("context")
    tensor = lax.axis_index("tensor")
    core = lax.axis_index("shard")
    first = context * tok
    place = jnp.stack([first, context, core, tensor]).astype(jnp.int32)
    grouped = n_context == 4
    x = inputs[0]
    cot = cotangent[0]
    row = lambda v: v[None, :]
    zero = jnp.zeros_like(b_out)
    table = jnp.stack(
        [
            first_norm_gain,
            first_norm_bias,
            b_out,
            b_down,
            second_norm_gain,
            second_norm_bias,
            zero,
            zero,
        ]
    )
    after = lambda v, dep: lax.optimization_barrier((v, dep))[0]

    swap = lambda v: lax.ppermute(v, "shard", [(0, 1), (1, 0)])
    along_x = lambda v: lax.ppermute(v, "context", [(0, 1), (1, 0), (2, 3), (3, 2)])
    along_y = lambda v: lax.ppermute(v, "context", [(0, 2), (2, 0), (1, 3), (3, 1)])
    shift_by = lambda v, d: lax.ppermute(
        v, "tensor", [(s, (s + d) % n_tensor) for s in range(n_tensor)]
    )

    def gather_direct(v):
        return [v] + [shift_by(v, d) for d in range(1, n_tensor)]

    def gather_line(v, hold=None):
        if n_tensor != 4:
            return gather_direct(v)
        move = lambda a, perm: lax.ppermute(a, "tensor", perm)
        two = move(v, [(0, 2), (1, 3), (2, 0), (3, 1)])
        right = move(v, [(0, 1), (1, 2), (2, 3)])
        left = move(v, [(3, 2), (2, 1), (1, 0)])
        far = move(two if hold is None else after(two, hold), [(2, 3), (1, 0)])
        return [
            v,
            jnp.where(tensor == 0, far, right),
            two,
            jnp.where(tensor == 3, far, left),
        ]

    def scatter_line(pieces):
        if n_tensor != 4:
            total = pieces[0].astype(f32)
            for d in range(1, n_tensor):
                total += shift_by(pieces[d].astype(bf16), -d).astype(f32)
            return total
        move = lambda a, perm: lax.ppermute(a.astype(bf16), "tensor", perm)
        far = move(jnp.where(tensor == 0, pieces[1], pieces[3]), [(0, 1), (3, 2)])
        right = move(pieces[3], [(0, 1), (1, 2), (2, 3)])
        left = move(pieces[1], [(3, 2), (2, 1), (1, 0)])
        two = move(
            pieces[2].astype(f32) + far.astype(f32), [(0, 2), (1, 3), (2, 0), (3, 1)]
        )
        return (
            pieces[0].astype(f32) + right.astype(f32) + left.astype(f32) + two.astype(f32)
        )

    def scatter_begin(mine, theirs):
        theirs = swap(theirs)
        if not grouped:
            both = (mine.astype(f32) + theirs.astype(f32)).astype(bf16)
            return lax.psum_scatter(both, "context", scatter_dimension=1, tiled=True)
        return fold(place, mine, theirs)

    def scatter_first(state):
        if not grouped:
            return state
        lo_send, lo_keep, hi_send, hi_keep = state
        r, s = along_x(lo_send).astype(f32), along_y(hi_send).astype(f32)
        return (
            lo_keep[0].astype(f32) + r[0],
            hi_keep[0].astype(f32) + s[0],
            (lo_keep[1].astype(f32) + r[1]).astype(bf16),
            (hi_keep[1].astype(f32) + s[1]).astype(bf16),
        )

    def scatter_second(state):
        if not grouped:
            return state
        lo, hi, lo_send, hi_send = state
        lo += along_y(lo_send).astype(f32)
        hi += along_x(hi_send).astype(f32)
        return jnp.concatenate([lo, hi], axis=2)

    bounds = [jnp.sum((segments[0] < d).astype(jnp.int32)) for d in range(1, 5)]
    seg = lax.dynamic_slice_in_dim(segments[0], first, tok, 0)
    starts = jnp.zeros_like(seg)
    for d in range(1, 5):
        starts = jnp.where(seg == d, bounds[d - 1], starts)

    def scalars(bk, bq):
        count = tok // bq
        begin = starts.reshape(count, bq)
        base = first + jnp.arange(count, dtype=jnp.int32) * bq
        lo = begin[:, 0] // bk
        diag = base // bk
        end = (base + bq + bk - 1) // bk
        full = jnp.minimum(jnp.maximum((begin[:, -1] + bk - 1) // bk, lo), diag)
        table = jnp.stack([lo, full, diag, end], axis=1).reshape(-1)
        return jnp.concatenate([place, table.astype(jnp.int32)])

    qkv_own = w_qkv.reshape(half, 3 * cols)
    low_one, qt, kt, vt = project(
        place,
        x,
        qkv_own,
        swap(qkv_own),
        b_qv,
        table,
    )

    kv = []
    head = 0
    for g in GROUPS:
        rows = slice(head * HD, (head + g) * HD)
        head += g
        k, v = kt[rows], vt[rows]
        if grouped:
            kx, vy = along_x(k), along_y(v)
            k_two, v_two = jnp.stack([k, kx]), jnp.stack([v, vy])
            kv.append([k, kx, along_y(k_two), v, vy, along_x(v_two)])
        else:
            kv.append([lax.all_gather(jnp.concatenate([k, v], axis=0), "context", axis=0)])

    def gather_weights(w, gather):
        own = jnp.stack(gather(w))
        return own, swap(own)

    terms, rest = [], b_fc
    for _ in range(3):
        term = lax.reduce_precision(rest, 8, 7)
        terms.append(term.astype(bf16).reshape(ffw // half, half))
        rest = rest - term
    terms = jnp.concatenate(terms, axis=0)
    terms = jnp.pad(terms, ((0, 16 - terms.shape[0]), (0, 0)))
    packed = jnp.concatenate([w_out, terms, w_fc[:, :half], w_fc[:, half:]], axis=0)
    gathered = lax.all_gather(w_down, "tensor", axis=0)
    dn = (gathered, swap(gathered))
    saved = []
    att = [[] for _ in range(n_tensor)]
    head = 0
    for g, held in zip(GROUPS, kv):
        lse, ot, *out = attend(scalars, row(starts), qt, held, head, g, BK_F, BQ_F, n_tensor)
        saved.append((lse, ot))
        att[0].append(out[0])
        for d in range(1, n_tensor):
            att[d].append(shift_by(out[d], d))
        head += g

    of = gather_weights(packed, lambda w: gather_line(w, saved[-1][0]))
    x_sub = lax.dynamic_slice_in_dim(x, tensor * sub, sub, 0)
    cot_sub = lax.dynamic_slice_in_dim(cot, tensor * sub, sub, 0)
    outputs_sub, grad_mid, mid_sums, fc_sums, *rest = middle(
        place,
        [piece for part in att for piece in part],
        x_sub,
        cot_sub,
        of,
        dn,
        cols,
        table,
    )
    d_att, (g_own, g_other) = rest[:n_tensor], rest[n_tensor:]
    do_parts = [d_att[0]] + [
        shift_by(d_att[d], -d) for d in range(1, n_tensor)
    ]

    def spread(v):
        pieces = gather_line(v)
        whole = jnp.zeros((tok, width), f32)
        for d in range(n_tensor):
            at = lax.rem(tensor - d + n_tensor, n_tensor) * sub
            whole = lax.dynamic_update_slice_in_dim(whole, pieces[d].astype(f32), at, 0)
        return whole[None]

    folded = scatter_begin(g_own, g_other)
    hop_one = folded[0] if grouped else folded
    outputs = lax.all_gather(after(outputs_sub, do_parts[-1]), "tensor", axis=0, tiled=True)
    wide = scatter_first(folded)

    dq_pieces, dkv_pieces, dqkv = [], [], []
    head = 0
    queries, keys, values = [], [], []
    sent = [[] for _ in range(n_tensor)]
    for g, held, (lse, ot) in zip(GROUPS, kv, saved):
        out = attend_back(
            scalars, row(starts), after(qt, hop_one), lse, ot, do_parts, held, head, g, BK_B, BQ_B
        )
        dq, dkv = out[:n_tensor], out[n_tensor:]
        if grouped:
            dk_keep, dk_send, dv_keep, dv_send = dkv
            dk_send, dv_send = after((dk_send, dv_send), (wide[2], wide[3]))
            r = along_x(dk_send).astype(f32)
            s = along_y(dv_send).astype(f32)
            r2 = along_y((dk_keep[1].astype(f32) + r[1]).astype(bf16)).astype(f32)
            s2 = along_x((dv_keep[1].astype(f32) + s[1]).astype(bf16)).astype(f32)
            dk = (dk_keep[0].astype(f32) + r[0] + r2).astype(bf16)
            dv = (dv_keep[0].astype(f32) + s[0] + s2).astype(bf16)
        else:
            both = lax.psum_scatter(dkv[0], "context", scatter_dimension=0, tiled=True)[0]
            dk, dv = both[: g * HD], both[g * HD :]
        queries.append(dq)
        keys.append(dk)
        values.append(dv)
        head += g

    wide = scatter_second(wide)
    wide_grads = scatter_line([wide[d] for d in range(n_tensor)])

    def part_of(v, d):
        at = lax.rem(tensor + d, n_tensor) * sub
        return lax.dynamic_slice_in_dim(v, at, sub, 1)

    grads = []
    both = jnp.concatenate(keys + values, axis=0)
    for d in range(n_tensor):
        pieces = [q[d] for q in queries] + [part_of(both, d)]
        grads += pieces if d == 0 else [shift_by(p, d) for p in pieces]
    pieces = len(GROUPS) + 1

    dq_whole = []
    for q in queries:
        whole = jnp.zeros((q[0].shape[0], tok), bf16)
        for d in range(n_tensor):
            at = lax.rem(tensor + d, n_tensor) * sub
            whole = lax.dynamic_update_slice_in_dim(whole, q[d], at, 1)
        dq_whole.append(whole)
    qkv_wide = jnp.pad(qkv_own, ((0, 0), (0, -3 * cols % 128)))
    qkv = lax.all_gather(after(qkv_wide, queries[-1][0]), "tensor", axis=0)
    qkv = (qkv, swap(qkv))
    input_sub, small = last(
        place, grads, pieces, qkv, x_sub, grad_mid, table, mid_sums, fc_sums
    )
    input_gradient = spread(input_sub)
    outputs = after(outputs, input_sub).astype(f32)[None]
    stacked = jnp.concatenate(
        dq_whole + [both, jnp.zeros((-3 * cols % 128, tok), bf16)], axis=0
    )
    qkv_grad = jnp.einsum(
        "td,ct->dc", low_one, after(stacked, input_sub), preferred_element_type=f32
    ).astype(bf16)
    qkv_mine = lax.dynamic_slice_in_dim(qkv_grad, core * half, half, 0)
    qkv_theirs = lax.dynamic_slice_in_dim(qkv_grad, (1 - core) * half, half, 0)
    qkv_grads = scatter_second(scatter_first(scatter_begin(qkv_mine[None], qkv_theirs[None])))[0]

    if grouped and n_tensor == 4 and n_shard == 2:
        small += swap(small)
        small += along_x(small)
        small += along_y(small)
        small += lax.ppermute(small, "tensor", [(0, 1), (1, 0), (2, 3), (3, 2)])
        small += lax.ppermute(small, "tensor", [(0, 2), (2, 0), (1, 3), (3, 1)])
    else:
        small = lax.psum(small, ("shard", "context", "tensor"))
    fc_total = lax.dynamic_index_in_dim(small, 6 + tensor, 0, keepdims=False)
    qv_total = lax.dynamic_index_in_dim(small, 6 + n_tensor + tensor, 0, keepdims=False)
    qv_total = jnp.stack([qv_total[:cols], qv_total[2 * cols : 3 * cols]])
    return (
        outputs,
        input_gradient,
        qkv_grads[:, : 3 * cols].astype(f32).reshape(-1, 3, cols),
        wide_grads[:, 2 * ffw : 2 * ffw + cols].T,
        wide_grads[:, :ffw],
        wide_grads[:, ffw : 2 * ffw].T,
        qv_total,
        small[0],
        fc_total,
        small[1],
        small[4],
        small[5],
        small[2],
        small[3],
    )


def solution(mesh):
    sizes = dict(mesh.shape)
    placed = (
        P("shard", "context", None),
        P("shard", None),
        P("shard", None, "tensor"),
        P("tensor", "shard"),
        P("shard", "tensor"),
        P("tensor", "shard"),
        P(None, "tensor"),
        P(),
        P("tensor"),
        P(),
        P(),
        P(),
        P(),
        P(),
        P("shard", "context", None),
    )
    return jax.shard_map(
        functools.partial(body, sizes["shard"], sizes["context"], sizes["tensor"]),
        mesh=mesh,
        in_specs=placed,
        out_specs=(
            P("shard", "context", None),
            P("shard", "context", None),
            P(("shard", "context"), None, "tensor"),
            P("tensor", ("shard", "context")),
            P(("shard", "context"), "tensor"),
            P("tensor", ("shard", "context")),
            P(None, "tensor"),
            P(),
            P("tensor"),
            P(),
            P(),
            P(),
            P(),
            P(),
        ),
        check_vma=False,
    )
```

```python
import functools

import jax
import jax.numpy as jnp
from jax import lax
from jax.experimental import pallas as pl
from jax.experimental.pallas import tpu as pltpu
from jax.sharding import PartitionSpec as P

HD = 64
EPS = 1e-05
NEG = -1e30
SCALE = float(HD) ** -0.5
VMEM_LIMIT = 56 * 1024 * 1024
GROUPS = (3,)
BK_F, BQ_F = 512, 512
BK_B, BQ_B = 512, 512
f32 = jnp.float32
bf16 = jnp.bfloat16
VM = pl.BlockSpec(memory_space=pltpu.VMEM)
SM = pl.BlockSpec(memory_space=pltpu.SMEM)
HBM = pl.BlockSpec(memory_space=pl.ANY)


def nn(a, b):
    return lax.dot_general(a, b, (((1,), (0,)), ((), ())), preferred_element_type=f32)


def tn(a, b):
    return lax.dot_general(a, b, (((0,), (0,)), ((), ())), preferred_element_type=f32)


def nt(a, b):
    return lax.dot_general(a, b, (((1,), (1,)), ((), ())), preferred_element_type=f32)


def params():
    return pltpu.CompilerParams(vmem_limit_bytes=VMEM_LIMIT)


def cost(microseconds):
    return pl.CostEstimate(
        flops=int(microseconds * 1.15e9), bytes_accessed=1 << 20, transcendentals=0
    )


def shape(dims, kind=bf16):
    return jax.ShapeDtypeStruct(dims, kind)


def halves(core, width):
    half = width // 2
    own = pl.ds(pl.multiple_of(core * half, 128), half)
    other = pl.ds(pl.multiple_of((1 - core) * half, 128), half)
    return own, other


def norm(value):
    centred = value - jnp.mean(value, axis=-1, keepdims=True)
    inverse = lax.rsqrt(jnp.mean(centred * centred, axis=-1, keepdims=True) + EPS)
    return centred * inverse, inverse


def norm_gradient(grad, normed, inverse, gain):
    scaled = grad * gain
    return inverse * (
        scaled
        - jnp.mean(scaled, axis=-1, keepdims=True)
        - normed * jnp.mean(scaled * normed, axis=-1, keepdims=True)
    )


def project_kernel(sc, x, w_own, w_other, b_qv, rows, low, qt, kt, vt):
    own, other = halves(sc[2], x.shape[1])
    cols = qt.shape[0]
    normed, _ = norm(x[...].astype(f32))
    low[...] = (normed * rows[0:1, :] + rows[1:2, :]).astype(bf16)
    projected = nn(low[:, own], w_own[...]) + nn(low[:, other], w_other[...])
    qt[...] = ((projected[:, :cols] + b_qv[0:1, :]) * SCALE).T.astype(bf16)
    kt[...] = projected[:, cols : 2 * cols].T.astype(bf16)
    vt[...] = (projected[:, 2 * cols :] + b_qv[1:2, :]).T.astype(bf16)


def project(place, x, w_own, w_other, b_qv, table):
    tok, width = x.shape
    cols = b_qv.shape[1]
    rows = min(256, tok)
    fixed = lambda a: pl.BlockSpec(a.shape, lambda i: (0,) * a.ndim)
    across = pl.BlockSpec((cols, rows), lambda i: (0, i))
    return pl.pallas_call(
        project_kernel,
        grid=(tok // rows,),
        in_specs=[SM, pl.BlockSpec((rows, width), lambda i: (i, 0))]
        + [fixed(a) for a in (w_own, w_other, b_qv, table)],
        out_specs=[pl.BlockSpec((rows, width), lambda i: (i, 0)), across, across, across],
        out_shape=[shape((tok, width))] + [shape((cols, tok))] * 3,
        compiler_params=params(),
        cost_estimate=cost(7),
        name="project",
    )(place, x, w_own, w_other, b_qv, table)


def key_loop(sc, i, step, carry):
    lo, full, diag, end = sc[4 * i + 4], sc[4 * i + 5], sc[4 * i + 6], sc[4 * i + 7]
    carry = lax.fori_loop(lo, full, functools.partial(step, True), carry)
    carry = lax.fori_loop(full, diag, functools.partial(step, False), carry)
    return lax.fori_loop(diag, end, functools.partial(step, True), carry)


def tile_mask(j, bk, bq, start, qpos):
    kpos = j * bk + lax.broadcasted_iota(jnp.int32, (bk, bq), 0)
    return (kpos >= start) & (kpos <= qpos)


def load_keys(sc, kv, held, sems):
    if len(kv) == 1:
        copies = [pltpu.make_async_copy(kv[0], held, sems.at[0])]
    else:
        k, k_x, k_yd, v, v_y, v_xd = kv
        rows = k.shape[0]
        pieces = [(k, 0, 0), (k_x, 0, 1), (k_yd.at[0], 0, 2), (k_yd.at[1], 0, 3)]
        pieces += [(v, 1, 0), (v_y, 1, 2), (v_xd.at[0], 1, 1), (v_xd.at[1], 1, 3)]
        copies = [
            pltpu.make_async_copy(
                piece, held.at[sc[1] ^ run, pl.ds(which * rows, rows), :], sems.at[n]
            )
            for n, (piece, which, run) in enumerate(pieces)
        ]
    for copy in copies:
        copy.start()
    for copy in copies:
        copy.wait()


def attend_kernel(first_head, heads, bk, bq, parts, n_kv, sc, qt, st, *refs):
    kv, refs = refs[:n_kv], refs[n_kv:]
    lse, ot, out, (held, acc, sems) = refs[0], refs[1], refs[2 : 2 + parts], refs[2 + parts :]
    i = pl.program_id(0)
    per = held.shape[2] // bk
    cols = heads * HD
    start = st[...]
    qpos = sc[0] + i * bq + lax.broadcasted_iota(jnp.int32, (1, bq), 1)

    @pl.when(i == 0)
    def _():
        load_keys(sc, kv, held, sems)

    acc[...] = jnp.zeros_like(acc)

    def step(masked, j, carry):
        r = j // per
        off = pl.multiple_of((j % per) * bk, bk)
        new = []
        if masked:
            ok = tile_mask(j, bk, bq, start, qpos)
        for h in range(heads):
            m, l = carry[h]
            hs = slice(h * HD, (h + 1) * HD)
            s = tn(
                held[r, hs, pl.ds(off, bk)],
                qt[(first_head + h) * HD : (first_head + h + 1) * HD, :],
            )
            if masked:
                s = jnp.where(ok, s, NEG)
            m2 = jnp.maximum(m, jnp.max(s, axis=0, keepdims=True))
            p = jnp.exp(s - m2)
            al = jnp.exp(m - m2)
            l = l * al + jnp.sum(p, axis=0, keepdims=True)
            v = held[r, cols + h * HD : cols + (h + 1) * HD, pl.ds(off, bk)]
            acc[hs, :] = acc[hs, :] * al + nn(v, p.astype(bf16))
            new.append((m2, l))
        return tuple(new)

    one = (jnp.full((1, bq), NEG, f32), jnp.zeros((1, bq), f32))
    res = key_loop(sc, i, step, (one,) * heads)
    here = pl.ds(pl.multiple_of(i * bq, bq), bq)
    for h in range(heads):
        m, l = res[h]
        ot[h * HD : (h + 1) * HD, here] = (acc[h * HD : (h + 1) * HD, :] / l).astype(bf16)
        lse[h : h + 1, :] = m + jnp.log(l)

    @pl.when(i == pl.num_programs(0) - 1)
    def _():
        send_parts(sc[3], ot, out)


def send_parts(me, source, out):
    parts, size = len(out), out[0].shape[1]
    for d in range(parts):
        if size % 128 == 0:
            at = pl.multiple_of(lax.rem(me + d, parts) * size, 128)
            out[d][...] = source[:, pl.ds(at, size)].astype(out[d].dtype)
        else:
            for n in range(parts):

                @pl.when(lax.rem(me + d, parts) == n)
                def _():
                    out[d][...] = source[:, n * size : (n + 1) * size].astype(out[d].dtype)


def take_parts(me, rows, parts, target):
    size = parts[0].shape[1]
    for d in range(len(parts)):
        if size % 128 == 0:
            at = pl.multiple_of(lax.rem(me + d, len(parts)) * size, 128)
            target[:, pl.ds(at, size)] = parts[d][rows, :]
        else:
            for n in range(len(parts)):

                @pl.when(lax.rem(me + d, len(parts)) == n)
                def _():
                    target[:, n * size : (n + 1) * size] = parts[d][rows, :]


def attend(scalars, starts, qt, kv, first_head, heads, bk, bq, parts):
    tok = qt.shape[1]
    cols = heads * HD
    runs = kv[0].shape[0] if len(kv) == 1 else 4
    bk, bq = min(bk, tok), min(bq, tok)
    whole = lambda a, b: pl.BlockSpec((a, b), lambda i: (0, 0))
    return pl.pallas_call(
        functools.partial(attend_kernel, first_head, heads, bk, bq, parts, len(kv)),
        grid=(tok // bq,),
        in_specs=[
            SM,
            pl.BlockSpec((qt.shape[0], bq), lambda i: (0, i)),
            pl.BlockSpec((1, bq), lambda i: (0, i)),
        ]
        + [HBM] * len(kv),
        out_specs=[pl.BlockSpec((heads, bq), lambda i: (0, i)), whole(cols, tok)]
        + [whole(cols, tok // parts)] * parts,
        scratch_shapes=[
            pltpu.VMEM((runs, 2 * cols, tok), bf16),
            pltpu.VMEM((cols, bq), f32),
            pltpu.SemaphoreType.DMA((8,)),
        ],
        out_shape=[shape((heads, tok), f32), shape((cols, tok))]
        + [shape((cols, tok // parts))] * parts,
        compiler_params=params(),
        cost_estimate=cost(20),
        name="attend",
    )(scalars(bk, bq), qt, starts, *kv)


def attend_back_kernel(first_head, heads, bk, bq, parts, n_kv, sc, qt, st, lse, ot, *refs):
    do_parts, refs = refs[:parts], refs[parts:]
    kv, refs = refs[:n_kv], refs[n_kv:]
    n_out = 1 if n_kv == 1 else 4
    dq, dkv, (held, acc, dqa, do_all, sems) = (
        refs[:parts],
        refs[parts : parts + n_out],
        refs[parts + n_out :],
    )
    i = pl.program_id(0)
    per = held.shape[2] // bk
    cols = heads * HD
    start = st[...]
    qpos = sc[0] + i * bq + lax.broadcasted_iota(jnp.int32, (1, bq), 1)
    here = pl.ds(pl.multiple_of(i * bq, bq), bq)

    @pl.when(i == 0)
    def _():
        acc[...] = jnp.zeros_like(acc)
        dqa[...] = jnp.zeros_like(dqa)
        take_parts(sc[3], slice(first_head * HD, (first_head + heads) * HD), do_parts, do_all)
        load_keys(sc, kv, held, sems)

    delta = [
        jnp.sum(
            do_all[h * HD : (h + 1) * HD, here].astype(f32)
            * ot[h * HD : (h + 1) * HD, :].astype(f32),
            axis=0,
            keepdims=True,
        )
        for h in range(heads)
    ]

    def step(masked, j, carry):
        r = j // per
        off = pl.multiple_of((j % per) * bk, bk)
        if masked:
            ok = tile_mask(j, bk, bq, start, qpos)
        for h in range(heads):
            hs = slice(h * HD, (h + 1) * HD)
            vs = slice(cols + h * HD, cols + (h + 1) * HD)
            k = held[r, hs, pl.ds(off, bk)]
            v = held[r, vs, pl.ds(off, bk)]
            q = qt[(first_head + h) * HD : (first_head + h + 1) * HD, :]
            do = do_all[hs, here]
            s = tn(k, q) - lse[h : h + 1, :]
            if masked:
                s = jnp.where(ok, s, NEG)
            p = jnp.exp(s)
            ds = (p * (tn(v, do) - delta[h])).astype(bf16)
            acc[r, vs, pl.ds(off, bk)] += nt(do, p.astype(bf16))
            acc[r, hs, pl.ds(off, bk)] += nt(q, ds)
            dqa[hs, here] += nn(k, ds)
        return carry

    key_loop(sc, i, step, 0)

    @pl.when(i == pl.num_programs(0) - 1)
    def _():
        dqa[...] = dqa[...] * SCALE
        send_parts(sc[3], dqa, dq)
        if n_out == 1:
            dkv[0][...] = acc[...].astype(bf16)
        else:
            for target, pair, rows in (
                (0, (0, 2), slice(0, cols)),
                (1, (1, 3), slice(0, cols)),
                (2, (0, 1), slice(cols, 2 * cols)),
                (3, (2, 3), slice(cols, 2 * cols)),
            ):
                for n in range(2):
                    dkv[target][n] = acc[sc[1] ^ pair[n], rows, :].astype(bf16)


def attend_back(scalars, starts, qt, lse, ot, do_parts, kv, first_head, heads, bk, bq):
    tok = qt.shape[1]
    cols = heads * HD
    parts = len(do_parts)
    runs = kv[0].shape[0] if len(kv) == 1 else 4
    bk, bq = min(bk, tok), min(bq, tok)
    whole = lambda *dims: pl.BlockSpec(dims, lambda i: (0,) * len(dims))
    out_kv = [(runs, 2 * cols, tok)] if len(kv) == 1 else [(2, cols, tok)] * 4
    return pl.pallas_call(
        functools.partial(attend_back_kernel, first_head, heads, bk, bq, parts, len(kv)),
        grid=(tok // bq,),
        in_specs=[
            SM,
            pl.BlockSpec((qt.shape[0], bq), lambda i: (0, i)),
            pl.BlockSpec((1, bq), lambda i: (0, i)),
            pl.BlockSpec((heads, bq), lambda i: (0, i)),
            pl.BlockSpec((cols, bq), lambda i: (0, i)),
        ]
        + [whole(*d.shape) for d in do_parts]
        + [HBM] * len(kv),
        out_specs=[whole(cols, tok // parts)] * parts + [whole(*d) for d in out_kv],
        scratch_shapes=[
            pltpu.VMEM((runs, 2 * cols, tok), bf16),
            pltpu.VMEM((runs, 2 * cols, tok), f32),
            pltpu.VMEM((cols, tok), f32),
            pltpu.VMEM((cols, tok), bf16),
            pltpu.SemaphoreType.DMA((8,)),
        ],
        out_shape=[shape((cols, tok // parts))] * parts + [shape(d) for d in out_kv],
        compiler_params=params(),
        cost_estimate=cost(26),
        name="attend_back",
    )(scalars(bk, bq), qt, starts, lse, ot, *do_parts, *kv)


ROOT = 0.7978845608028654


def middle_kernel(n_att, parts, sc, *refs):
    att, refs = refs[:n_att], refs[n_att:]
    x, cot, of_own, of_other, dn_own, dn_other, rows = refs[:7]
    refs = refs[7:]
    outputs, grad_mid, sums, fc_sums = refs[:4]
    d_att, (g_own, g_other) = refs[4 : 4 + parts], refs[4 + parts : 6 + parts]
    mid, att_t, low, low_t, cot_t, mlp, back = refs[6 + parts :]
    d = pl.program_id(0)
    width = x.shape[1]
    own, other = halves(sc[2], width)
    half = width // 2
    ffw = dn_own.shape[1]
    count = ffw // half
    cols = att_t.shape[0] // parts
    b_out, b_down, gain, shift = (rows[n : n + 1, :] for n in range(2, 6))

    @pl.when(d == 0)
    def _():
        group = n_att // parts
        row = 0
        for part in range(parts):
            for g in range(group):
                piece = att[part * group + g]
                att_t[row : row + piece.shape[0], :] = piece[...]
                row += piece.shape[0]
        att_low = att_t[...].T
        mine = theirs = 0.0
        for part in range(parts):
            piece = att_low[:, part * cols : (part + 1) * cols]
            mine += nn(piece, of_own[part, :cols, :])
            theirs += nn(piece, of_other[part, :cols, :])
        mid[:, own] = mine
        mid[:, other] = theirs
        mid[...] = x[...].astype(f32) + mid[...] + b_out
        normed, _ = norm(mid[...])
        low[...] = (normed * gain + shift).astype(bf16)
        low_t[...] = low[...].T
        cot_t[...] = cot[...].T
        mlp[...] = jnp.zeros_like(mlp)
        back[...] = jnp.zeros_like(back)

    own_rows = pl.ds(pl.multiple_of(sc[2] * half, half), half)
    other_rows = pl.ds(pl.multiple_of((1 - sc[2]) * half, half), half)
    terms = of_own[d, cols : cols + 16, :].astype(f32)
    pieces = [slice(cols + 16 + n * half, cols + 16 + (n + 1) * half) for n in range(count)]
    u = [
        nn(low[:, own], of_own[d, at, :])
        + nn(low[:, other], of_other[d, at, :])
        + sum(terms[t * count + n : t * count + n + 1, :] for t in range(3))
        for n, at in enumerate(pieces)
    ]
    u = jnp.concatenate(u, axis=1)
    t = jnp.tanh(ROOT * (u + 0.044715 * (u * u * u)))
    act = (0.5 * u * (1.0 + t)).astype(bf16)
    slope = 0.5 * (1.0 + t) + (0.5 * ROOT) * u * (1.0 - t * t) * (1.0 + 0.134145 * (u * u))
    d_act = nt(cot[:, own], dn_own[0]) + nt(cot[:, other], dn_other[0])
    dh = (d_act * slope).astype(bf16)
    mlp[:, own] += nn(act, dn_own[0])
    mlp[:, other] += nn(act, dn_other[0])
    for n, at in enumerate(pieces):
        dh_n = dh[:, n * half : (n + 1) * half]
        back[:, own] += nt(dh_n, of_own[d, at, :])
        back[:, other] += nt(dh_n, of_other[d, at, :])
    g_own[d, :, :ffw] = nn(low_t[own_rows, :], dh).astype(bf16)
    g_other[d, :, :ffw] = nn(low_t[other_rows, :], dh).astype(bf16)
    g_own[d, :, ffw : 2 * ffw] = nn(cot_t[own_rows, :], act).astype(bf16)
    g_other[d, :, ffw : 2 * ffw] = nn(cot_t[other_rows, :], act).astype(bf16)
    fc_sums[lax.rem(sc[3] - d + parts, parts)] = jnp.sum(dh.astype(f32), axis=0, keepdims=True)

    @pl.when(d == parts - 1)
    def _():
        normed, inverse = norm(mid[...])
        outputs[...] = (mid[...] + mlp[...] + b_down).astype(bf16)
        upper = cot[...].astype(f32)
        grad = back[...]
        down = upper + norm_gradient(grad, normed, inverse, gain)
        grad_mid[...] = down
        sums[0:1, :] = jnp.sum(down, axis=0, keepdims=True)
        sums[1:2, :] = jnp.sum(upper, axis=0, keepdims=True)
        sums[2:3, :] = jnp.sum(grad * normed, axis=0, keepdims=True)
        sums[3:4, :] = jnp.sum(grad, axis=0, keepdims=True)
        low[...] = down.astype(bf16)
        low_t[...] = low[...].T
        g_own[:, :, 2 * ffw + cols :] = jnp.zeros_like(g_own[:, :, 2 * ffw + cols :])
        g_other[:, :, 2 * ffw + cols :] = jnp.zeros_like(g_other[:, :, 2 * ffw + cols :])
        for part in range(parts):
            at = slice(part * cols, (part + 1) * cols)
            g_own[part, :, 2 * ffw : 2 * ffw + cols] = nt(low_t[own_rows, :], att_t[at, :]).astype(bf16)
            g_other[part, :, 2 * ffw : 2 * ffw + cols] = nt(low_t[other_rows, :], att_t[at, :]).astype(bf16)
            d_att[part][...] = (
                nt(of_own[part, :cols, :], low[:, own]) + nt(of_other[part, :cols, :], low[:, other])
            ).astype(bf16)


def middle(place, att, x, cot, of, dn, cols, table):
    parts, ffw, half = dn[0].shape
    sub, width = x.shape
    whole = lambda *dims: pl.BlockSpec(
        dims, lambda i, sc: (0,) * len(dims), pipeline_mode=pl.Buffered(1)
    )
    placed = pl.BlockSpec(
        (1, ffw, half), lambda i, sc: (i, 0, 0)
    )
    once = lambda a: whole(*a.shape)
    grads = (parts, half, 128 * ((2 * ffw + cols + 127) // 128))
    return pl.pallas_call(
        functools.partial(middle_kernel, len(att), parts),
        grid_spec=pltpu.PrefetchScalarGridSpec(
            num_scalar_prefetch=1,
            grid=(parts,),
            in_specs=[once(a) for a in att]
            + [once(x), once(cot), once(of[0]), once(of[1]), placed, placed, once(table)],
            out_specs=[whole(sub, width), whole(sub, width), whole(4, width), whole(parts, 1, ffw)]
            + [whole(cols, sub)] * parts
            + [whole(*grads)] * 2,
            scratch_shapes=[
                pltpu.VMEM((sub, width), f32),
                pltpu.VMEM((parts * cols, sub), bf16),
                pltpu.VMEM((sub, width), bf16),
                pltpu.VMEM((width, sub), bf16),
                pltpu.VMEM((width, sub), bf16),
                pltpu.VMEM((sub, width), f32),
                pltpu.VMEM((sub, width), f32),
            ],
        ),
        out_shape=[
            shape((sub, width)),
            shape((sub, width), f32),
            shape((4, width), f32),
            shape((parts, 1, ffw), f32),
        ]
        + [shape((cols, sub))] * parts
        + [shape(grads)] * 2,
        compiler_params=params(),
        cost_estimate=cost(19),
        name="middle",
    )(place, *att, x, cot, of[0], of[1], dn[0], dn[1], table)


def last_kernel(parts, pieces, sc, *refs):
    grads, refs = refs[: parts * pieces], refs[parts * pieces :]
    w_own, w_other, x, grad_mid, rows, mid_sums, fc_sums, out, sums, back_t, stacked = refs
    half = w_own.shape[1]
    wide = w_own.shape[2]
    own_rows = pl.ds(pl.multiple_of(sc[2] * half, half), half)
    other_rows = pl.ds(pl.multiple_of((1 - sc[2]) * half, half), half)
    ones = jnp.ones((8, x.shape[0]), bf16)
    sums[...] = jnp.zeros_like(sums)
    stacked[...] = jnp.zeros_like(stacked)
    for part in range(parts):
        row = 0
        for n in range(pieces):
            piece = grads[part * pieces + n]
            stacked[row : row + piece.shape[0], :] = piece[...]
            row += piece.shape[0]
        at = lax.rem(sc[3] - part + parts, parts)
        mine, theirs = nn(w_own[at], stacked[...]), nn(w_other[at], stacked[...])
        if part == 0:
            back_t[own_rows, :], back_t[other_rows, :] = mine, theirs
        else:
            back_t[own_rows, :] += mine
            back_t[other_rows, :] += theirs
        sums[pl.ds(6 + parts + at, 1), :wide] = nt(ones, stacked[...])[0:1, :]
    back = back_t[...].T
    normed, inverse = norm(x[...].astype(f32))
    out[...] = (grad_mid[...] + norm_gradient(back, normed, inverse, rows[0:1, :])).astype(bf16)
    sums[0:4, :] = mid_sums[...]
    sums[4:5, :] = jnp.sum(back * normed, axis=0, keepdims=True)
    sums[5:6, :] = jnp.sum(back, axis=0, keepdims=True)
    for part in range(parts):
        sums[6 + part : 7 + part, :] = fc_sums[part]


def last(place, grads, pieces, w, x, grad_mid, table, mid_sums, fc_sums):
    parts = w[0].shape[0]
    sub, width = x.shape
    rows = 8 * ((6 + 2 * parts + 7) // 8)
    return pl.pallas_call(
        functools.partial(last_kernel, parts, pieces),
        in_specs=[SM] + [VM] * (len(grads) + 7),
        out_specs=[VM, VM],
        out_shape=[shape((sub, width)), shape((rows, width), f32)],
        scratch_shapes=[pltpu.VMEM((width, sub), f32), pltpu.VMEM((w[0].shape[2], sub), bf16)],
        compiler_params=params(),
        cost_estimate=cost(6),
        name="last",
    )(place, *grads, w[0], w[1], x, grad_mid, table, mid_sums, fc_sums)


def fold_kernel(cut, sc, mine, theirs, lo_send, lo_keep, hi_send, hi_keep):
    i = pl.program_id(0)
    total = (mine[...].astype(f32) + theirs[...].astype(f32)).astype(bf16)
    lo, hi = total[None, :, :, :cut], total[None, :, :, cut:]

    @pl.when(i < 2)
    def _():
        lo_send[...] = lo

    @pl.when(i >= 2)
    def _():
        lo_keep[...] = lo

    @pl.when((i == 1) | (i == 2))
    def _():
        hi_send[...] = hi

    @pl.when((i == 0) | (i == 3))
    def _():
        hi_keep[...] = hi


def fold(place, mine, theirs):
    parts, rows, wide = mine.shape
    size = rows // 4
    cut = (wide // 256) * 128 if wide % 256 == 0 else (wide // 256 + 1) * 128
    block = pl.BlockSpec(
        (parts, size, wide),
        lambda i, sc: (
            0,
            sc[1] ^ jnp.where(i == 0, 1, jnp.where(i == 1, 3, jnp.where(i == 2, 2, 0))),
            0,
        ),
    )
    out = lambda width, index: pl.BlockSpec(
        (1, parts, size, width), lambda i, sc: (index(i), 0, 0, 0)
    )
    lo, hi = cut, wide - cut
    return pl.pallas_call(
        functools.partial(fold_kernel, cut),
        grid_spec=pltpu.PrefetchScalarGridSpec(
            num_scalar_prefetch=1,
            grid=(4,),
            in_specs=[block, block],
            out_specs=[
                out(lo, lambda i: jnp.minimum(i, 1)),
                out(lo, lambda i: jnp.where(i == 3, 0, 1)),
                out(hi, lambda i: jnp.where(i < 2, 1, 0)),
                out(hi, lambda i: jnp.where(i == 3, 0, 1)),
            ],
        ),
        out_shape=[
            shape((2, parts, size, lo)),
            shape((2, parts, size, lo)),
            shape((2, parts, size, hi)),
            shape((2, parts, size, hi)),
        ],
        compiler_params=params(),
        cost_estimate=cost(1 + 6 * parts / 4),
        name="fold",
    )(place, mine, theirs)


def body(
    n_shard,
    n_context,
    n_tensor,
    inputs,
    segments,
    w_qkv,
    w_out,
    w_fc,
    w_down,
    b_qv,
    b_out,
    b_fc,
    b_down,
    first_norm_gain,
    first_norm_bias,
    second_norm_gain,
    second_norm_bias,
    cotangent,
):
    _, tok, width = inputs.shape
    length = segments.shape[1]
    half, _, cols = w_qkv.shape
    heads = cols // HD
    ffw = w_fc.shape[1]
    sub = tok // n_tensor
    context = lax.axis_index("context")
    tensor = lax.axis_index("tensor")
    core = lax.axis_index("shard")
    first = context * tok
    place = jnp.stack([first, context, core, tensor]).astype(jnp.int32)
    grouped = n_context == 4
    x = inputs[0]
    cot = cotangent[0]
    row = lambda v: v[None, :]
    zero = jnp.zeros_like(b_out)
    table = jnp.concatenate(
        [
            first_norm_gain,
            first_norm_bias,
            b_out,
            b_down,
            second_norm_gain,
            second_norm_bias,
            zero,
            zero,
        ]
    ).reshape(8, width)
    after = lambda v, dep: lax.optimization_barrier((v, dep))[0]

    swap = lambda v: lax.ppermute(v, "shard", [(0, 1), (1, 0)])
    along_x = lambda v: lax.ppermute(v, "context", [(0, 1), (1, 0), (2, 3), (3, 2)])
    along_y = lambda v: lax.ppermute(v, "context", [(0, 2), (2, 0), (1, 3), (3, 1)])
    shift_by = lambda v, d: lax.ppermute(
        v, "tensor", [(s, (s + d) % n_tensor) for s in range(n_tensor)]
    )

    def gather_direct(v):
        return [v] + [shift_by(v, d) for d in range(1, n_tensor)]

    def gather_begin(v):
        if n_tensor != 4:
            return tuple(gather_direct(v))
        move = lambda perm: lax.ppermute(v, "tensor", perm)
        return (
            v,
            move([(0, 2), (1, 3), (2, 0), (3, 1)]),
            move([(0, 1), (1, 2), (2, 3)]),
            move([(3, 2), (2, 1), (1, 0)]),
        )

    def gather_end(state, hold=()):
        if n_tensor != 4:
            return list(state)
        v, two, right, left = state
        two = after(two, hold)
        far = lax.ppermute(two, "tensor", [(2, 3), (1, 0)])
        return [
            v,
            jnp.where(tensor == 0, far, right),
            two,
            jnp.where(tensor == 3, far, left),
        ]

    def scatter_line(pieces):
        if n_tensor != 4:
            total = pieces[0].astype(f32)
            for d in range(1, n_tensor):
                total += shift_by(pieces[d].astype(bf16), -d).astype(f32)
            return total
        move = lambda a, perm: lax.ppermute(a.astype(bf16), "tensor", perm)
        far = move(jnp.where(tensor == 0, pieces[1], pieces[3]), [(0, 1), (3, 2)])
        right = move(pieces[3], [(0, 1), (1, 2), (2, 3)])
        left = move(pieces[1], [(3, 2), (2, 1), (1, 0)])
        two = move(
            pieces[2].astype(f32) + far.astype(f32), [(0, 2), (1, 3), (2, 0), (3, 1)]
        )
        return (
            pieces[0].astype(f32) + right.astype(f32) + left.astype(f32) + two.astype(f32)
        )

    def scatter_begin(mine, theirs):
        theirs = swap(theirs)
        if not grouped:
            both = (mine.astype(f32) + theirs.astype(f32)).astype(bf16)
            return lax.psum_scatter(both, "context", scatter_dimension=1, tiled=True)
        return fold(place, mine, theirs)

    def scatter_first(state):
        if not grouped:
            return state
        lo_send, lo_keep, hi_send, hi_keep = state
        r, s = along_x(lo_send).astype(f32), along_y(hi_send).astype(f32)
        return (
            lo_keep[0].astype(f32) + r[0],
            hi_keep[0].astype(f32) + s[0],
            (lo_keep[1].astype(f32) + r[1]).astype(bf16),
            (hi_keep[1].astype(f32) + s[1]).astype(bf16),
        )

    def scatter_second(state):
        if not grouped:
            return state
        lo, hi, lo_send, hi_send = state
        lo += along_y(lo_send).astype(f32)
        hi += along_x(hi_send).astype(f32)
        return jnp.concatenate([lo, hi], axis=2)

    bounds = [jnp.sum((segments[0] < d).astype(jnp.int32)) for d in range(1, 5)]
    seg = lax.dynamic_slice_in_dim(segments[0], first, tok, 0)
    starts = jnp.zeros_like(seg)
    for d in range(1, 5):
        starts = jnp.where(seg == d, bounds[d - 1], starts)

    def scalars(bk, bq):
        count = tok // bq
        begin = starts.reshape(count, bq)
        base = first + jnp.arange(count, dtype=jnp.int32) * bq
        lo = begin[:, 0] // bk
        diag = base // bk
        end = (base + bq + bk - 1) // bk
        full = jnp.minimum(jnp.maximum((begin[:, -1] + bk - 1) // bk, lo), diag)
        table = jnp.stack([lo, full, diag, end], axis=1).reshape(-1)
        return jnp.concatenate([place, table.astype(jnp.int32)])

    qkv_own = w_qkv.reshape(half, 3 * cols)
    low_one, qt, kt, vt = project(
        place,
        x,
        qkv_own,
        swap(qkv_own),
        b_qv,
        table,
    )

    terms, rest = [], b_fc
    for _ in range(3):
        term = lax.reduce_precision(rest, 8, 7)
        terms.append(term.astype(bf16).reshape(ffw // half, half))
        rest = rest - term
    terms = jnp.concatenate(terms, axis=0)
    terms = jnp.pad(terms, ((0, 16 - terms.shape[0]), (0, 0)))
    packed = jnp.concatenate([w_out, terms, w_fc[:, :half], w_fc[:, half:]], axis=0)
    packed = gather_begin(packed)
    kv = []
    hold = ()
    head = 0
    for g in GROUPS:
        rows = slice(head * HD, (head + g) * HD)
        head += g
        k, v = kt[rows], vt[rows]
        if grouped:
            kx, vy = along_x(k), along_y(v)
            k_two, v_two = jnp.stack([k, kx]), jnp.stack([v, vy])
            k_two, v_two = after((k_two, v_two), packed[1])
            k_yd, v_xd = along_y(k_two), along_x(v_two)
            hold = (k_two, v_two)
            kv.append([k, kx, k_yd, v, vy, v_xd])
        else:
            kv.append([lax.all_gather(jnp.concatenate([k, v], axis=0), "context", axis=0)])

    dn = gather_begin(after(w_down, packed[1]))
    saved = []
    att = [[] for _ in range(n_tensor)]
    head = 0
    for g, held in zip(GROUPS, kv):
        results = attend(scalars, row(starts), after(qt, packed[1:]), held, head, g, BK_F, BQ_F, n_tensor)
        lse, ot, *out = after(results, dn[1:])
        saved.append((lse, ot))
        att[0].append(out[0])
        for d in range(1, n_tensor):
            att[d].append(shift_by(out[d], d))
        head += g

    of = jnp.stack(after(gather_end(packed, hold), saved[-1][0]))
    of = (of, swap(of))
    dn = jnp.stack(gather_end(dn, saved[-1][0]))
    dn = (dn, swap(dn))
    x_sub = lax.dynamic_slice_in_dim(x, tensor * sub, sub, 0)
    cot_sub = lax.dynamic_slice_in_dim(cot, tensor * sub, sub, 0)
    outputs_sub, grad_mid, mid_sums, fc_sums, *rest = middle(
        place,
        [piece for part in att for piece in part],
        x_sub,
        cot_sub,
        of,
        dn,
        cols,
        table,
    )
    d_att, (g_own, g_other) = rest[:n_tensor], rest[n_tensor:]
    do_parts = [d_att[0]] + [
        shift_by(d_att[d], -d) for d in range(1, n_tensor)
    ]

    def spread(pieces):
        whole = jnp.zeros((tok, width), f32)
        for d in range(n_tensor):
            at = lax.rem(tensor - d + n_tensor, n_tensor) * sub
            whole = lax.dynamic_update_slice_in_dim(whole, pieces[d].astype(f32), at, 0)
        return whole[None]

    folded = scatter_begin(g_own, g_other)
    hop_one = folded[0] if grouped else folded
    outputs = gather_begin(after(outputs_sub, do_parts))
    wide = scatter_first(folded)
    wide_sends = wide[2:]
    wide = scatter_second(wide)

    dq_pieces, dkv_pieces, dqkv = [], [], []
    head = 0
    queries, keys, values = [], [], []
    sent = [[] for _ in range(n_tensor)]
    for g, held, (lse, ot) in zip(GROUPS, kv, saved):
        out = attend_back(
            scalars, row(starts), after(qt, hop_one), lse, ot, do_parts, held, head, g, BK_B, BQ_B
        )
        back_done = out[-1]
        dq, dkv = after(out[:n_tensor], (outputs[1:3], wide_sends)), out[n_tensor:]
        if grouped:
            dk_keep, dk_send, dv_keep, dv_send = dkv
            dk_send, dv_send = after((dk_send, dv_send), (wide_sends, outputs[1:3]))
            r = along_x(dk_send).astype(f32)
            s = along_y(dv_send).astype(f32)
            r2 = along_y((dk_keep[1].astype(f32) + r[1]).astype(bf16)).astype(f32)
            s2 = along_x((dv_keep[1].astype(f32) + s[1]).astype(bf16)).astype(f32)
            back_done = (r2, s2)
            dk = (dk_keep[0].astype(f32) + r[0] + r2).astype(bf16)
            dv = (dv_keep[0].astype(f32) + s[0] + s2).astype(bf16)
        else:
            both = lax.psum_scatter(dkv[0], "context", scatter_dimension=0, tiled=True)[0]
            dk, dv = both[: g * HD], both[g * HD :]
        queries.append(dq)
        keys.append(dk)
        values.append(dv)
        head += g

    wide_grads = scatter_line([wide[d] for d in range(n_tensor)])

    def part_of(v, d):
        at = lax.rem(tensor + d, n_tensor) * sub
        return lax.dynamic_slice_in_dim(v, at, sub, 1)

    grads = []
    both = jnp.concatenate(keys + values, axis=0)
    for d in range(n_tensor):
        pieces = [q[d] for q in queries] + [part_of(both, d)]
        grads += pieces if d == 0 else [shift_by(p, d) for p in pieces]
    pieces = len(GROUPS) + 1

    dq_whole = []
    for q in queries:
        whole = jnp.zeros((q[0].shape[0], tok), bf16)
        for d in range(n_tensor):
            at = lax.rem(tensor + d, n_tensor) * sub
            whole = lax.dynamic_update_slice_in_dim(whole, q[d], at, 1)
        dq_whole.append(whole)
    qkv_wide = jnp.pad(qkv_own, ((0, 0), (0, -3 * cols % 128)))
    qkv = lax.all_gather(after(qkv_wide, out[-1]), "tensor", axis=0)
    qkv = (qkv, swap(qkv))
    input_sub, small = last(
        place, grads, pieces, qkv, x_sub, grad_mid, table, mid_sums, fc_sums
    )
    input_gradient = spread(gather_direct(input_sub))
    outputs = spread(after(gather_end(outputs, back_done), input_sub))
    stacked = jnp.concatenate(
        dq_whole + [both, jnp.zeros((-3 * cols % 128, tok), bf16)], axis=0
    )
    qkv_grad = jnp.einsum(
        "td,ct->dc", low_one, after(stacked, input_sub), preferred_element_type=f32
    ).astype(bf16)
    qkv_mine = lax.dynamic_slice_in_dim(qkv_grad, core * half, half, 0)
    qkv_theirs = lax.dynamic_slice_in_dim(qkv_grad, (1 - core) * half, half, 0)
    qkv_grads = scatter_second(scatter_first(scatter_begin(qkv_mine[None], qkv_theirs[None])))[0]

    if grouped and n_tensor == 4 and n_shard == 2:
        small += swap(small)
        small += along_x(small)
        small += along_y(small)
        small += lax.ppermute(small, "tensor", [(0, 1), (1, 0), (2, 3), (3, 2)])
        small += lax.ppermute(small, "tensor", [(0, 2), (2, 0), (1, 3), (3, 1)])
    else:
        small = lax.psum(small, ("shard", "context", "tensor"))
    fc_total = lax.dynamic_index_in_dim(small, 6 + tensor, 0, keepdims=False)
    qv_total = lax.dynamic_index_in_dim(small, 6 + n_tensor + tensor, 0, keepdims=False)
    qv_total = jnp.stack([qv_total[:cols], qv_total[2 * cols : 3 * cols]])
    return (
        outputs,
        input_gradient,
        qkv_grads[:, : 3 * cols].astype(f32).reshape(-1, 3, cols),
        wide_grads[:, 2 * ffw : 2 * ffw + cols].T,
        wide_grads[:, :ffw],
        wide_grads[:, ffw : 2 * ffw].T,
        qv_total,
        small[0],
        fc_total,
        small[1],
        small[4],
        small[5],
        small[2],
        small[3],
    )


def solution(mesh):
    sizes = dict(mesh.shape)
    placed = (
        P("shard", "context", None),
        P("shard", None),
        P("shard", None, "tensor"),
        P("tensor", "shard"),
        P("shard", "tensor"),
        P("tensor", "shard"),
        P(None, "tensor"),
        P(),
        P("tensor"),
        P(),
        P(),
        P(),
        P(),
        P(),
        P("shard", "context", None),
    )
    return jax.shard_map(
        functools.partial(body, sizes["shard"], sizes["context"], sizes["tensor"]),
        mesh=mesh,
        in_specs=placed,
        out_specs=(
            P("shard", "context", None),
            P("shard", "context", None),
            P(("shard", "context"), None, "tensor"),
            P("tensor", ("shard", "context")),
            P(("shard", "context"), "tensor"),
            P("tensor", ("shard", "context")),
            P(None, "tensor"),
            P(),
            P("tensor"),
            P(),
            P(),
            P(),
            P(),
            P(),
        ),
        check_vma=False,
    )
```

```python
import functools

import jax
import jax.numpy as jnp
from jax import lax
from jax.experimental import pallas as pl
from jax.experimental.pallas import tpu as pltpu
from jax.sharding import PartitionSpec as P

HD = 64
EPS = 1e-05
NEG = -1e30
SCALE = float(HD) ** -0.5
VMEM_LIMIT = 56 * 1024 * 1024
GROUPS = (3,)
BK_F, BQ_F = 512, 512
BK_B, BQ_B = 512, 512
f32 = jnp.float32
bf16 = jnp.bfloat16
VM = pl.BlockSpec(memory_space=pltpu.VMEM)
SM = pl.BlockSpec(memory_space=pltpu.SMEM)
HBM = pl.BlockSpec(memory_space=pl.ANY)


def nn(a, b):
    return lax.dot_general(a, b, (((1,), (0,)), ((), ())), preferred_element_type=f32)


def tn(a, b):
    return lax.dot_general(a, b, (((0,), (0,)), ((), ())), preferred_element_type=f32)


def nt(a, b):
    return lax.dot_general(a, b, (((1,), (1,)), ((), ())), preferred_element_type=f32)


def params():
    return pltpu.CompilerParams(vmem_limit_bytes=VMEM_LIMIT)


def cost(microseconds):
    return pl.CostEstimate(
        flops=int(microseconds * 1.15e9), bytes_accessed=1 << 20, transcendentals=0
    )


def shape(dims, kind=bf16):
    return jax.ShapeDtypeStruct(dims, kind)


def halves(core, width):
    half = width // 2
    own = pl.ds(pl.multiple_of(core * half, 128), half)
    other = pl.ds(pl.multiple_of((1 - core) * half, 128), half)
    return own, other


def norm(value):
    centred = value - jnp.mean(value, axis=-1, keepdims=True)
    inverse = lax.rsqrt(jnp.mean(centred * centred, axis=-1, keepdims=True) + EPS)
    return centred * inverse, inverse


def norm_gradient(grad, normed, inverse, gain):
    scaled = grad * gain
    return inverse * (
        scaled
        - jnp.mean(scaled, axis=-1, keepdims=True)
        - normed * jnp.mean(scaled * normed, axis=-1, keepdims=True)
    )


def project_kernel(sc, x, w_own, w_other, b_qv, rows, low, qt, kt, vt):
    own, other = halves(sc[2], x.shape[1])
    cols = qt.shape[0]
    normed, _ = norm(x[...].astype(f32))
    low[...] = (normed * rows[0:1, :] + rows[1:2, :]).astype(bf16)
    projected = nn(low[:, own], w_own[...]) + nn(low[:, other], w_other[...])
    qt[...] = ((projected[:, :cols] + b_qv[0:1, :]) * SCALE).T.astype(bf16)
    kt[...] = projected[:, cols : 2 * cols].T.astype(bf16)
    vt[...] = (projected[:, 2 * cols :] + b_qv[1:2, :]).T.astype(bf16)


def project(place, x, w_own, w_other, b_qv, table):
    tok, width = x.shape
    cols = b_qv.shape[1]
    rows = min(256, tok)
    fixed = lambda a: pl.BlockSpec(a.shape, lambda i: (0,) * a.ndim)
    across = pl.BlockSpec((cols, rows), lambda i: (0, i))
    return pl.pallas_call(
        project_kernel,
        grid=(tok // rows,),
        in_specs=[SM, pl.BlockSpec((rows, width), lambda i: (i, 0))]
        + [fixed(a) for a in (w_own, w_other, b_qv, table)],
        out_specs=[pl.BlockSpec((rows, width), lambda i: (i, 0)), across, across, across],
        out_shape=[shape((tok, width))] + [shape((cols, tok))] * 3,
        compiler_params=params(),
        cost_estimate=cost(7),
        name="project",
    )(place, x, w_own, w_other, b_qv, table)


def key_loop(sc, i, step, carry):
    lo, full, diag, end = sc[4 * i + 4], sc[4 * i + 5], sc[4 * i + 6], sc[4 * i + 7]
    carry = lax.fori_loop(lo, full, functools.partial(step, True), carry)
    carry = lax.fori_loop(full, diag, functools.partial(step, False), carry)
    return lax.fori_loop(diag, end, functools.partial(step, True), carry)


def tile_mask(j, bk, bq, start, qpos):
    kpos = j * bk + lax.broadcasted_iota(jnp.int32, (bk, bq), 0)
    return (kpos >= start) & (kpos <= qpos)


def load_keys(sc, kv, held, sems):
    if len(kv) == 1:
        copies = [pltpu.make_async_copy(kv[0], held, sems.at[0])]
    else:
        k, k_x, k_yd, v, v_y, v_xd = kv
        rows = k.shape[0]
        pieces = [(k, 0, 0), (k_x, 0, 1), (k_yd.at[0], 0, 2), (k_yd.at[1], 0, 3)]
        pieces += [(v, 1, 0), (v_y, 1, 2), (v_xd.at[0], 1, 1), (v_xd.at[1], 1, 3)]
        copies = [
            pltpu.make_async_copy(
                piece, held.at[sc[1] ^ run, pl.ds(which * rows, rows), :], sems.at[n]
            )
            for n, (piece, which, run) in enumerate(pieces)
        ]
    for copy in copies:
        copy.start()
    for copy in copies:
        copy.wait()


def attend_kernel(first_head, heads, bk, bq, parts, n_kv, sc, qt, st, *refs):
    kv, refs = refs[:n_kv], refs[n_kv:]
    lse, ot, out, (held, acc, sems) = refs[0], refs[1], refs[2 : 2 + parts], refs[2 + parts :]
    i = pl.program_id(0)
    per = held.shape[2] // bk
    cols = heads * HD
    start = st[...]
    qpos = sc[0] + i * bq + lax.broadcasted_iota(jnp.int32, (1, bq), 1)

    @pl.when(i == 0)
    def _():
        load_keys(sc, kv, held, sems)

    acc[...] = jnp.zeros_like(acc)

    def step(masked, j, carry):
        r = j // per
        off = pl.multiple_of((j % per) * bk, bk)
        new = []
        if masked:
            ok = tile_mask(j, bk, bq, start, qpos)
        for h in range(heads):
            m, l = carry[h]
            hs = slice(h * HD, (h + 1) * HD)
            s = tn(
                held[r, hs, pl.ds(off, bk)],
                qt[(first_head + h) * HD : (first_head + h + 1) * HD, :],
            )
            if masked:
                s = jnp.where(ok, s, NEG)
            m2 = jnp.maximum(m, jnp.max(s, axis=0, keepdims=True))
            p = jnp.exp(s - m2)
            al = jnp.exp(m - m2)
            l = l * al + jnp.sum(p, axis=0, keepdims=True)
            v = held[r, cols + h * HD : cols + (h + 1) * HD, pl.ds(off, bk)]
            acc[hs, :] = acc[hs, :] * al + nn(v, p.astype(bf16))
            new.append((m2, l))
        return tuple(new)

    one = (jnp.full((1, bq), NEG, f32), jnp.zeros((1, bq), f32))
    res = key_loop(sc, i, step, (one,) * heads)
    here = pl.ds(pl.multiple_of(i * bq, bq), bq)
    for h in range(heads):
        m, l = res[h]
        ot[h * HD : (h + 1) * HD, here] = (acc[h * HD : (h + 1) * HD, :] / l).astype(bf16)
        lse[h : h + 1, :] = m + jnp.log(l)

    @pl.when(i == pl.num_programs(0) - 1)
    def _():
        send_parts(sc[3], ot, out)


def send_parts(me, source, out):
    parts, size = len(out), out[0].shape[1]
    for d in range(parts):
        if size % 128 == 0:
            at = pl.multiple_of(lax.rem(me + d, parts) * size, 128)
            out[d][...] = source[:, pl.ds(at, size)].astype(out[d].dtype)
        else:
            for n in range(parts):

                @pl.when(lax.rem(me + d, parts) == n)
                def _():
                    out[d][...] = source[:, n * size : (n + 1) * size].astype(out[d].dtype)


def take_parts(me, rows, parts, target):
    size = parts[0].shape[1]
    for d in range(len(parts)):
        if size % 128 == 0:
            at = pl.multiple_of(lax.rem(me + d, len(parts)) * size, 128)
            target[:, pl.ds(at, size)] = parts[d][rows, :]
        else:
            for n in range(len(parts)):

                @pl.when(lax.rem(me + d, len(parts)) == n)
                def _():
                    target[:, n * size : (n + 1) * size] = parts[d][rows, :]


def attend(scalars, starts, qt, kv, first_head, heads, bk, bq, parts):
    tok = qt.shape[1]
    cols = heads * HD
    runs = kv[0].shape[0] if len(kv) == 1 else 4
    bk, bq = min(bk, tok), min(bq, tok)
    whole = lambda a, b: pl.BlockSpec((a, b), lambda i: (0, 0))
    return pl.pallas_call(
        functools.partial(attend_kernel, first_head, heads, bk, bq, parts, len(kv)),
        grid=(tok // bq,),
        in_specs=[
            SM,
            pl.BlockSpec((qt.shape[0], bq), lambda i: (0, i)),
            pl.BlockSpec((1, bq), lambda i: (0, i)),
        ]
        + [HBM] * len(kv),
        out_specs=[pl.BlockSpec((heads, bq), lambda i: (0, i)), whole(cols, tok)]
        + [whole(cols, tok // parts)] * parts,
        scratch_shapes=[
            pltpu.VMEM((runs, 2 * cols, tok), bf16),
            pltpu.VMEM((cols, bq), f32),
            pltpu.SemaphoreType.DMA((8,)),
        ],
        out_shape=[shape((heads, tok), f32), shape((cols, tok))]
        + [shape((cols, tok // parts))] * parts,
        compiler_params=params(),
        cost_estimate=cost(20),
        name="attend",
    )(scalars(bk, bq), qt, starts, *kv)


def attend_back_kernel(first_head, heads, bk, bq, parts, n_kv, sc, qt, st, lse, ot, *refs):
    do_parts, refs = refs[:parts], refs[parts:]
    kv, refs = refs[:n_kv], refs[n_kv + 1 :]
    n_out = 1 if n_kv == 1 else 4
    dq, dkv, (held, acc, dqa, do_all, sems) = (
        refs[:parts],
        refs[parts : parts + n_out],
        refs[parts + n_out + 1 :],
    )
    i = pl.program_id(0)
    per = held.shape[2] // bk
    cols = heads * HD
    start = st[...]
    qpos = sc[0] + i * bq + lax.broadcasted_iota(jnp.int32, (1, bq), 1)
    here = pl.ds(pl.multiple_of(i * bq, bq), bq)

    @pl.when(i == 0)
    def _():
        acc[...] = jnp.zeros_like(acc)
        dqa[...] = jnp.zeros_like(dqa)
        take_parts(sc[3], slice(first_head * HD, (first_head + heads) * HD), do_parts, do_all)
        load_keys(sc, kv, held, sems)

    delta = [
        jnp.sum(
            do_all[h * HD : (h + 1) * HD, here].astype(f32)
            * ot[h * HD : (h + 1) * HD, :].astype(f32),
            axis=0,
            keepdims=True,
        )
        for h in range(heads)
    ]

    def step(masked, j, carry):
        r = j // per
        off = pl.multiple_of((j % per) * bk, bk)
        if masked:
            ok = tile_mask(j, bk, bq, start, qpos)
        for h in range(heads):
            hs = slice(h * HD, (h + 1) * HD)
            vs = slice(cols + h * HD, cols + (h + 1) * HD)
            k = held[r, hs, pl.ds(off, bk)]
            v = held[r, vs, pl.ds(off, bk)]
            q = qt[(first_head + h) * HD : (first_head + h + 1) * HD, :]
            do = do_all[hs, here]
            s = tn(k, q) - lse[h : h + 1, :]
            if masked:
                s = jnp.where(ok, s, NEG)
            p = jnp.exp(s)
            ds = (p * (tn(v, do) - delta[h])).astype(bf16)
            acc[r, vs, pl.ds(off, bk)] += nt(do, p.astype(bf16))
            acc[r, hs, pl.ds(off, bk)] += nt(q, ds)
            dqa[hs, here] += nn(k, ds)
        return carry

    key_loop(sc, i, step, 0)

    @pl.when(i == pl.num_programs(0) - 1)
    def _():
        dqa[...] = dqa[...] * SCALE
        send_parts(sc[3], dqa, dq)
        if n_out == 1:
            dkv[0][...] = acc[...].astype(bf16)
        else:
            for target, pair, rows in (
                (0, (0, 2), slice(0, cols)),
                (1, (1, 3), slice(0, cols)),
                (2, (0, 1), slice(cols, 2 * cols)),
                (3, (2, 3), slice(cols, 2 * cols)),
            ):
                for n in range(2):
                    dkv[target][n] = acc[sc[1] ^ pair[n], rows, :].astype(bf16)


def attend_back(scalars, starts, qt, lse, ot, do_parts, kv, carried, first_head, heads, bk, bq):
    tok = qt.shape[1]
    cols = heads * HD
    parts = len(do_parts)
    runs = kv[0].shape[0] if len(kv) == 1 else 4
    bk, bq = min(bk, tok), min(bq, tok)
    whole = lambda *dims: pl.BlockSpec(dims, lambda i: (0,) * len(dims))
    out_kv = [(runs, 2 * cols, tok)] if len(kv) == 1 else [(2, cols, tok)] * 4
    return pl.pallas_call(
        functools.partial(attend_back_kernel, first_head, heads, bk, bq, parts, len(kv)),
        grid=(tok // bq,),
        in_specs=[
            SM,
            pl.BlockSpec((qt.shape[0], bq), lambda i: (0, i)),
            pl.BlockSpec((1, bq), lambda i: (0, i)),
            pl.BlockSpec((heads, bq), lambda i: (0, i)),
            pl.BlockSpec((cols, bq), lambda i: (0, i)),
        ]
        + [whole(*d.shape) for d in do_parts]
        + [HBM] * (len(kv) + 1),
        out_specs=[whole(cols, tok // parts)] * parts + [whole(*d) for d in out_kv] + [HBM],
        scratch_shapes=[
            pltpu.VMEM((runs, 2 * cols, tok), bf16),
            pltpu.VMEM((runs, 2 * cols, tok), f32),
            pltpu.VMEM((cols, tok), f32),
            pltpu.VMEM((cols, tok), bf16),
            pltpu.SemaphoreType.DMA((8,)),
        ],
        out_shape=[shape((cols, tok // parts))] * parts
        + [shape(d) for d in out_kv]
        + [shape(carried.shape)],
        input_output_aliases={5 + parts + len(kv): parts + len(out_kv)},
        compiler_params=params(),
        cost_estimate=cost(26),
        name="attend_back",
    )(scalars(bk, bq), qt, starts, lse, ot, *do_parts, *kv, carried)


ROOT = 0.7978845608028654


def middle_kernel(n_att, parts, sc, *refs):
    att, refs = refs[:n_att], refs[n_att:]
    x, cot, of_own, of_other, dn_own, dn_other, rows = refs[:7]
    refs = refs[7:]
    outputs, grad_mid, sums, fc_sums = refs[:4]
    d_att, (g_own, g_other) = refs[4 : 4 + parts], refs[4 + parts : 6 + parts]
    mid, att_t, low, low_t, cot_t, mlp, back = refs[6 + parts :]
    d = pl.program_id(0)
    width = x.shape[1]
    own, other = halves(sc[2], width)
    half = width // 2
    ffw = dn_own.shape[1]
    count = ffw // half
    cols = att_t.shape[0] // parts
    b_out, b_down, gain, shift = (rows[n : n + 1, :] for n in range(2, 6))

    @pl.when(d == 0)
    def _():
        group = n_att // parts
        row = 0
        for part in range(parts):
            for g in range(group):
                piece = att[part * group + g]
                att_t[row : row + piece.shape[0], :] = piece[...]
                row += piece.shape[0]
        att_low = att_t[...].T
        mine = theirs = 0.0
        for part in range(parts):
            piece = att_low[:, part * cols : (part + 1) * cols]
            mine += nn(piece, of_own[part, :cols, :])
            theirs += nn(piece, of_other[part, :cols, :])
        mid[:, own] = mine
        mid[:, other] = theirs
        mid[...] = x[...].astype(f32) + mid[...] + b_out
        normed, _ = norm(mid[...])
        low[...] = (normed * gain + shift).astype(bf16)
        low_t[...] = low[...].T
        cot_t[...] = cot[...].T
        mlp[...] = jnp.zeros_like(mlp)
        back[...] = jnp.zeros_like(back)

    own_rows = pl.ds(pl.multiple_of(sc[2] * half, half), half)
    other_rows = pl.ds(pl.multiple_of((1 - sc[2]) * half, half), half)
    terms = of_own[d, cols : cols + 16, :].astype(f32)
    pieces = [slice(cols + 16 + n * half, cols + 16 + (n + 1) * half) for n in range(count)]
    u = [
        nn(low[:, own], of_own[d, at, :])
        + nn(low[:, other], of_other[d, at, :])
        + sum(terms[t * count + n : t * count + n + 1, :] for t in range(3))
        for n, at in enumerate(pieces)
    ]
    u = jnp.concatenate(u, axis=1)
    t = jnp.tanh(ROOT * (u + 0.044715 * (u * u * u)))
    act = (0.5 * u * (1.0 + t)).astype(bf16)
    slope = 0.5 * (1.0 + t) + (0.5 * ROOT) * u * (1.0 - t * t) * (1.0 + 0.134145 * (u * u))
    d_act = nt(cot[:, own], dn_own[0]) + nt(cot[:, other], dn_other[0])
    dh = (d_act * slope).astype(bf16)
    mlp[:, own] += nn(act, dn_own[0])
    mlp[:, other] += nn(act, dn_other[0])
    for n, at in enumerate(pieces):
        dh_n = dh[:, n * half : (n + 1) * half]
        back[:, own] += nt(dh_n, of_own[d, at, :])
        back[:, other] += nt(dh_n, of_other[d, at, :])
    g_own[d, :, :ffw] = nn(low_t[own_rows, :], dh).astype(bf16)
    g_other[d, :, :ffw] = nn(low_t[other_rows, :], dh).astype(bf16)
    g_own[d, :, ffw : 2 * ffw] = nn(cot_t[own_rows, :], act).astype(bf16)
    g_other[d, :, ffw : 2 * ffw] = nn(cot_t[other_rows, :], act).astype(bf16)
    fc_sums[lax.rem(sc[3] - d + parts, parts)] = jnp.sum(dh.astype(f32), axis=0, keepdims=True)

    @pl.when(d == parts - 1)
    def _():
        normed, inverse = norm(mid[...])
        outputs[...] = (mid[...] + mlp[...] + b_down).astype(bf16)
        upper = cot[...].astype(f32)
        grad = back[...]
        down = upper + norm_gradient(grad, normed, inverse, gain)
        grad_mid[...] = down
        sums[0:1, :] = jnp.sum(down, axis=0, keepdims=True)
        sums[1:2, :] = jnp.sum(upper, axis=0, keepdims=True)
        sums[2:3, :] = jnp.sum(grad * normed, axis=0, keepdims=True)
        sums[3:4, :] = jnp.sum(grad, axis=0, keepdims=True)
        low[...] = down.astype(bf16)
        low_t[...] = low[...].T
        g_own[:, :, 2 * ffw + cols :] = jnp.zeros_like(g_own[:, :, 2 * ffw + cols :])
        g_other[:, :, 2 * ffw + cols :] = jnp.zeros_like(g_other[:, :, 2 * ffw + cols :])
        for part in range(parts):
            at = slice(part * cols, (part + 1) * cols)
            g_own[part, :, 2 * ffw : 2 * ffw + cols] = nt(low_t[own_rows, :], att_t[at, :]).astype(bf16)
            g_other[part, :, 2 * ffw : 2 * ffw + cols] = nt(low_t[other_rows, :], att_t[at, :]).astype(bf16)
            d_att[part][...] = (
                nt(of_own[part, :cols, :], low[:, own]) + nt(of_other[part, :cols, :], low[:, other])
            ).astype(bf16)


def middle(place, att, x, cot, of, dn, cols, table):
    parts, ffw, half = dn[0].shape
    sub, width = x.shape
    whole = lambda *dims: pl.BlockSpec(
        dims, lambda i, sc: (0,) * len(dims), pipeline_mode=pl.Buffered(1)
    )
    placed = pl.BlockSpec(
        (1, ffw, half), lambda i, sc: (i, 0, 0)
    )
    once = lambda a: whole(*a.shape)
    grads = (parts, half, 128 * ((2 * ffw + cols + 127) // 128))
    return pl.pallas_call(
        functools.partial(middle_kernel, len(att), parts),
        grid_spec=pltpu.PrefetchScalarGridSpec(
            num_scalar_prefetch=1,
            grid=(parts,),
            in_specs=[once(a) for a in att]
            + [once(x), once(cot), once(of[0]), once(of[1]), placed, placed, once(table)],
            out_specs=[whole(sub, width), whole(sub, width), whole(4, width), whole(parts, 1, ffw)]
            + [whole(cols, sub)] * parts
            + [whole(*grads)] * 2,
            scratch_shapes=[
                pltpu.VMEM((sub, width), f32),
                pltpu.VMEM((parts * cols, sub), bf16),
                pltpu.VMEM((sub, width), bf16),
                pltpu.VMEM((width, sub), bf16),
                pltpu.VMEM((width, sub), bf16),
                pltpu.VMEM((sub, width), f32),
                pltpu.VMEM((sub, width), f32),
            ],
        ),
        out_shape=[
            shape((sub, width)),
            shape((sub, width), f32),
            shape((4, width), f32),
            shape((parts, 1, ffw), f32),
        ]
        + [shape((cols, sub))] * parts
        + [shape(grads)] * 2,
        compiler_params=params(),
        cost_estimate=cost(19),
        name="middle",
    )(place, *att, x, cot, of[0], of[1], dn[0], dn[1], table)


def last_kernel(parts, pieces, sc, *refs):
    grads, refs = refs[: parts * pieces], refs[parts * pieces :]
    w_own, w_other, x, grad_mid, rows, mid_sums, fc_sums, out, sums, back_t, stacked = refs
    half = w_own.shape[1]
    wide = w_own.shape[2]
    own_rows = pl.ds(pl.multiple_of(sc[2] * half, half), half)
    other_rows = pl.ds(pl.multiple_of((1 - sc[2]) * half, half), half)
    ones = jnp.ones((8, x.shape[0]), bf16)
    sums[...] = jnp.zeros_like(sums)
    stacked[...] = jnp.zeros_like(stacked)
    for part in range(parts):
        row = 0
        for n in range(pieces):
            piece = grads[part * pieces + n]
            stacked[row : row + piece.shape[0], :] = piece[...]
            row += piece.shape[0]
        at = lax.rem(sc[3] - part + parts, parts)
        mine, theirs = nn(w_own[at], stacked[...]), nn(w_other[at], stacked[...])
        if part == 0:
            back_t[own_rows, :], back_t[other_rows, :] = mine, theirs
        else:
            back_t[own_rows, :] += mine
            back_t[other_rows, :] += theirs
        sums[pl.ds(6 + parts + at, 1), :wide] = nt(ones, stacked[...])[0:1, :]
    back = back_t[...].T
    normed, inverse = norm(x[...].astype(f32))
    out[...] = (grad_mid[...] + norm_gradient(back, normed, inverse, rows[0:1, :])).astype(bf16)
    sums[0:4, :] = mid_sums[...]
    sums[4:5, :] = jnp.sum(back * normed, axis=0, keepdims=True)
    sums[5:6, :] = jnp.sum(back, axis=0, keepdims=True)
    for part in range(parts):
        sums[6 + part : 7 + part, :] = fc_sums[part]


def last(place, grads, pieces, w, x, grad_mid, table, mid_sums, fc_sums):
    parts = w[0].shape[0]
    sub, width = x.shape
    rows = 8 * ((6 + 2 * parts + 7) // 8)
    return pl.pallas_call(
        functools.partial(last_kernel, parts, pieces),
        in_specs=[SM] + [VM] * (len(grads) + 7),
        out_specs=[VM, VM],
        out_shape=[shape((sub, width)), shape((rows, width), f32)],
        scratch_shapes=[pltpu.VMEM((width, sub), f32), pltpu.VMEM((w[0].shape[2], sub), bf16)],
        compiler_params=params(),
        cost_estimate=cost(6),
        name="last",
    )(place, *grads, w[0], w[1], x, grad_mid, table, mid_sums, fc_sums)


def fold_kernel(cut, sc, mine, theirs, lo_send, lo_keep, hi_send, hi_keep):
    i = pl.program_id(0)
    total = (mine[...].astype(f32) + theirs[...].astype(f32)).astype(bf16)
    lo, hi = total[None, :, :, :cut], total[None, :, :, cut:]

    @pl.when(i < 2)
    def _():
        lo_send[...] = lo

    @pl.when(i >= 2)
    def _():
        lo_keep[...] = lo

    @pl.when((i == 1) | (i == 2))
    def _():
        hi_send[...] = hi

    @pl.when((i == 0) | (i == 3))
    def _():
        hi_keep[...] = hi


def fold(place, mine, theirs):
    parts, rows, wide = mine.shape
    size = rows // 4
    cut = (wide // 256) * 128 if wide % 256 == 0 else (wide // 256 + 1) * 128
    block = pl.BlockSpec(
        (parts, size, wide),
        lambda i, sc: (
            0,
            sc[1] ^ jnp.where(i == 0, 1, jnp.where(i == 1, 3, jnp.where(i == 2, 2, 0))),
            0,
        ),
    )
    out = lambda width, index: pl.BlockSpec(
        (1, parts, size, width), lambda i, sc: (index(i), 0, 0, 0)
    )
    lo, hi = cut, wide - cut
    return pl.pallas_call(
        functools.partial(fold_kernel, cut),
        grid_spec=pltpu.PrefetchScalarGridSpec(
            num_scalar_prefetch=1,
            grid=(4,),
            in_specs=[block, block],
            out_specs=[
                out(lo, lambda i: jnp.minimum(i, 1)),
                out(lo, lambda i: jnp.where(i == 3, 0, 1)),
                out(hi, lambda i: jnp.where(i < 2, 1, 0)),
                out(hi, lambda i: jnp.where(i == 3, 0, 1)),
            ],
        ),
        out_shape=[
            shape((2, parts, size, lo)),
            shape((2, parts, size, lo)),
            shape((2, parts, size, hi)),
            shape((2, parts, size, hi)),
        ],
        compiler_params=params(),
        cost_estimate=cost(1 + 6 * parts / 4),
        name="fold",
    )(place, mine, theirs)


def body(
    n_shard,
    n_context,
    n_tensor,
    inputs,
    segments,
    w_qkv,
    w_out,
    w_fc,
    w_down,
    b_qv,
    b_out,
    b_fc,
    b_down,
    first_norm_gain,
    first_norm_bias,
    second_norm_gain,
    second_norm_bias,
    cotangent,
):
    _, tok, width = inputs.shape
    length = segments.shape[1]
    half, _, cols = w_qkv.shape
    heads = cols // HD
    ffw = w_fc.shape[1]
    sub = tok // n_tensor
    context = lax.axis_index("context")
    tensor = lax.axis_index("tensor")
    core = lax.axis_index("shard")
    first = context * tok
    place = jnp.stack([first, context, core, tensor]).astype(jnp.int32)
    grouped = n_context == 4
    x = inputs[0]
    cot = cotangent[0]
    row = lambda v: v[None, :]
    zero = jnp.zeros_like(b_out)
    table = jnp.concatenate(
        [
            first_norm_gain,
            first_norm_bias,
            b_out,
            b_down,
            second_norm_gain,
            second_norm_bias,
            zero,
            zero,
        ]
    ).reshape(8, width)
    after = lambda v, dep: lax.optimization_barrier((v, dep))[0]

    swap = lambda v: lax.ppermute(v, "shard", [(0, 1), (1, 0)])
    along_x = lambda v: lax.ppermute(v, "context", [(0, 1), (1, 0), (2, 3), (3, 2)])
    along_y = lambda v: lax.ppermute(v, "context", [(0, 2), (2, 0), (1, 3), (3, 1)])
    shift_by = lambda v, d: lax.ppermute(
        v, "tensor", [(s, (s + d) % n_tensor) for s in range(n_tensor)]
    )

    def gather_direct(v):
        return [v] + [shift_by(v, d) for d in range(1, n_tensor)]

    def gather_begin(v):
        if n_tensor != 4:
            return tuple(gather_direct(v))
        move = lambda perm: lax.ppermute(v, "tensor", perm)
        return (
            v,
            move([(0, 2), (1, 3), (2, 0), (3, 1)]),
            move([(0, 1), (1, 2), (2, 3)]),
            move([(3, 2), (2, 1), (1, 0)]),
        )

    def gather_end(state, hold=()):
        if n_tensor != 4:
            return list(state)
        v, two, right, left = state
        two = after(two, hold)
        far = lax.ppermute(two, "tensor", [(2, 3), (1, 0)])
        return [
            v,
            jnp.where(tensor == 0, far, right),
            two,
            jnp.where(tensor == 3, far, left),
        ]

    def scatter_line(pieces):
        if n_tensor != 4:
            total = pieces[0].astype(f32)
            for d in range(1, n_tensor):
                total += shift_by(pieces[d].astype(bf16), -d).astype(f32)
            return total
        move = lambda a, perm: lax.ppermute(a.astype(bf16), "tensor", perm)
        far = move(jnp.where(tensor == 0, pieces[1], pieces[3]), [(0, 1), (3, 2)])
        right = move(pieces[3], [(0, 1), (1, 2), (2, 3)])
        left = move(pieces[1], [(3, 2), (2, 1), (1, 0)])
        two = move(
            pieces[2].astype(f32) + far.astype(f32), [(0, 2), (1, 3), (2, 0), (3, 1)]
        )
        return (
            pieces[0].astype(f32) + right.astype(f32) + left.astype(f32) + two.astype(f32)
        )

    def scatter_begin(mine, theirs):
        theirs = swap(theirs)
        if not grouped:
            both = (mine.astype(f32) + theirs.astype(f32)).astype(bf16)
            return lax.psum_scatter(both, "context", scatter_dimension=1, tiled=True)
        return fold(place, mine, theirs)

    def scatter_first(state):
        if not grouped:
            return state
        lo_send, lo_keep, hi_send, hi_keep = state
        r, s = along_x(lo_send).astype(f32), along_y(hi_send).astype(f32)
        return (
            lo_keep[0].astype(f32) + r[0],
            hi_keep[0].astype(f32) + s[0],
            (lo_keep[1].astype(f32) + r[1]).astype(bf16),
            (hi_keep[1].astype(f32) + s[1]).astype(bf16),
        )

    def scatter_second(state):
        if not grouped:
            return state
        lo, hi, lo_send, hi_send = state
        lo += along_y(lo_send).astype(f32)
        hi += along_x(hi_send).astype(f32)
        return jnp.concatenate([lo, hi], axis=2)

    bounds = [jnp.sum((segments[0] < d).astype(jnp.int32)) for d in range(1, 5)]
    seg = lax.dynamic_slice_in_dim(segments[0], first, tok, 0)
    starts = jnp.zeros_like(seg)
    for d in range(1, 5):
        starts = jnp.where(seg == d, bounds[d - 1], starts)

    def scalars(bk, bq):
        count = tok // bq
        begin = starts.reshape(count, bq)
        base = first + jnp.arange(count, dtype=jnp.int32) * bq
        lo = begin[:, 0] // bk
        diag = base // bk
        end = (base + bq + bk - 1) // bk
        full = jnp.minimum(jnp.maximum((begin[:, -1] + bk - 1) // bk, lo), diag)
        table = jnp.stack([lo, full, diag, end], axis=1).reshape(-1)
        return jnp.concatenate([place, table.astype(jnp.int32)])

    qkv_own = w_qkv.reshape(half, 3 * cols)
    low_one, qt, kt, vt = project(
        place,
        x,
        qkv_own,
        swap(qkv_own),
        b_qv,
        table,
    )

    terms, rest = [], b_fc
    for _ in range(3):
        term = lax.reduce_precision(rest, 8, 7)
        terms.append(term.astype(bf16).reshape(ffw // half, half))
        rest = rest - term
    terms = jnp.concatenate(terms, axis=0)
    terms = jnp.pad(terms, ((0, 16 - terms.shape[0]), (0, 0)))
    packed = jnp.concatenate([w_out, terms, w_fc[:, :half], w_fc[:, half:]], axis=0)
    packed = gather_begin(packed)
    kv = []
    hold = ()
    head = 0
    for g in GROUPS:
        rows = slice(head * HD, (head + g) * HD)
        head += g
        k, v = kt[rows], vt[rows]
        if grouped:
            kx, vy = along_x(k), along_y(v)
            k_two, v_two = jnp.stack([k, kx]), jnp.stack([v, vy])
            k_two, v_two = after((k_two, v_two), packed[1:])
            k_yd, v_xd = along_y(k_two), along_x(v_two)
            hold = (k_two, v_two)
            kv.append([k, kx, k_yd, v, vy, v_xd])
        else:
            kv.append([lax.all_gather(jnp.concatenate([k, v], axis=0), "context", axis=0)])

    dn = gather_begin(after(w_down, packed[1]))
    saved = []
    att = [[] for _ in range(n_tensor)]
    head = 0
    for g, held in zip(GROUPS, kv):
        results = attend(scalars, row(starts), after(qt, packed[1:]), held, head, g, BK_F, BQ_F, n_tensor)
        lse, ot, *out = after(results, dn[1:])
        saved.append((lse, ot))
        att[0].append(out[0])
        for d in range(1, n_tensor):
            att[d].append(shift_by(out[d], d))
        head += g

    of = jnp.stack(after(gather_end(packed, hold), saved[-1][0]))
    of = (of, swap(of))
    dn = jnp.stack(gather_end(dn, saved[-1][0]))
    dn = (dn, swap(dn))
    x_sub = lax.dynamic_slice_in_dim(x, tensor * sub, sub, 0)
    cot_sub = lax.dynamic_slice_in_dim(cot, tensor * sub, sub, 0)
    outputs_sub, grad_mid, mid_sums, fc_sums, *rest = middle(
        place,
        [piece for part in att for piece in part],
        x_sub,
        cot_sub,
        of,
        dn,
        cols,
        table,
    )
    d_att, (g_own, g_other) = rest[:n_tensor], rest[n_tensor:]
    do_parts = [d_att[0]] + [
        shift_by(d_att[d], -d) for d in range(1, n_tensor)
    ]

    def spread(pieces):
        whole = jnp.zeros((tok, width), f32)
        for d in range(n_tensor):
            at = lax.rem(tensor - d + n_tensor, n_tensor) * sub
            whole = lax.dynamic_update_slice_in_dim(whole, pieces[d].astype(f32), at, 0)
        return whole[None]

    folded = scatter_begin(g_own, g_other)
    hop_one = folded[0] if grouped else folded
    carried = jnp.pad(qkv_own, ((0, 0), (0, -3 * cols % 128)))
    folded = scatter_begin(g_own, g_other)
    hop_one = folded[0] if grouped else folded
    qkv_wide = jnp.pad(qkv_own, ((0, 0), (0, width - 3 * cols)))
    outputs_and_qkv = lax.all_gather(
        jnp.concatenate([outputs_sub, qkv_wide], axis=0), "tensor", axis=0
    )
    outputs = gather_direct(after(outputs_sub, do_parts))
    wide = scatter_first(folded)
    wide_sends = wide[2:]
    wide = scatter_second(wide)

    dq_pieces, dkv_pieces, dqkv = [], [], []
    head = 0
    queries, keys, values = [], [], []
    sent = [[] for _ in range(n_tensor)]
    for g, held, (lse, ot) in zip(GROUPS, kv, saved):
        out = attend_back(
            scalars, row(starts), after(qt, hop_one), lse, ot, do_parts, held, carried, head, g, BK_B, BQ_B
        )
        back_done = out[-1]
        *out, carried = out
        dq, dkv = after(out[:n_tensor], (wide_sends, outputs[1:])), out[n_tensor:]
        if grouped:
            dk_keep, dk_send, dv_keep, dv_send = dkv
            dk_send, dv_send = after((dk_send, dv_send), (wide_sends, outputs[1:]))
            r = along_x(dk_send).astype(f32)
            s = along_y(dv_send).astype(f32)
            r2 = along_y((dk_keep[1].astype(f32) + r[1]).astype(bf16)).astype(f32)
            s2 = along_x((dv_keep[1].astype(f32) + s[1]).astype(bf16)).astype(f32)
            dk = (dk_keep[0].astype(f32) + r[0] + r2).astype(bf16)
            dv = (dv_keep[0].astype(f32) + s[0] + s2).astype(bf16)
        else:
            both = lax.psum_scatter(dkv[0], "context", scatter_dimension=0, tiled=True)[0]
            dk, dv = both[: g * HD], both[g * HD :]
        queries.append(dq)
        keys.append(dk)
        values.append(dv)
        head += g

    wide_grads = scatter_line([wide[d] for d in range(n_tensor)])

    def part_of(v, d):
        at = lax.rem(tensor + d, n_tensor) * sub
        return lax.dynamic_slice_in_dim(v, at, sub, 1)

    grads = []
    both = jnp.concatenate(keys + values, axis=0)
    for d in range(n_tensor):
        piece = jnp.concatenate([q[d] for q in queries] + [part_of(both, d)], axis=0)
        grads.append(shift_by(piece, d) if d else piece)
    pieces = 1

    dq_whole = []
    for q in queries:
        whole = jnp.zeros((q[0].shape[0], tok), bf16)
        for d in range(n_tensor):
            at = lax.rem(tensor + d, n_tensor) * sub
            whole = lax.dynamic_update_slice_in_dim(whole, q[d], at, 1)
        dq_whole.append(whole)
    qkv = lax.all_gather(carried, "tensor", axis=0)
    qkv = (qkv, swap(qkv))
    stacked = jnp.concatenate(
        dq_whole + [both, jnp.zeros((-3 * cols % 128, tok), bf16)], axis=0
    )
    qkv_grad = jnp.einsum(
        "td,ct->dc", low_one, stacked, preferred_element_type=f32
    ).astype(bf16)
    qkv_mine = lax.dynamic_slice_in_dim(qkv_grad, core * half, half, 0)
    qkv_theirs = lax.dynamic_slice_in_dim(qkv_grad, (1 - core) * half, half, 0)
    qkv_folded = scatter_begin(qkv_mine[None], qkv_theirs[None])

    input_sub, small = last(
        place, grads, pieces, qkv, x_sub, after(grad_mid, qkv_folded), table, mid_sums, fc_sums
    )
    input_gradient = spread(gather_direct(input_sub))
    outputs = spread(outputs)
    qkv_grads = scatter_second(scatter_first(qkv_folded))[0]

    if grouped and n_tensor == 4 and n_shard == 2:
        small += swap(small)
        small += along_x(small)
        small += along_y(small)
        small += lax.ppermute(small, "tensor", [(0, 1), (1, 0), (2, 3), (3, 2)])
        small += lax.ppermute(small, "tensor", [(0, 2), (2, 0), (1, 3), (3, 1)])
    else:
        small = lax.psum(small, ("shard", "context", "tensor"))
    fc_total = lax.dynamic_index_in_dim(small, 6 + tensor, 0, keepdims=False)
    qv_total = lax.dynamic_index_in_dim(small, 6 + n_tensor + tensor, 0, keepdims=False)
    qv_total = jnp.stack([qv_total[:cols], qv_total[2 * cols : 3 * cols]])
    return (
        outputs,
        input_gradient,
        qkv_grads[:, : 3 * cols].astype(f32).reshape(-1, 3, cols),
        wide_grads[:, 2 * ffw : 2 * ffw + cols].T,
        wide_grads[:, :ffw],
        wide_grads[:, ffw : 2 * ffw].T,
        qv_total,
        small[0],
        fc_total,
        small[1],
        small[4],
        small[5],
        small[2],
        small[3],
    )


def solution(mesh):
    sizes = dict(mesh.shape)
    placed = (
        P("shard", "context", None),
        P("shard", None),
        P("shard", None, "tensor"),
        P("tensor", "shard"),
        P("shard", "tensor"),
        P("tensor", "shard"),
        P(None, "tensor"),
        P(),
        P("tensor"),
        P(),
        P(),
        P(),
        P(),
        P(),
        P("shard", "context", None),
    )
    return jax.shard_map(
        functools.partial(body, sizes["shard"], sizes["context"], sizes["tensor"]),
        mesh=mesh,
        in_specs=placed,
        out_specs=(
            P("shard", "context", None),
            P("shard", "context", None),
            P(("shard", "context"), None, "tensor"),
            P("tensor", ("shard", "context")),
            P(("shard", "context"), "tensor"),
            P("tensor", ("shard", "context")),
            P(None, "tensor"),
            P(),
            P("tensor"),
            P(),
            P(),
            P(),
            P(),
            P(),
        ),
        check_vma=False,
    )
```

```python
import functools

import jax
import jax.numpy as jnp
from jax import lax
from jax.experimental import pallas as pl
from jax.experimental.pallas import tpu as pltpu
from jax.sharding import PartitionSpec as P

HD = 64
EPS = 1e-05
NEG = -1e30
SCALE = float(HD) ** -0.5
VMEM_LIMIT = 56 * 1024 * 1024
GROUPS = (3,)
BK_F, BQ_F = 512, 512
BK_B, BQ_B = 512, 512
f32 = jnp.float32
bf16 = jnp.bfloat16
VM = pl.BlockSpec(memory_space=pltpu.VMEM)
SM = pl.BlockSpec(memory_space=pltpu.SMEM)
HBM = pl.BlockSpec(memory_space=pl.ANY)


def nn(a, b):
    return lax.dot_general(a, b, (((1,), (0,)), ((), ())), preferred_element_type=f32)


def tn(a, b):
    return lax.dot_general(a, b, (((0,), (0,)), ((), ())), preferred_element_type=f32)


def nt(a, b):
    return lax.dot_general(a, b, (((1,), (1,)), ((), ())), preferred_element_type=f32)


def params():
    return pltpu.CompilerParams(vmem_limit_bytes=VMEM_LIMIT)


def cost(microseconds):
    return pl.CostEstimate(
        flops=int(microseconds * 1.15e9), bytes_accessed=1 << 20, transcendentals=0
    )


def shape(dims, kind=bf16):
    return jax.ShapeDtypeStruct(dims, kind)


def halves(core, width):
    half = width // 2
    own = pl.ds(pl.multiple_of(core * half, 128), half)
    other = pl.ds(pl.multiple_of((1 - core) * half, 128), half)
    return own, other


def norm(value):
    centred = value - jnp.mean(value, axis=-1, keepdims=True)
    inverse = lax.rsqrt(jnp.mean(centred * centred, axis=-1, keepdims=True) + EPS)
    return centred * inverse, inverse


def norm_gradient(grad, normed, inverse, gain):
    scaled = grad * gain
    return inverse * (
        scaled
        - jnp.mean(scaled, axis=-1, keepdims=True)
        - normed * jnp.mean(scaled * normed, axis=-1, keepdims=True)
    )


def project_kernel(sc, x, w_own, w_other, b_qv, rows, low, qt, kt, vt):
    own, other = halves(sc[2], x.shape[1])
    cols = qt.shape[0]
    normed, _ = norm(x[...].astype(f32))
    low[...] = (normed * rows[0:1, :] + rows[1:2, :]).astype(bf16)
    projected = nn(low[:, own], w_own[...]) + nn(low[:, other], w_other[...])
    qt[...] = ((projected[:, :cols] + b_qv[0:1, :]) * SCALE).T.astype(bf16)
    kt[...] = projected[:, cols : 2 * cols].T.astype(bf16)
    vt[...] = (projected[:, 2 * cols :] + b_qv[1:2, :]).T.astype(bf16)


def project(place, x, w_own, w_other, b_qv, table):
    tok, width = x.shape
    cols = b_qv.shape[1]
    rows = min(256, tok)
    fixed = lambda a: pl.BlockSpec(a.shape, lambda i: (0,) * a.ndim)
    across = pl.BlockSpec((cols, rows), lambda i: (0, i))
    return pl.pallas_call(
        project_kernel,
        grid=(tok // rows,),
        in_specs=[SM, pl.BlockSpec((rows, width), lambda i: (i, 0))]
        + [fixed(a) for a in (w_own, w_other, b_qv, table)],
        out_specs=[pl.BlockSpec((rows, width), lambda i: (i, 0)), across, across, across],
        out_shape=[shape((tok, width))] + [shape((cols, tok))] * 3,
        compiler_params=params(),
        cost_estimate=cost(7),
        name="project",
    )(place, x, w_own, w_other, b_qv, table)


def key_loop(sc, i, step, carry):
    lo, full, diag, end = sc[4 * i + 4], sc[4 * i + 5], sc[4 * i + 6], sc[4 * i + 7]
    carry = lax.fori_loop(lo, full, functools.partial(step, True), carry)
    carry = lax.fori_loop(full, diag, functools.partial(step, False), carry)
    return lax.fori_loop(diag, end, functools.partial(step, True), carry)


def tile_mask(j, bk, bq, start, qpos):
    kpos = j * bk + lax.broadcasted_iota(jnp.int32, (bk, bq), 0)
    return (kpos >= start) & (kpos <= qpos)


def load_keys(sc, kv, held, sems):
    if len(kv) == 1:
        copies = [pltpu.make_async_copy(kv[0], held, sems.at[0])]
    else:
        k, k_x, k_yd, v, v_y, v_xd = kv
        rows = k.shape[0]
        pieces = [(k, 0, 0), (k_x, 0, 1), (k_yd.at[0], 0, 2), (k_yd.at[1], 0, 3)]
        pieces += [(v, 1, 0), (v_y, 1, 2), (v_xd.at[0], 1, 1), (v_xd.at[1], 1, 3)]
        copies = [
            pltpu.make_async_copy(
                piece, held.at[sc[1] ^ run, pl.ds(which * rows, rows), :], sems.at[n]
            )
            for n, (piece, which, run) in enumerate(pieces)
        ]
    for copy in copies:
        copy.start()
    for copy in copies:
        copy.wait()


def attend_kernel(first_head, heads, bk, bq, parts, n_kv, sc, qt, st, *refs):
    kv, refs = refs[:n_kv], refs[n_kv:]
    lse, ot, out, (held, acc, sems) = refs[0], refs[1], refs[2 : 2 + parts], refs[2 + parts :]
    i = pl.program_id(0)
    per = held.shape[2] // bk
    cols = heads * HD
    start = st[...]
    qpos = sc[0] + i * bq + lax.broadcasted_iota(jnp.int32, (1, bq), 1)

    @pl.when(i == 0)
    def _():
        load_keys(sc, kv, held, sems)

    acc[...] = jnp.zeros_like(acc)

    def step(masked, j, carry):
        r = j // per
        off = pl.multiple_of((j % per) * bk, bk)
        new = []
        if masked:
            ok = tile_mask(j, bk, bq, start, qpos)
        for h in range(heads):
            m, l = carry[h]
            hs = slice(h * HD, (h + 1) * HD)
            s = tn(
                held[r, hs, pl.ds(off, bk)],
                qt[(first_head + h) * HD : (first_head + h + 1) * HD, :],
            )
            if masked:
                s = jnp.where(ok, s, NEG)
            m2 = jnp.maximum(m, jnp.max(s, axis=0, keepdims=True))
            p = jnp.exp(s - m2)
            al = jnp.exp(m - m2)
            l = l * al + jnp.sum(p, axis=0, keepdims=True)
            v = held[r, cols + h * HD : cols + (h + 1) * HD, pl.ds(off, bk)]
            acc[hs, :] = acc[hs, :] * al + nn(v, p.astype(bf16))
            new.append((m2, l))
        return tuple(new)

    one = (jnp.full((1, bq), NEG, f32), jnp.zeros((1, bq), f32))
    res = key_loop(sc, i, step, (one,) * heads)
    here = pl.ds(pl.multiple_of(i * bq, bq), bq)
    for h in range(heads):
        m, l = res[h]
        ot[h * HD : (h + 1) * HD, here] = (acc[h * HD : (h + 1) * HD, :] / l).astype(bf16)
        lse[h : h + 1, :] = m + jnp.log(l)

    @pl.when(i == pl.num_programs(0) - 1)
    def _():
        send_parts(sc[3], ot, out)


def send_parts(me, source, out):
    parts, size = len(out), out[0].shape[1]
    for d in range(parts):
        if size % 128 == 0:
            at = pl.multiple_of(lax.rem(me + d, parts) * size, 128)
            out[d][...] = source[:, pl.ds(at, size)].astype(out[d].dtype)
        else:
            for n in range(parts):

                @pl.when(lax.rem(me + d, parts) == n)
                def _():
                    out[d][...] = source[:, n * size : (n + 1) * size].astype(out[d].dtype)


def take_parts(me, rows, parts, target):
    size = parts[0].shape[1]
    for d in range(len(parts)):
        if size % 128 == 0:
            at = pl.multiple_of(lax.rem(me + d, len(parts)) * size, 128)
            target[:, pl.ds(at, size)] = parts[d][rows, :]
        else:
            for n in range(len(parts)):

                @pl.when(lax.rem(me + d, len(parts)) == n)
                def _():
                    target[:, n * size : (n + 1) * size] = parts[d][rows, :]


def attend(scalars, starts, qt, kv, first_head, heads, bk, bq, parts):
    tok = qt.shape[1]
    cols = heads * HD
    runs = kv[0].shape[0] if len(kv) == 1 else 4
    bk, bq = min(bk, tok), min(bq, tok)
    whole = lambda a, b: pl.BlockSpec((a, b), lambda i: (0, 0))
    return pl.pallas_call(
        functools.partial(attend_kernel, first_head, heads, bk, bq, parts, len(kv)),
        grid=(tok // bq,),
        in_specs=[
            SM,
            pl.BlockSpec((qt.shape[0], bq), lambda i: (0, i)),
            pl.BlockSpec((1, bq), lambda i: (0, i)),
        ]
        + [HBM] * len(kv),
        out_specs=[pl.BlockSpec((heads, bq), lambda i: (0, i)), whole(cols, tok)]
        + [whole(cols, tok // parts)] * parts,
        scratch_shapes=[
            pltpu.VMEM((runs, 2 * cols, tok), bf16),
            pltpu.VMEM((cols, bq), f32),
            pltpu.SemaphoreType.DMA((8,)),
        ],
        out_shape=[shape((heads, tok), f32), shape((cols, tok))]
        + [shape((cols, tok // parts))] * parts,
        compiler_params=params(),
        cost_estimate=cost(20),
        name="attend",
    )(scalars(bk, bq), qt, starts, *kv)


def attend_back_kernel(first_head, heads, bk, bq, parts, n_kv, sc, qt, st, lse, ot, *refs):
    do_parts, refs = refs[:parts], refs[parts:]
    kv, refs = refs[:n_kv], refs[n_kv + 1 :]
    n_out = 1 if n_kv == 1 else 4
    dq, dkv, (held, acc, dqa, do_all, sems) = (
        refs[:parts],
        refs[parts : parts + n_out],
        refs[parts + n_out + 1 :],
    )
    i = pl.program_id(0)
    per = held.shape[2] // bk
    cols = heads * HD
    start = st[...]
    qpos = sc[0] + i * bq + lax.broadcasted_iota(jnp.int32, (1, bq), 1)
    here = pl.ds(pl.multiple_of(i * bq, bq), bq)

    @pl.when(i == 0)
    def _():
        acc[...] = jnp.zeros_like(acc)
        dqa[...] = jnp.zeros_like(dqa)
        take_parts(sc[3], slice(first_head * HD, (first_head + heads) * HD), do_parts, do_all)
        load_keys(sc, kv, held, sems)

    delta = [
        jnp.sum(
            do_all[h * HD : (h + 1) * HD, here].astype(f32)
            * ot[h * HD : (h + 1) * HD, :].astype(f32),
            axis=0,
            keepdims=True,
        )
        for h in range(heads)
    ]

    def step(masked, j, carry):
        r = j // per
        off = pl.multiple_of((j % per) * bk, bk)
        if masked:
            ok = tile_mask(j, bk, bq, start, qpos)
        for h in range(heads):
            hs = slice(h * HD, (h + 1) * HD)
            vs = slice(cols + h * HD, cols + (h + 1) * HD)
            k = held[r, hs, pl.ds(off, bk)]
            v = held[r, vs, pl.ds(off, bk)]
            q = qt[(first_head + h) * HD : (first_head + h + 1) * HD, :]
            do = do_all[hs, here]
            s = tn(k, q) - lse[h : h + 1, :]
            if masked:
                s = jnp.where(ok, s, NEG)
            p = jnp.exp(s)
            ds = (p * (tn(v, do) - delta[h])).astype(bf16)
            acc[r, vs, pl.ds(off, bk)] += nt(do, p.astype(bf16))
            acc[r, hs, pl.ds(off, bk)] += nt(q, ds)
            dqa[hs, here] += nn(k, ds)
        return carry

    key_loop(sc, i, step, 0)

    @pl.when(i == pl.num_programs(0) - 1)
    def _():
        dqa[...] = dqa[...] * SCALE
        send_parts(sc[3], dqa, dq)
        if n_out == 1:
            dkv[0][...] = acc[...].astype(bf16)
        else:
            for target, pair, rows in (
                (0, (0, 2), slice(0, cols)),
                (1, (1, 3), slice(0, cols)),
                (2, (0, 1), slice(cols, 2 * cols)),
                (3, (2, 3), slice(cols, 2 * cols)),
            ):
                for n in range(2):
                    dkv[target][n] = acc[sc[1] ^ pair[n], rows, :].astype(bf16)


def attend_back(scalars, starts, qt, lse, ot, do_parts, kv, carried, first_head, heads, bk, bq):
    tok = qt.shape[1]
    cols = heads * HD
    parts = len(do_parts)
    runs = kv[0].shape[0] if len(kv) == 1 else 4
    bk, bq = min(bk, tok), min(bq, tok)
    whole = lambda *dims: pl.BlockSpec(dims, lambda i: (0,) * len(dims))
    out_kv = [(runs, 2 * cols, tok)] if len(kv) == 1 else [(2, cols, tok)] * 4
    return pl.pallas_call(
        functools.partial(attend_back_kernel, first_head, heads, bk, bq, parts, len(kv)),
        grid=(tok // bq,),
        in_specs=[
            SM,
            pl.BlockSpec((qt.shape[0], bq), lambda i: (0, i)),
            pl.BlockSpec((1, bq), lambda i: (0, i)),
            pl.BlockSpec((heads, bq), lambda i: (0, i)),
            pl.BlockSpec((cols, bq), lambda i: (0, i)),
        ]
        + [whole(*d.shape) for d in do_parts]
        + [HBM] * (len(kv) + 1),
        out_specs=[whole(cols, tok // parts)] * parts + [whole(*d) for d in out_kv] + [HBM],
        scratch_shapes=[
            pltpu.VMEM((runs, 2 * cols, tok), bf16),
            pltpu.VMEM((runs, 2 * cols, tok), f32),
            pltpu.VMEM((cols, tok), f32),
            pltpu.VMEM((cols, tok), bf16),
            pltpu.SemaphoreType.DMA((8,)),
        ],
        out_shape=[shape((cols, tok // parts))] * parts
        + [shape(d) for d in out_kv]
        + [shape(carried.shape)],
        input_output_aliases={5 + parts + len(kv): parts + len(out_kv)},
        compiler_params=params(),
        cost_estimate=cost(26),
        name="attend_back",
    )(scalars(bk, bq), qt, starts, lse, ot, *do_parts, *kv, carried)


ROOT = 0.7978845608028654


def middle_kernel(n_att, parts, sc, *refs):
    att, refs = refs[:n_att], refs[n_att:]
    x, cot, of_own, of_other, dn_own, dn_other, rows = refs[:7]
    refs = refs[7:]
    outputs, grad_mid, sums, fc_sums = refs[:4]
    d_att, (g_own, g_other) = refs[4 : 4 + parts], refs[4 + parts : 6 + parts]
    mid, att_t, low, low_t, cot_t, mlp, back = refs[6 + parts :]
    d = pl.program_id(0)
    width = x.shape[1]
    own, other = halves(sc[2], width)
    half = width // 2
    ffw = dn_own.shape[1]
    count = ffw // half
    cols = att_t.shape[0] // parts
    b_out, b_down, gain, shift = (rows[n : n + 1, :] for n in range(2, 6))

    @pl.when(d == 0)
    def _():
        group = n_att // parts
        row = 0
        for part in range(parts):
            for g in range(group):
                piece = att[part * group + g]
                att_t[row : row + piece.shape[0], :] = piece[...]
                row += piece.shape[0]
        att_low = att_t[...].T
        mine = theirs = 0.0
        for part in range(parts):
            piece = att_low[:, part * cols : (part + 1) * cols]
            mine += nn(piece, of_own[part, :cols, :])
            theirs += nn(piece, of_other[part, :cols, :])
        mid[:, own] = mine
        mid[:, other] = theirs
        mid[...] = x[...].astype(f32) + mid[...] + b_out
        normed, _ = norm(mid[...])
        low[...] = (normed * gain + shift).astype(bf16)
        low_t[...] = low[...].T
        cot_t[...] = cot[...].T
        mlp[...] = jnp.zeros_like(mlp)
        back[...] = jnp.zeros_like(back)

    own_rows = pl.ds(pl.multiple_of(sc[2] * half, half), half)
    other_rows = pl.ds(pl.multiple_of((1 - sc[2]) * half, half), half)
    terms = of_own[d, cols : cols + 16, :].astype(f32)
    pieces = [slice(cols + 16 + n * half, cols + 16 + (n + 1) * half) for n in range(count)]
    u = [
        nn(low[:, own], of_own[d, at, :])
        + nn(low[:, other], of_other[d, at, :])
        + sum(terms[t * count + n : t * count + n + 1, :] for t in range(3))
        for n, at in enumerate(pieces)
    ]
    u = jnp.concatenate(u, axis=1)
    t = jnp.tanh(ROOT * (u + 0.044715 * (u * u * u)))
    act = (0.5 * u * (1.0 + t)).astype(bf16)
    slope = 0.5 * (1.0 + t) + (0.5 * ROOT) * u * (1.0 - t * t) * (1.0 + 0.134145 * (u * u))
    d_act = nt(cot[:, own], dn_own[0]) + nt(cot[:, other], dn_other[0])
    dh = (d_act * slope).astype(bf16)
    mlp[:, own] += nn(act, dn_own[0])
    mlp[:, other] += nn(act, dn_other[0])
    for n, at in enumerate(pieces):
        dh_n = dh[:, n * half : (n + 1) * half]
        back[:, own] += nt(dh_n, of_own[d, at, :])
        back[:, other] += nt(dh_n, of_other[d, at, :])
    g_own[d, :, :ffw] = nn(low_t[own_rows, :], dh).astype(bf16)
    g_other[d, :, :ffw] = nn(low_t[other_rows, :], dh).astype(bf16)
    g_own[d, :, ffw : 2 * ffw] = nn(cot_t[own_rows, :], act).astype(bf16)
    g_other[d, :, ffw : 2 * ffw] = nn(cot_t[other_rows, :], act).astype(bf16)
    fc_sums[lax.rem(sc[3] - d + parts, parts)] = jnp.sum(dh.astype(f32), axis=0, keepdims=True)

    @pl.when(d == parts - 1)
    def _():
        normed, inverse = norm(mid[...])
        outputs[...] = (mid[...] + mlp[...] + b_down).astype(bf16)
        upper = cot[...].astype(f32)
        grad = back[...]
        down = upper + norm_gradient(grad, normed, inverse, gain)
        grad_mid[...] = down
        sums[0:1, :] = jnp.sum(down, axis=0, keepdims=True)
        sums[1:2, :] = jnp.sum(upper, axis=0, keepdims=True)
        sums[2:3, :] = jnp.sum(grad * normed, axis=0, keepdims=True)
        sums[3:4, :] = jnp.sum(grad, axis=0, keepdims=True)
        low[...] = down.astype(bf16)
        low_t[...] = low[...].T
        g_own[:, :, 2 * ffw + cols :] = jnp.zeros_like(g_own[:, :, 2 * ffw + cols :])
        g_other[:, :, 2 * ffw + cols :] = jnp.zeros_like(g_other[:, :, 2 * ffw + cols :])
        for part in range(parts):
            at = slice(part * cols, (part + 1) * cols)
            g_own[part, :, 2 * ffw : 2 * ffw + cols] = nt(low_t[own_rows, :], att_t[at, :]).astype(bf16)
            g_other[part, :, 2 * ffw : 2 * ffw + cols] = nt(low_t[other_rows, :], att_t[at, :]).astype(bf16)
            d_att[part][...] = (
                nt(of_own[part, :cols, :], low[:, own]) + nt(of_other[part, :cols, :], low[:, other])
            ).astype(bf16)


def middle(place, att, x, cot, of, dn, cols, table):
    parts, ffw, half = dn[0].shape
    sub, width = x.shape
    whole = lambda *dims: pl.BlockSpec(
        dims, lambda i, sc: (0,) * len(dims), pipeline_mode=pl.Buffered(1)
    )
    placed = pl.BlockSpec(
        (1, ffw, half), lambda i, sc: (i, 0, 0)
    )
    once = lambda a: whole(*a.shape)
    grads = (parts, half, 128 * ((2 * ffw + cols + 127) // 128))
    return pl.pallas_call(
        functools.partial(middle_kernel, len(att), parts),
        grid_spec=pltpu.PrefetchScalarGridSpec(
            num_scalar_prefetch=1,
            grid=(parts,),
            in_specs=[once(a) for a in att]
            + [once(x), once(cot), once(of[0]), once(of[1]), placed, placed, once(table)],
            out_specs=[whole(sub, width), whole(sub, width), whole(4, width), whole(parts, 1, ffw)]
            + [whole(cols, sub)] * parts
            + [whole(*grads)] * 2,
            scratch_shapes=[
                pltpu.VMEM((sub, width), f32),
                pltpu.VMEM((parts * cols, sub), bf16),
                pltpu.VMEM((sub, width), bf16),
                pltpu.VMEM((width, sub), bf16),
                pltpu.VMEM((width, sub), bf16),
                pltpu.VMEM((sub, width), f32),
                pltpu.VMEM((sub, width), f32),
            ],
        ),
        out_shape=[
            shape((sub, width)),
            shape((sub, width), f32),
            shape((4, width), f32),
            shape((parts, 1, ffw), f32),
        ]
        + [shape((cols, sub))] * parts
        + [shape(grads)] * 2,
        compiler_params=params(),
        cost_estimate=cost(19),
        name="middle",
    )(place, *att, x, cot, of[0], of[1], dn[0], dn[1], table)


def last_kernel(parts, pieces, sc, *refs):
    grads, refs = refs[: parts * pieces], refs[parts * pieces :]
    w_own, w_other, x, grad_mid, rows, mid_sums, fc_sums, out, sums, back_t, stacked = refs
    half = w_own.shape[1]
    wide = w_own.shape[2]
    own_rows = pl.ds(pl.multiple_of(sc[2] * half, half), half)
    other_rows = pl.ds(pl.multiple_of((1 - sc[2]) * half, half), half)
    ones = jnp.ones((8, x.shape[0]), bf16)
    sums[...] = jnp.zeros_like(sums)
    stacked[...] = jnp.zeros_like(stacked)
    for part in range(parts):
        row = 0
        for n in range(pieces):
            piece = grads[part * pieces + n]
            stacked[row : row + piece.shape[0], :] = piece[...]
            row += piece.shape[0]
        at = lax.rem(sc[3] - part + parts, parts)
        mine, theirs = nn(w_own[at], stacked[...]), nn(w_other[at], stacked[...])
        if part == 0:
            back_t[own_rows, :], back_t[other_rows, :] = mine, theirs
        else:
            back_t[own_rows, :] += mine
            back_t[other_rows, :] += theirs
        sums[pl.ds(6 + parts + at, 1), :wide] = nt(ones, stacked[...])[0:1, :]
    back = back_t[...].T
    normed, inverse = norm(x[...].astype(f32))
    out[...] = (grad_mid[...] + norm_gradient(back, normed, inverse, rows[0:1, :])).astype(bf16)
    sums[0:4, :] = mid_sums[...]
    sums[4:5, :] = jnp.sum(back * normed, axis=0, keepdims=True)
    sums[5:6, :] = jnp.sum(back, axis=0, keepdims=True)
    for part in range(parts):
        sums[6 + part : 7 + part, :] = fc_sums[part]


def last(place, grads, pieces, w, x, grad_mid, table, mid_sums, fc_sums):
    parts = w[0].shape[0]
    sub, width = x.shape
    rows = 8 * ((6 + 2 * parts + 7) // 8)
    return pl.pallas_call(
        functools.partial(last_kernel, parts, pieces),
        in_specs=[SM] + [VM] * (len(grads) + 7),
        out_specs=[VM, VM],
        out_shape=[shape((sub, width)), shape((rows, width), f32)],
        scratch_shapes=[pltpu.VMEM((width, sub), f32), pltpu.VMEM((w[0].shape[2], sub), bf16)],
        compiler_params=params(),
        cost_estimate=cost(6),
        name="last",
    )(place, *grads, w[0], w[1], x, grad_mid, table, mid_sums, fc_sums)


def fold_kernel(cut, sc, mine, theirs, lo_send, lo_keep, hi_send, hi_keep):
    i = pl.program_id(0)
    total = (mine[...].astype(f32) + theirs[...].astype(f32)).astype(bf16)
    lo, hi = total[None, :, :, :cut], total[None, :, :, cut:]

    @pl.when(i < 2)
    def _():
        lo_send[...] = lo

    @pl.when(i >= 2)
    def _():
        lo_keep[...] = lo

    @pl.when((i == 1) | (i == 2))
    def _():
        hi_send[...] = hi

    @pl.when((i == 0) | (i == 3))
    def _():
        hi_keep[...] = hi


def fold(place, mine, theirs):
    parts, rows, wide = mine.shape
    size = rows // 4
    cut = (wide // 256) * 128 if wide % 256 == 0 else (wide // 256 + 1) * 128
    block = pl.BlockSpec(
        (parts, size, wide),
        lambda i, sc: (
            0,
            sc[1] ^ jnp.where(i == 0, 1, jnp.where(i == 1, 3, jnp.where(i == 2, 2, 0))),
            0,
        ),
    )
    out = lambda width, index: pl.BlockSpec(
        (1, parts, size, width), lambda i, sc: (index(i), 0, 0, 0)
    )
    lo, hi = cut, wide - cut
    return pl.pallas_call(
        functools.partial(fold_kernel, cut),
        grid_spec=pltpu.PrefetchScalarGridSpec(
            num_scalar_prefetch=1,
            grid=(4,),
            in_specs=[block, block],
            out_specs=[
                out(lo, lambda i: jnp.minimum(i, 1)),
                out(lo, lambda i: jnp.where(i == 3, 0, 1)),
                out(hi, lambda i: jnp.where(i < 2, 1, 0)),
                out(hi, lambda i: jnp.where(i == 3, 0, 1)),
            ],
        ),
        out_shape=[
            shape((2, parts, size, lo)),
            shape((2, parts, size, lo)),
            shape((2, parts, size, hi)),
            shape((2, parts, size, hi)),
        ],
        compiler_params=params(),
        cost_estimate=cost(1 + 6 * parts / 4),
        name="fold",
    )(place, mine, theirs)


def body(
    n_shard,
    n_context,
    n_tensor,
    inputs,
    segments,
    w_qkv,
    w_out,
    w_fc,
    w_down,
    b_qv,
    b_out,
    b_fc,
    b_down,
    first_norm_gain,
    first_norm_bias,
    second_norm_gain,
    second_norm_bias,
    cotangent,
):
    _, tok, width = inputs.shape
    length = segments.shape[1]
    half, _, cols = w_qkv.shape
    heads = cols // HD
    ffw = w_fc.shape[1]
    sub = tok // n_tensor
    context = lax.axis_index("context")
    tensor = lax.axis_index("tensor")
    core = lax.axis_index("shard")
    first = context * tok
    place = jnp.stack([first, context, core, tensor]).astype(jnp.int32)
    grouped = n_context == 4
    x = inputs[0]
    cot = cotangent[0]
    row = lambda v: v[None, :]
    zero = jnp.zeros_like(b_out)
    table = jnp.concatenate(
        [
            first_norm_gain,
            first_norm_bias,
            b_out,
            b_down,
            second_norm_gain,
            second_norm_bias,
            zero,
            zero,
        ]
    ).reshape(8, width)
    after = lambda v, dep: lax.optimization_barrier((v, dep))[0]

    swap = lambda v: lax.ppermute(v, "shard", [(0, 1), (1, 0)])
    along_x = lambda v: lax.ppermute(v, "context", [(0, 1), (1, 0), (2, 3), (3, 2)])
    along_y = lambda v: lax.ppermute(v, "context", [(0, 2), (2, 0), (1, 3), (3, 1)])
    shift_by = lambda v, d: lax.ppermute(
        v, "tensor", [(s, (s + d) % n_tensor) for s in range(n_tensor)]
    )

    def gather_direct(v):
        return [v] + [shift_by(v, d) for d in range(1, n_tensor)]

    def gather_begin(v):
        if n_tensor != 4:
            return tuple(gather_direct(v))
        move = lambda perm: lax.ppermute(v, "tensor", perm)
        return (
            v,
            move([(0, 2), (1, 3), (2, 0), (3, 1)]),
            move([(0, 1), (1, 2), (2, 3)]),
            move([(3, 2), (2, 1), (1, 0)]),
        )

    def gather_end(state, hold=()):
        if n_tensor != 4:
            return list(state)
        v, two, right, left = state
        two = after(two, hold)
        far = lax.ppermute(two, "tensor", [(2, 3), (1, 0)])
        return [
            v,
            jnp.where(tensor == 0, far, right),
            two,
            jnp.where(tensor == 3, far, left),
        ]

    def scatter_line(pieces):
        if n_tensor != 4:
            total = pieces[0].astype(f32)
            for d in range(1, n_tensor):
                total += shift_by(pieces[d].astype(bf16), -d).astype(f32)
            return total
        move = lambda a, perm: lax.ppermute(a.astype(bf16), "tensor", perm)
        far = move(jnp.where(tensor == 0, pieces[1], pieces[3]), [(0, 1), (3, 2)])
        right = move(pieces[3], [(0, 1), (1, 2), (2, 3)])
        left = move(pieces[1], [(3, 2), (2, 1), (1, 0)])
        two = move(
            pieces[2].astype(f32) + far.astype(f32), [(0, 2), (1, 3), (2, 0), (3, 1)]
        )
        return (
            pieces[0].astype(f32) + right.astype(f32) + left.astype(f32) + two.astype(f32)
        )

    def scatter_begin(mine, theirs):
        theirs = swap(theirs)
        if not grouped:
            both = (mine.astype(f32) + theirs.astype(f32)).astype(bf16)
            return lax.psum_scatter(both, "context", scatter_dimension=1, tiled=True)
        return fold(place, mine, theirs)

    def scatter_first(state):
        if not grouped:
            return state
        lo_send, lo_keep, hi_send, hi_keep = state
        r, s = along_x(lo_send).astype(f32), along_y(hi_send).astype(f32)
        return (
            lo_keep[0].astype(f32) + r[0],
            hi_keep[0].astype(f32) + s[0],
            (lo_keep[1].astype(f32) + r[1]).astype(bf16),
            (hi_keep[1].astype(f32) + s[1]).astype(bf16),
        )

    def scatter_second(state):
        if not grouped:
            return state
        lo, hi, lo_send, hi_send = state
        lo += along_y(lo_send).astype(f32)
        hi += along_x(hi_send).astype(f32)
        return jnp.concatenate([lo, hi], axis=2)

    bounds = [jnp.sum((segments[0] < d).astype(jnp.int32)) for d in range(1, 5)]
    seg = lax.dynamic_slice_in_dim(segments[0], first, tok, 0)
    starts = jnp.zeros_like(seg)
    for d in range(1, 5):
        starts = jnp.where(seg == d, bounds[d - 1], starts)

    def scalars(bk, bq):
        count = tok // bq
        begin = starts.reshape(count, bq)
        base = first + jnp.arange(count, dtype=jnp.int32) * bq
        lo = begin[:, 0] // bk
        diag = base // bk
        end = (base + bq + bk - 1) // bk
        full = jnp.minimum(jnp.maximum((begin[:, -1] + bk - 1) // bk, lo), diag)
        table = jnp.stack([lo, full, diag, end], axis=1).reshape(-1)
        return jnp.concatenate([place, table.astype(jnp.int32)])

    qkv_own = w_qkv.reshape(half, 3 * cols)
    low_one, qt, kt, vt = project(
        place,
        x,
        qkv_own,
        swap(qkv_own),
        b_qv,
        table,
    )

    terms, rest = [], b_fc
    for _ in range(3):
        term = lax.reduce_precision(rest, 8, 7)
        terms.append(term.astype(bf16).reshape(ffw // half, half))
        rest = rest - term
    terms = jnp.concatenate(terms, axis=0)
    terms = jnp.pad(terms, ((0, 16 - terms.shape[0]), (0, 0)))
    packed = jnp.concatenate([w_out, terms, w_fc[:, :half], w_fc[:, half:]], axis=0)
    packed = gather_begin(packed)
    kv = []
    hold = ()
    head = 0
    for g in GROUPS:
        rows = slice(head * HD, (head + g) * HD)
        head += g
        k, v = kt[rows], vt[rows]
        if grouped:
            kx, vy = along_x(k), along_y(v)
            k_two, v_two = jnp.stack([k, kx]), jnp.stack([v, vy])
            k_two, v_two = after((k_two, v_two), packed[1:])
            k_yd, v_xd = along_y(k_two), along_x(v_two)
            hold = (k_two, v_two)
            kv.append([k, kx, k_yd, v, vy, v_xd])
        else:
            kv.append([lax.all_gather(jnp.concatenate([k, v], axis=0), "context", axis=0)])

    dn = gather_begin(after(w_down, packed[1]))
    saved = []
    att = [[] for _ in range(n_tensor)]
    head = 0
    for g, held in zip(GROUPS, kv):
        results = attend(scalars, row(starts), after(qt, packed[1:]), held, head, g, BK_F, BQ_F, n_tensor)
        lse, ot, *out = results
        saved.append((lse, ot))
        att[0].append(out[0])
        for d in range(1, n_tensor):
            att[d].append(shift_by(out[d], d))
        head += g

    of = jnp.stack(after(gather_end(packed, hold), att[1:]))
    of = (of, swap(of))
    dn = jnp.stack(gather_end(dn, att[1:]))
    dn = (dn, swap(dn))
    x_sub = lax.dynamic_slice_in_dim(x, tensor * sub, sub, 0)
    cot_sub = lax.dynamic_slice_in_dim(cot, tensor * sub, sub, 0)
    outputs_sub, grad_mid, mid_sums, fc_sums, *rest = middle(
        place,
        [piece for part in att for piece in part],
        x_sub,
        cot_sub,
        of,
        dn,
        cols,
        table,
    )
    d_att, (g_own, g_other) = rest[:n_tensor], rest[n_tensor:]
    do_parts = [d_att[0]] + [
        shift_by(d_att[d], -d) for d in range(1, n_tensor)
    ]

    def spread(pieces):
        whole = jnp.zeros((tok, width), f32)
        for d in range(n_tensor):
            at = lax.rem(tensor - d + n_tensor, n_tensor) * sub
            whole = lax.dynamic_update_slice_in_dim(whole, pieces[d].astype(f32), at, 0)
        return whole[None]

    folded = scatter_begin(g_own, g_other)
    hop_one = folded[0] if grouped else folded
    qkv_wide = jnp.pad(qkv_own, ((0, 0), (0, width - 3 * cols)))
    carried = jnp.concatenate([outputs_sub, qkv_wide], axis=0)
    folded = scatter_begin(g_own, g_other)
    hop_one = folded[0] if grouped else folded
    qkv_wide = jnp.pad(qkv_own, ((0, 0), (0, width - 3 * cols)))
    outputs_and_qkv = lax.all_gather(
        jnp.concatenate([outputs_sub, qkv_wide], axis=0), "tensor", axis=0
    )
    wide = scatter_first(folded)
    wide_sends = wide[2:]
    wide = scatter_second(wide)

    dq_pieces, dkv_pieces, dqkv = [], [], []
    head = 0
    queries, keys, values = [], [], []
    sent = [[] for _ in range(n_tensor)]
    for g, held, (lse, ot) in zip(GROUPS, kv, saved):
        out = attend_back(
            scalars, row(starts), after(qt, hop_one), lse, ot, do_parts, held, carried, head, g, BK_B, BQ_B
        )
        back_done = out[-1]
        *out, carried = out
        dq, dkv = after(out[:n_tensor], wide_sends), out[n_tensor:]
        if grouped:
            dk_keep, dk_send, dv_keep, dv_send = dkv
            dk_send, dv_send = after((dk_send, dv_send), wide_sends)
            r = along_x(dk_send).astype(f32)
            s = along_y(dv_send).astype(f32)
            r2 = along_y((dk_keep[1].astype(f32) + r[1]).astype(bf16)).astype(f32)
            s2 = along_x((dv_keep[1].astype(f32) + s[1]).astype(bf16)).astype(f32)
            dk = (dk_keep[0].astype(f32) + r[0] + r2).astype(bf16)
            dv = (dv_keep[0].astype(f32) + s[0] + s2).astype(bf16)
        else:
            both = lax.psum_scatter(dkv[0], "context", scatter_dimension=0, tiled=True)[0]
            dk, dv = both[: g * HD], both[g * HD :]
        queries.append(dq)
        keys.append(dk)
        values.append(dv)
        head += g

    wide_grads = scatter_line([wide[d] for d in range(n_tensor)])

    def part_of(v, d):
        at = lax.rem(tensor + d, n_tensor) * sub
        return lax.dynamic_slice_in_dim(v, at, sub, 1)

    grads = []
    both = jnp.concatenate(keys + values, axis=0)
    for d in range(n_tensor):
        piece = jnp.concatenate([q[d] for q in queries] + [part_of(both, d)], axis=0)
        grads.append(shift_by(piece, d) if d else piece)
    pieces = 1

    dq_whole = []
    for q in queries:
        whole = jnp.zeros((q[0].shape[0], tok), bf16)
        for d in range(n_tensor):
            at = lax.rem(tensor + d, n_tensor) * sub
            whole = lax.dynamic_update_slice_in_dim(whole, q[d], at, 1)
        dq_whole.append(whole)
    outputs_and_qkv = lax.all_gather(carried, "tensor", axis=0)
    outputs = outputs_and_qkv[:, :sub].reshape(tok, width)
    qkv = outputs_and_qkv[:, sub:]
    qkv = (qkv, swap(qkv))
    stacked = jnp.concatenate(
        dq_whole + [both, jnp.zeros((-3 * cols % 128, tok), bf16)], axis=0
    )
    qkv_grad = jnp.einsum(
        "td,ct->dc", low_one, stacked, preferred_element_type=f32
    ).astype(bf16)
    qkv_mine = lax.dynamic_slice_in_dim(qkv_grad, core * half, half, 0)
    qkv_theirs = lax.dynamic_slice_in_dim(qkv_grad, (1 - core) * half, half, 0)
    qkv_folded = scatter_begin(qkv_mine[None], qkv_theirs[None])

    input_sub, small = last(
        place, grads, pieces, qkv, x_sub, after(grad_mid, qkv_folded), table, mid_sums, fc_sums
    )
    input_gradient = spread(gather_direct(input_sub))
    outputs = after(outputs, input_sub).astype(f32)[None]
    qkv_grads = scatter_second(scatter_first(qkv_folded))[0]

    if grouped and n_tensor == 4 and n_shard == 2:
        small += swap(small)
        small += along_x(small)
        small += along_y(small)
        small += lax.ppermute(small, "tensor", [(0, 1), (1, 0), (2, 3), (3, 2)])
        small += lax.ppermute(small, "tensor", [(0, 2), (2, 0), (1, 3), (3, 1)])
    else:
        small = lax.psum(small, ("shard", "context", "tensor"))
    fc_total = lax.dynamic_index_in_dim(small, 6 + tensor, 0, keepdims=False)
    qv_total = lax.dynamic_index_in_dim(small, 6 + n_tensor + tensor, 0, keepdims=False)
    qv_total = jnp.stack([qv_total[:cols], qv_total[2 * cols : 3 * cols]])
    return (
        outputs,
        input_gradient,
        qkv_grads[:, : 3 * cols].astype(f32).reshape(-1, 3, cols),
        wide_grads[:, 2 * ffw : 2 * ffw + cols].T,
        wide_grads[:, :ffw],
        wide_grads[:, ffw : 2 * ffw].T,
        qv_total,
        small[0],
        fc_total,
        small[1],
        small[4],
        small[5],
        small[2],
        small[3],
    )


def solution(mesh):
    sizes = dict(mesh.shape)
    placed = (
        P("shard", "context", None),
        P("shard", None),
        P("shard", None, "tensor"),
        P("tensor", "shard"),
        P("shard", "tensor"),
        P("tensor", "shard"),
        P(None, "tensor"),
        P(),
        P("tensor"),
        P(),
        P(),
        P(),
        P(),
        P(),
        P("shard", "context", None),
    )
    return jax.shard_map(
        functools.partial(body, sizes["shard"], sizes["context"], sizes["tensor"]),
        mesh=mesh,
        in_specs=placed,
        out_specs=(
            P("shard", "context", None),
            P("shard", "context", None),
            P(("shard", "context"), None, "tensor"),
            P("tensor", ("shard", "context")),
            P(("shard", "context"), "tensor"),
            P("tensor", ("shard", "context")),
            P(None, "tensor"),
            P(),
            P("tensor"),
            P(),
            P(),
            P(),
            P(),
            P(),
        ),
        check_vma=False,
    )
```

```python
import functools

import jax
import jax.numpy as jnp
from jax import lax
from jax.experimental import pallas as pl
from jax.experimental.pallas import tpu as pltpu
from jax.sharding import PartitionSpec as P

HD = 64
EPS = 1e-05
NEG = -1e30
SCALE = float(HD) ** -0.5
VMEM_LIMIT = 56 * 1024 * 1024
GROUPS = (3,)
BK_F, BQ_F = 512, 512
BK_B, BQ_B = 512, 512
f32 = jnp.float32
bf16 = jnp.bfloat16
VM = pl.BlockSpec(memory_space=pltpu.VMEM)
SM = pl.BlockSpec(memory_space=pltpu.SMEM)
HBM = pl.BlockSpec(memory_space=pl.ANY)


def nn(a, b):
    return lax.dot_general(a, b, (((1,), (0,)), ((), ())), preferred_element_type=f32)


def tn(a, b):
    return lax.dot_general(a, b, (((0,), (0,)), ((), ())), preferred_element_type=f32)


def nt(a, b):
    return lax.dot_general(a, b, (((1,), (1,)), ((), ())), preferred_element_type=f32)


def params():
    return pltpu.CompilerParams(vmem_limit_bytes=VMEM_LIMIT)


def cost(microseconds):
    return pl.CostEstimate(
        flops=int(microseconds * 1.15e9), bytes_accessed=1 << 20, transcendentals=0
    )


def shape(dims, kind=bf16):
    return jax.ShapeDtypeStruct(dims, kind)


def halves(core, width):
    half = width // 2
    own = pl.ds(pl.multiple_of(core * half, 128), half)
    other = pl.ds(pl.multiple_of((1 - core) * half, 128), half)
    return own, other


def norm(value):
    centred = value - jnp.mean(value, axis=-1, keepdims=True)
    inverse = lax.rsqrt(jnp.mean(centred * centred, axis=-1, keepdims=True) + EPS)
    return centred * inverse, inverse


def norm_gradient(grad, normed, inverse, gain):
    scaled = grad * gain
    return inverse * (
        scaled
        - jnp.mean(scaled, axis=-1, keepdims=True)
        - normed * jnp.mean(scaled * normed, axis=-1, keepdims=True)
    )


def project_kernel(sc, x, w_own, w_other, b_qv, rows, low, qt, kt, vt):
    own, other = halves(sc[2], x.shape[1])
    cols = qt.shape[0]
    normed, _ = norm(x[...].astype(f32))
    low[...] = (normed * rows[0:1, :] + rows[1:2, :]).astype(bf16)
    projected = nn(low[:, own], w_own[...]) + nn(low[:, other], w_other[...])
    qt[...] = ((projected[:, :cols] + b_qv[0:1, :]) * SCALE).T.astype(bf16)
    kt[...] = projected[:, cols : 2 * cols].T.astype(bf16)
    vt[...] = (projected[:, 2 * cols :] + b_qv[1:2, :]).T.astype(bf16)


def project(place, x, w_own, w_other, b_qv, table):
    tok, width = x.shape
    cols = b_qv.shape[1]
    rows = min(256, tok)
    fixed = lambda a: pl.BlockSpec(a.shape, lambda i: (0,) * a.ndim)
    across = pl.BlockSpec((cols, rows), lambda i: (0, i))
    return pl.pallas_call(
        project_kernel,
        grid=(tok // rows,),
        in_specs=[SM, pl.BlockSpec((rows, width), lambda i: (i, 0))]
        + [fixed(a) for a in (w_own, w_other, b_qv, table)],
        out_specs=[pl.BlockSpec((rows, width), lambda i: (i, 0)), across, across, across],
        out_shape=[shape((tok, width))] + [shape((cols, tok))] * 3,
        compiler_params=params(),
        cost_estimate=cost(7),
        name="project",
    )(place, x, w_own, w_other, b_qv, table)


def key_loop(sc, i, step, carry):
    lo, full, diag, end = sc[4 * i + 4], sc[4 * i + 5], sc[4 * i + 6], sc[4 * i + 7]
    carry = lax.fori_loop(lo, full, functools.partial(step, True), carry)
    carry = lax.fori_loop(full, diag, functools.partial(step, False), carry)
    return lax.fori_loop(diag, end, functools.partial(step, True), carry)


def tile_mask(j, bk, bq, start, qpos):
    kpos = j * bk + lax.broadcasted_iota(jnp.int32, (bk, bq), 0)
    return (kpos >= start) & (kpos <= qpos)


def load_keys(sc, kv, held, sems):
    if len(kv) == 1:
        copies = [pltpu.make_async_copy(kv[0], held, sems.at[0])]
    else:
        k, k_x, k_yd, v, v_y, v_xd = kv
        rows = k.shape[0]
        pieces = [(k, 0, 0), (k_x, 0, 1), (k_yd.at[0], 0, 2), (k_yd.at[1], 0, 3)]
        pieces += [(v, 1, 0), (v_y, 1, 2), (v_xd.at[0], 1, 1), (v_xd.at[1], 1, 3)]
        copies = [
            pltpu.make_async_copy(
                piece, held.at[sc[1] ^ run, pl.ds(which * rows, rows), :], sems.at[n]
            )
            for n, (piece, which, run) in enumerate(pieces)
        ]
    for copy in copies:
        copy.start()
    for copy in copies:
        copy.wait()


def attend_kernel(first_head, heads, bk, bq, parts, n_kv, sc, qt, st, *refs):
    kv, refs = refs[:n_kv], refs[n_kv:]
    lse, ot, out, (held, acc, sems) = refs[0], refs[1], refs[2 : 2 + parts], refs[2 + parts :]
    i = pl.program_id(0)
    per = held.shape[2] // bk
    cols = heads * HD
    start = st[...]
    qpos = sc[0] + i * bq + lax.broadcasted_iota(jnp.int32, (1, bq), 1)

    @pl.when(i == 0)
    def _():
        load_keys(sc, kv, held, sems)

    acc[...] = jnp.zeros_like(acc)

    def step(masked, j, carry):
        r = j // per
        off = pl.multiple_of((j % per) * bk, bk)
        new = []
        if masked:
            ok = tile_mask(j, bk, bq, start, qpos)
        for h in range(heads):
            m, l = carry[h]
            hs = slice(h * HD, (h + 1) * HD)
            s = tn(
                held[r, hs, pl.ds(off, bk)],
                qt[(first_head + h) * HD : (first_head + h + 1) * HD, :],
            )
            if masked:
                s = jnp.where(ok, s, NEG)
            m2 = jnp.maximum(m, jnp.max(s, axis=0, keepdims=True))
            p = jnp.exp(s - m2)
            al = jnp.exp(m - m2)
            l = l * al + jnp.sum(p, axis=0, keepdims=True)
            v = held[r, cols + h * HD : cols + (h + 1) * HD, pl.ds(off, bk)]
            acc[hs, :] = acc[hs, :] * al + nn(v, p.astype(bf16))
            new.append((m2, l))
        return tuple(new)

    one = (jnp.full((1, bq), NEG, f32), jnp.zeros((1, bq), f32))
    res = key_loop(sc, i, step, (one,) * heads)
    here = pl.ds(pl.multiple_of(i * bq, bq), bq)
    for h in range(heads):
        m, l = res[h]
        ot[h * HD : (h + 1) * HD, here] = (acc[h * HD : (h + 1) * HD, :] / l).astype(bf16)
        lse[h : h + 1, :] = m + jnp.log(l)

    @pl.when(i == pl.num_programs(0) - 1)
    def _():
        send_parts(sc[3], ot, out)


def send_parts(me, source, out):
    parts, size = len(out), out[0].shape[1]
    for d in range(parts):
        if size % 128 == 0:
            at = pl.multiple_of(lax.rem(me + d, parts) * size, 128)
            out[d][...] = source[:, pl.ds(at, size)].astype(out[d].dtype)
        else:
            for n in range(parts):

                @pl.when(lax.rem(me + d, parts) == n)
                def _():
                    out[d][...] = source[:, n * size : (n + 1) * size].astype(out[d].dtype)


def take_parts(me, rows, parts, target):
    size = parts[0].shape[1]
    for d in range(len(parts)):
        if size % 128 == 0:
            at = pl.multiple_of(lax.rem(me + d, len(parts)) * size, 128)
            target[:, pl.ds(at, size)] = parts[d][rows, :]
        else:
            for n in range(len(parts)):

                @pl.when(lax.rem(me + d, len(parts)) == n)
                def _():
                    target[:, n * size : (n + 1) * size] = parts[d][rows, :]


def attend(scalars, starts, qt, kv, first_head, heads, bk, bq, parts):
    tok = qt.shape[1]
    cols = heads * HD
    runs = kv[0].shape[0] if len(kv) == 1 else 4
    bk, bq = min(bk, tok), min(bq, tok)
    whole = lambda a, b: pl.BlockSpec((a, b), lambda i: (0, 0))
    return pl.pallas_call(
        functools.partial(attend_kernel, first_head, heads, bk, bq, parts, len(kv)),
        grid=(tok // bq,),
        in_specs=[
            SM,
            pl.BlockSpec((qt.shape[0], bq), lambda i: (0, i)),
            pl.BlockSpec((1, bq), lambda i: (0, i)),
        ]
        + [HBM] * len(kv),
        out_specs=[pl.BlockSpec((heads, bq), lambda i: (0, i)), whole(cols, tok)]
        + [whole(cols, tok // parts)] * parts,
        scratch_shapes=[
            pltpu.VMEM((runs, 2 * cols, tok), bf16),
            pltpu.VMEM((cols, bq), f32),
            pltpu.SemaphoreType.DMA((8,)),
        ],
        out_shape=[shape((heads, tok), f32), shape((cols, tok))]
        + [shape((cols, tok // parts))] * parts,
        compiler_params=params(),
        cost_estimate=cost(20),
        name="attend",
    )(scalars(bk, bq), qt, starts, *kv)


def attend_back_kernel(first_head, heads, bk, bq, parts, n_kv, sc, qt, st, lse, ot, *refs):
    do_parts, refs = refs[:parts], refs[parts:]
    kv, refs = refs[:n_kv], refs[n_kv + 1 :]
    n_out = 1 if n_kv == 1 else 4
    dq, dkv, (held, acc, dqa, do_all, sems) = (
        refs[:parts],
        refs[parts : parts + n_out],
        refs[parts + n_out + 1 :],
    )
    i = pl.program_id(0)
    per = held.shape[2] // bk
    cols = heads * HD
    start = st[...]
    qpos = sc[0] + i * bq + lax.broadcasted_iota(jnp.int32, (1, bq), 1)
    here = pl.ds(pl.multiple_of(i * bq, bq), bq)

    @pl.when(i == 0)
    def _():
        acc[...] = jnp.zeros_like(acc)
        dqa[...] = jnp.zeros_like(dqa)
        take_parts(sc[3], slice(first_head * HD, (first_head + heads) * HD), do_parts, do_all)
        load_keys(sc, kv, held, sems)

    delta = [
        jnp.sum(
            do_all[h * HD : (h + 1) * HD, here].astype(f32)
            * ot[h * HD : (h + 1) * HD, :].astype(f32),
            axis=0,
            keepdims=True,
        )
        for h in range(heads)
    ]

    def step(masked, j, carry):
        r = j // per
        off = pl.multiple_of((j % per) * bk, bk)
        if masked:
            ok = tile_mask(j, bk, bq, start, qpos)
        for h in range(heads):
            hs = slice(h * HD, (h + 1) * HD)
            vs = slice(cols + h * HD, cols + (h + 1) * HD)
            k = held[r, hs, pl.ds(off, bk)]
            v = held[r, vs, pl.ds(off, bk)]
            q = qt[(first_head + h) * HD : (first_head + h + 1) * HD, :]
            do = do_all[hs, here]
            s = tn(k, q) - lse[h : h + 1, :]
            if masked:
                s = jnp.where(ok, s, NEG)
            p = jnp.exp(s)
            ds = (p * (tn(v, do) - delta[h])).astype(bf16)
            acc[r, vs, pl.ds(off, bk)] += nt(do, p.astype(bf16))
            acc[r, hs, pl.ds(off, bk)] += nt(q, ds)
            dqa[hs, here] += nn(k, ds)
        return carry

    key_loop(sc, i, step, 0)

    @pl.when(i == pl.num_programs(0) - 1)
    def _():
        dqa[...] = dqa[...] * SCALE
        send_parts(sc[3], dqa, dq)
        if n_out == 1:
            dkv[0][...] = acc[...].astype(bf16)
        else:
            for target, pair, rows in (
                (0, (0, 2), slice(0, cols)),
                (1, (1, 3), slice(0, cols)),
                (2, (0, 1), slice(cols, 2 * cols)),
                (3, (2, 3), slice(cols, 2 * cols)),
            ):
                for n in range(2):
                    dkv[target][n] = acc[sc[1] ^ pair[n], rows, :].astype(bf16)


def attend_back(scalars, starts, qt, lse, ot, do_parts, kv, carried, first_head, heads, bk, bq):
    tok = qt.shape[1]
    cols = heads * HD
    parts = len(do_parts)
    runs = kv[0].shape[0] if len(kv) == 1 else 4
    bk, bq = min(bk, tok), min(bq, tok)
    whole = lambda *dims: pl.BlockSpec(dims, lambda i: (0,) * len(dims))
    out_kv = [(runs, 2 * cols, tok)] if len(kv) == 1 else [(2, cols, tok)] * 4
    return pl.pallas_call(
        functools.partial(attend_back_kernel, first_head, heads, bk, bq, parts, len(kv)),
        grid=(tok // bq,),
        in_specs=[
            SM,
            pl.BlockSpec((qt.shape[0], bq), lambda i: (0, i)),
            pl.BlockSpec((1, bq), lambda i: (0, i)),
            pl.BlockSpec((heads, bq), lambda i: (0, i)),
            pl.BlockSpec((cols, bq), lambda i: (0, i)),
        ]
        + [whole(*d.shape) for d in do_parts]
        + [HBM] * (len(kv) + 1),
        out_specs=[whole(cols, tok // parts)] * parts + [whole(*d) for d in out_kv] + [HBM],
        scratch_shapes=[
            pltpu.VMEM((runs, 2 * cols, tok), bf16),
            pltpu.VMEM((runs, 2 * cols, tok), f32),
            pltpu.VMEM((cols, tok), f32),
            pltpu.VMEM((cols, tok), bf16),
            pltpu.SemaphoreType.DMA((8,)),
        ],
        out_shape=[shape((cols, tok // parts))] * parts
        + [shape(d) for d in out_kv]
        + [shape(carried.shape)],
        input_output_aliases={5 + parts + len(kv): parts + len(out_kv)},
        compiler_params=params(),
        cost_estimate=cost(26),
        name="attend_back",
    )(scalars(bk, bq), qt, starts, lse, ot, *do_parts, *kv, carried)


ROOT = 0.7978845608028654


def middle_kernel(n_att, parts, sc, *refs):
    att, refs = refs[:n_att], refs[n_att:]
    x, cot, of_own, of_other, dn_own, dn_other, rows = refs[:7]
    refs = refs[7:]
    outputs, grad_mid, sums, fc_sums = refs[:4]
    d_att, (g_own, g_other) = refs[4 : 4 + parts], refs[4 + parts : 6 + parts]
    mid, att_t, low, low_t, cot_t, mlp, back = refs[6 + parts :]
    d = pl.program_id(0)
    width = x.shape[1]
    own, other = halves(sc[2], width)
    half = width // 2
    ffw = dn_own.shape[1]
    count = ffw // half
    cols = att_t.shape[0] // parts
    b_out, b_down, gain, shift = (rows[n : n + 1, :] for n in range(2, 6))

    @pl.when(d == 0)
    def _():
        group = n_att // parts
        row = 0
        for part in range(parts):
            for g in range(group):
                piece = att[part * group + g]
                att_t[row : row + piece.shape[0], :] = piece[...]
                row += piece.shape[0]
        att_low = att_t[...].T
        mine = theirs = 0.0
        for part in range(parts):
            piece = att_low[:, part * cols : (part + 1) * cols]
            mine += nn(piece, of_own[part, :cols, :])
            theirs += nn(piece, of_other[part, :cols, :])
        mid[:, own] = mine
        mid[:, other] = theirs
        mid[...] = x[...].astype(f32) + mid[...] + b_out
        normed, _ = norm(mid[...])
        low[...] = (normed * gain + shift).astype(bf16)
        low_t[...] = low[...].T
        cot_t[...] = cot[...].T
        mlp[...] = jnp.zeros_like(mlp)
        back[...] = jnp.zeros_like(back)

    own_rows = pl.ds(pl.multiple_of(sc[2] * half, half), half)
    other_rows = pl.ds(pl.multiple_of((1 - sc[2]) * half, half), half)
    terms = of_own[d, cols : cols + 16, :].astype(f32)
    pieces = [slice(cols + 16 + n * half, cols + 16 + (n + 1) * half) for n in range(count)]
    u = [
        nn(low[:, own], of_own[d, at, :])
        + nn(low[:, other], of_other[d, at, :])
        + sum(terms[t * count + n : t * count + n + 1, :] for t in range(3))
        for n, at in enumerate(pieces)
    ]
    u = jnp.concatenate(u, axis=1)
    t = jnp.tanh(ROOT * (u + 0.044715 * (u * u * u)))
    act = (0.5 * u * (1.0 + t)).astype(bf16)
    slope = 0.5 * (1.0 + t) + (0.5 * ROOT) * u * (1.0 - t * t) * (1.0 + 0.134145 * (u * u))
    d_act = nt(cot[:, own], dn_own[0]) + nt(cot[:, other], dn_other[0])
    dh = (d_act * slope).astype(bf16)
    mlp[:, own] += nn(act, dn_own[0])
    mlp[:, other] += nn(act, dn_other[0])
    for n, at in enumerate(pieces):
        dh_n = dh[:, n * half : (n + 1) * half]
        back[:, own] += nt(dh_n, of_own[d, at, :])
        back[:, other] += nt(dh_n, of_other[d, at, :])
    g_own[d, :, :ffw] = nn(low_t[own_rows, :], dh).astype(bf16)
    g_other[d, :, :ffw] = nn(low_t[other_rows, :], dh).astype(bf16)
    g_own[d, :, ffw : 2 * ffw] = nn(cot_t[own_rows, :], act).astype(bf16)
    g_other[d, :, ffw : 2 * ffw] = nn(cot_t[other_rows, :], act).astype(bf16)
    fc_sums[lax.rem(sc[3] - d + parts, parts)] = jnp.sum(dh.astype(f32), axis=0, keepdims=True)

    @pl.when(d == parts - 1)
    def _():
        normed, inverse = norm(mid[...])
        outputs[...] = (mid[...] + mlp[...] + b_down).astype(bf16)
        upper = cot[...].astype(f32)
        grad = back[...]
        down = upper + norm_gradient(grad, normed, inverse, gain)
        grad_mid[...] = down
        sums[0:1, :] = jnp.sum(down, axis=0, keepdims=True)
        sums[1:2, :] = jnp.sum(upper, axis=0, keepdims=True)
        sums[2:3, :] = jnp.sum(grad * normed, axis=0, keepdims=True)
        sums[3:4, :] = jnp.sum(grad, axis=0, keepdims=True)
        low[...] = down.astype(bf16)
        low_t[...] = low[...].T
        g_own[:, :, 2 * ffw + cols :] = jnp.zeros_like(g_own[:, :, 2 * ffw + cols :])
        g_other[:, :, 2 * ffw + cols :] = jnp.zeros_like(g_other[:, :, 2 * ffw + cols :])
        for part in range(parts):
            at = slice(part * cols, (part + 1) * cols)
            g_own[part, :, 2 * ffw : 2 * ffw + cols] = nt(low_t[own_rows, :], att_t[at, :]).astype(bf16)
            g_other[part, :, 2 * ffw : 2 * ffw + cols] = nt(low_t[other_rows, :], att_t[at, :]).astype(bf16)
            d_att[part][...] = (
                nt(of_own[part, :cols, :], low[:, own]) + nt(of_other[part, :cols, :], low[:, other])
            ).astype(bf16)


def middle(place, att, x, cot, of, dn, cols, table):
    parts, ffw, half = dn[0].shape
    sub, width = x.shape
    whole = lambda *dims: pl.BlockSpec(
        dims, lambda i, sc: (0,) * len(dims), pipeline_mode=pl.Buffered(1)
    )
    placed = pl.BlockSpec(
        (1, ffw, half), lambda i, sc: (i, 0, 0)
    )
    once = lambda a: whole(*a.shape)
    grads = (parts, half, 128 * ((2 * ffw + cols + 127) // 128))
    return pl.pallas_call(
        functools.partial(middle_kernel, len(att), parts),
        grid_spec=pltpu.PrefetchScalarGridSpec(
            num_scalar_prefetch=1,
            grid=(parts,),
            in_specs=[once(a) for a in att]
            + [once(x), once(cot), once(of[0]), once(of[1]), placed, placed, once(table)],
            out_specs=[whole(sub, width), whole(sub, width), whole(4, width), whole(parts, 1, ffw)]
            + [whole(cols, sub)] * parts
            + [whole(*grads)] * 2,
            scratch_shapes=[
                pltpu.VMEM((sub, width), f32),
                pltpu.VMEM((parts * cols, sub), bf16),
                pltpu.VMEM((sub, width), bf16),
                pltpu.VMEM((width, sub), bf16),
                pltpu.VMEM((width, sub), bf16),
                pltpu.VMEM((sub, width), f32),
                pltpu.VMEM((sub, width), f32),
            ],
        ),
        out_shape=[
            shape((sub, width)),
            shape((sub, width), f32),
            shape((4, width), f32),
            shape((parts, 1, ffw), f32),
        ]
        + [shape((cols, sub))] * parts
        + [shape(grads)] * 2,
        compiler_params=params(),
        cost_estimate=cost(19),
        name="middle",
    )(place, *att, x, cot, of[0], of[1], dn[0], dn[1], table)


def last_kernel(parts, pieces, sc, *refs):
    grads, refs = refs[: parts * pieces], refs[parts * pieces :]
    w_own, w_other, x, grad_mid, rows, mid_sums, fc_sums, out, sums, back_t, stacked = refs
    half = w_own.shape[1]
    wide = w_own.shape[2]
    own_rows = pl.ds(pl.multiple_of(sc[2] * half, half), half)
    other_rows = pl.ds(pl.multiple_of((1 - sc[2]) * half, half), half)
    ones = jnp.ones((8, x.shape[0]), bf16)
    sums[...] = jnp.zeros_like(sums)
    stacked[...] = jnp.zeros_like(stacked)
    for part in range(parts):
        row = 0
        for n in range(pieces):
            piece = grads[part * pieces + n]
            stacked[row : row + piece.shape[0], :] = piece[...]
            row += piece.shape[0]
        at = lax.rem(sc[3] - part + parts, parts)
        mine, theirs = nn(w_own[at], stacked[...]), nn(w_other[at], stacked[...])
        if part == 0:
            back_t[own_rows, :], back_t[other_rows, :] = mine, theirs
        else:
            back_t[own_rows, :] += mine
            back_t[other_rows, :] += theirs
        sums[pl.ds(6 + parts + at, 1), :wide] = nt(ones, stacked[...])[0:1, :]
    back = back_t[...].T
    normed, inverse = norm(x[...].astype(f32))
    out[...] = (grad_mid[...] + norm_gradient(back, normed, inverse, rows[0:1, :])).astype(bf16)
    sums[0:4, :] = mid_sums[...]
    sums[4:5, :] = jnp.sum(back * normed, axis=0, keepdims=True)
    sums[5:6, :] = jnp.sum(back, axis=0, keepdims=True)
    for part in range(parts):
        sums[6 + part : 7 + part, :] = fc_sums[part]


def last(place, grads, pieces, w, x, grad_mid, table, mid_sums, fc_sums):
    parts = w[0].shape[0]
    sub, width = x.shape
    rows = 8 * ((6 + 2 * parts + 7) // 8)
    return pl.pallas_call(
        functools.partial(last_kernel, parts, pieces),
        in_specs=[SM] + [VM] * (len(grads) + 7),
        out_specs=[VM, VM],
        out_shape=[shape((sub, width)), shape((rows, width), f32)],
        scratch_shapes=[pltpu.VMEM((width, sub), f32), pltpu.VMEM((w[0].shape[2], sub), bf16)],
        compiler_params=params(),
        cost_estimate=cost(6),
        name="last",
    )(place, *grads, w[0], w[1], x, grad_mid, table, mid_sums, fc_sums)


def fold_kernel(cut, sc, mine, theirs, *refs):
    lo_send, lo_keep, hi_send, hi_keep = refs[-4:]
    i = pl.program_id(0)
    total = (mine[...].astype(f32) + theirs[...].astype(f32)).astype(bf16)
    lo, hi = total[None, :, :, :cut], total[None, :, :, cut:]

    @pl.when(i < 2)
    def _():
        lo_send[...] = lo

    @pl.when(i >= 2)
    def _():
        lo_keep[...] = lo

    @pl.when((i == 1) | (i == 2))
    def _():
        hi_send[...] = hi

    @pl.when((i == 0) | (i == 3))
    def _():
        hi_keep[...] = hi


def fold(place, mine, theirs, hold):
    parts, rows, wide = mine.shape
    size = rows // 4
    cut = (wide // 256) * 128 if wide % 256 == 0 else (wide // 256 + 1) * 128
    block = pl.BlockSpec(
        (parts, size, wide),
        lambda i, sc: (
            0,
            sc[1] ^ jnp.where(i == 0, 1, jnp.where(i == 1, 3, jnp.where(i == 2, 2, 0))),
            0,
        ),
    )
    out = lambda width, index: pl.BlockSpec(
        (1, parts, size, width), lambda i, sc: (index(i), 0, 0, 0)
    )
    lo, hi = cut, wide - cut
    return pl.pallas_call(
        functools.partial(fold_kernel, cut),
        grid_spec=pltpu.PrefetchScalarGridSpec(
            num_scalar_prefetch=1,
            grid=(4,),
            in_specs=[block, block] + [HBM] * len(hold),
            out_specs=[
                out(lo, lambda i: jnp.minimum(i, 1)),
                out(lo, lambda i: jnp.where(i == 3, 0, 1)),
                out(hi, lambda i: jnp.where(i < 2, 1, 0)),
                out(hi, lambda i: jnp.where(i == 3, 0, 1)),
            ],
        ),
        out_shape=[
            shape((2, parts, size, lo)),
            shape((2, parts, size, lo)),
            shape((2, parts, size, hi)),
            shape((2, parts, size, hi)),
        ],
        compiler_params=params(),
        cost_estimate=cost(1 + 6 * parts / 4),
        name="fold",
    )(place, mine, theirs, *hold)


def body(
    n_shard,
    n_context,
    n_tensor,
    inputs,
    segments,
    w_qkv,
    w_out,
    w_fc,
    w_down,
    b_qv,
    b_out,
    b_fc,
    b_down,
    first_norm_gain,
    first_norm_bias,
    second_norm_gain,
    second_norm_bias,
    cotangent,
):
    _, tok, width = inputs.shape
    length = segments.shape[1]
    half, _, cols = w_qkv.shape
    heads = cols // HD
    ffw = w_fc.shape[1]
    sub = tok // n_tensor
    context = lax.axis_index("context")
    tensor = lax.axis_index("tensor")
    core = lax.axis_index("shard")
    first = context * tok
    place = jnp.stack([first, context, core, tensor]).astype(jnp.int32)
    grouped = n_context == 4
    x = inputs[0]
    cot = cotangent[0]
    row = lambda v: v[None, :]
    zero = jnp.zeros_like(b_out)
    table = jnp.concatenate(
        [
            first_norm_gain,
            first_norm_bias,
            b_out,
            b_down,
            second_norm_gain,
            second_norm_bias,
            zero,
            zero,
        ]
    ).reshape(8, width)
    after = lambda v, dep: lax.optimization_barrier((v, dep))[0]

    swap = lambda v: lax.ppermute(v, "shard", [(0, 1), (1, 0)])
    along_x = lambda v: lax.ppermute(v, "context", [(0, 1), (1, 0), (2, 3), (3, 2)])
    along_y = lambda v: lax.ppermute(v, "context", [(0, 2), (2, 0), (1, 3), (3, 1)])
    shift_by = lambda v, d: lax.ppermute(
        v, "tensor", [(s, (s + d) % n_tensor) for s in range(n_tensor)]
    )

    def gather_direct(v):
        return [v] + [shift_by(v, d) for d in range(1, n_tensor)]

    def gather_begin(v):
        if n_tensor != 4:
            return tuple(gather_direct(v))
        move = lambda perm: lax.ppermute(v, "tensor", perm)
        return (
            v,
            move([(0, 2), (1, 3), (2, 0), (3, 1)]),
            move([(0, 1), (1, 2), (2, 3)]),
            move([(3, 2), (2, 1), (1, 0)]),
        )

    def gather_end(state, hold=()):
        if n_tensor != 4:
            return list(state)
        v, two, right, left = state
        two = after(two, hold)
        far = lax.ppermute(two, "tensor", [(2, 3), (1, 0)])
        return [
            v,
            jnp.where(tensor == 0, far, right),
            two,
            jnp.where(tensor == 3, far, left),
        ]

    def scatter_line(pieces):
        if n_tensor != 4:
            total = pieces[0].astype(f32)
            for d in range(1, n_tensor):
                total += shift_by(pieces[d].astype(bf16), -d).astype(f32)
            return total
        move = lambda a, perm: lax.ppermute(a.astype(bf16), "tensor", perm)
        far = move(jnp.where(tensor == 0, pieces[1], pieces[3]), [(0, 1), (3, 2)])
        right = move(pieces[3], [(0, 1), (1, 2), (2, 3)])
        left = move(pieces[1], [(3, 2), (2, 1), (1, 0)])
        two = move(
            pieces[2].astype(f32) + far.astype(f32), [(0, 2), (1, 3), (2, 0), (3, 1)]
        )
        return (
            pieces[0].astype(f32) + right.astype(f32) + left.astype(f32) + two.astype(f32)
        )

    def scatter_begin(mine, theirs, hold=()):
        theirs = swap(theirs)
        if not grouped:
            both = (mine.astype(f32) + theirs.astype(f32)).astype(bf16)
            return lax.psum_scatter(both, "context", scatter_dimension=1, tiled=True)
        return fold(place, mine, theirs, hold)

    def scatter_first(state):
        if not grouped:
            return state
        lo_send, lo_keep, hi_send, hi_keep = state
        r, s = along_x(lo_send).astype(f32), along_y(hi_send).astype(f32)
        return (
            lo_keep[0].astype(f32) + r[0],
            hi_keep[0].astype(f32) + s[0],
            (lo_keep[1].astype(f32) + r[1]).astype(bf16),
            (hi_keep[1].astype(f32) + s[1]).astype(bf16),
        )

    def scatter_second(state):
        if not grouped:
            return state
        lo, hi, lo_send, hi_send = state
        lo += along_y(lo_send).astype(f32)
        hi += along_x(hi_send).astype(f32)
        return jnp.concatenate([lo, hi], axis=2)

    bounds = [jnp.sum((segments[0] < d).astype(jnp.int32)) for d in range(1, 5)]
    seg = lax.dynamic_slice_in_dim(segments[0], first, tok, 0)
    starts = jnp.zeros_like(seg)
    for d in range(1, 5):
        starts = jnp.where(seg == d, bounds[d - 1], starts)

    def scalars(bk, bq):
        count = tok // bq
        begin = starts.reshape(count, bq)
        base = first + jnp.arange(count, dtype=jnp.int32) * bq
        lo = begin[:, 0] // bk
        diag = base // bk
        end = (base + bq + bk - 1) // bk
        full = jnp.minimum(jnp.maximum((begin[:, -1] + bk - 1) // bk, lo), diag)
        table = jnp.stack([lo, full, diag, end], axis=1).reshape(-1)
        return jnp.concatenate([place, table.astype(jnp.int32)])

    qkv_own = w_qkv.reshape(half, 3 * cols)
    low_one, qt, kt, vt = project(
        place,
        x,
        qkv_own,
        swap(qkv_own),
        b_qv,
        table,
    )

    terms, rest = [], b_fc
    for _ in range(3):
        term = lax.reduce_precision(rest, 8, 7)
        terms.append(term.astype(bf16).reshape(ffw // half, half))
        rest = rest - term
    terms = jnp.concatenate(terms, axis=0)
    terms = jnp.pad(terms, ((0, 16 - terms.shape[0]), (0, 0)))
    packed = jnp.concatenate([w_out, terms, w_fc[:, :half], w_fc[:, half:]], axis=0)
    packed = gather_begin(packed)
    kv = []
    hold = ()
    head = 0
    for g in GROUPS:
        rows = slice(head * HD, (head + g) * HD)
        head += g
        k, v = kt[rows], vt[rows]
        if grouped:
            kx, vy = along_x(k), along_y(v)
            k_two, v_two = jnp.stack([k, kx]), jnp.stack([v, vy])
            k_two, v_two = after((k_two, v_two), packed[1:])
            k_yd, v_xd = along_y(k_two), along_x(v_two)
            hold = (k_two, v_two)
            kv.append([k, kx, k_yd, v, vy, v_xd])
        else:
            kv.append([lax.all_gather(jnp.concatenate([k, v], axis=0), "context", axis=0)])

    dn = gather_begin(after(w_down, packed[1]))
    saved = []
    att = [[] for _ in range(n_tensor)]
    head = 0
    for g, held in zip(GROUPS, kv):
        results = attend(scalars, row(starts), after(qt, packed[1:]), held, head, g, BK_F, BQ_F, n_tensor)
        lse, ot, *out = results
        saved.append((lse, ot))
        att[0].append(out[0])
        for d in range(1, n_tensor):
            att[d].append(shift_by(out[d], d))
        head += g

    of = jnp.stack(after(gather_end(packed, hold), att[1:]))
    of = (of, swap(of))
    dn = jnp.stack(gather_end(dn, att[1:]))
    dn = (dn, swap(dn))
    x_sub = lax.dynamic_slice_in_dim(x, tensor * sub, sub, 0)
    cot_sub = lax.dynamic_slice_in_dim(cot, tensor * sub, sub, 0)
    outputs_sub, grad_mid, mid_sums, fc_sums, *rest = middle(
        place,
        [piece for part in att for piece in part],
        x_sub,
        cot_sub,
        of,
        dn,
        cols,
        table,
    )
    d_att, (g_own, g_other) = rest[:n_tensor], rest[n_tensor:]
    do_parts = [d_att[0]] + [
        shift_by(d_att[d], -d) for d in range(1, n_tensor)
    ]

    def spread(pieces):
        whole = jnp.zeros((tok, width), f32)
        for d in range(n_tensor):
            at = lax.rem(tensor - d + n_tensor, n_tensor) * sub
            whole = lax.dynamic_update_slice_in_dim(whole, pieces[d].astype(f32), at, 0)
        return whole[None]


    qkv_wide = jnp.pad(qkv_own, ((0, 0), (0, width - 3 * cols)))
    carried = jnp.concatenate([outputs_sub, qkv_wide], axis=0)

    head = 0
    queries, keys, values = [], [], []
    sent = [[] for _ in range(n_tensor)]
    for g, held, (lse, ot) in zip(GROUPS, kv, saved):
        out = attend_back(
            scalars, row(starts), qt, lse, ot, do_parts, held, carried, head, g, BK_B, BQ_B
        )
        *out, carried = out
        dq, dkv = out[:n_tensor], out[n_tensor:]
        if grouped:
            dk_keep, dk_send, dv_keep, dv_send = dkv
            r, s = along_x(dk_send), along_y(dv_send)
            hold = (r, s)
            r, s = r.astype(f32), s.astype(f32)
            r2 = along_y((dk_keep[1].astype(f32) + r[1]).astype(bf16)).astype(f32)
            s2 = along_x((dv_keep[1].astype(f32) + s[1]).astype(bf16)).astype(f32)
            dk = (dk_keep[0].astype(f32) + r[0] + r2).astype(bf16)
            dv = (dv_keep[0].astype(f32) + s[0] + s2).astype(bf16)
        else:
            both = lax.psum_scatter(dkv[0], "context", scatter_dimension=0, tiled=True)[0]
            dk, dv = both[: g * HD], both[g * HD :]
        queries.append(dq)
        keys.append(dk)
        values.append(dv)
        head += g

    folded = scatter_begin(g_own, g_other, hold)
    wide = scatter_first(folded)
    both_sends = after(jnp.concatenate(keys + values, axis=0), wide[2:] if grouped else wide)
    wide = scatter_second(wide)
    wide_grads = scatter_line([wide[d] for d in range(n_tensor)])

    def part_of(v, d):
        at = lax.rem(tensor + d, n_tensor) * sub
        return lax.dynamic_slice_in_dim(v, at, sub, 1)

    grads = []
    both = jnp.concatenate(keys + values, axis=0)
    for d in range(n_tensor):
        piece = jnp.concatenate([q[d] for q in queries] + [part_of(both_sends, d)], axis=0)
        grads.append(shift_by(piece, d) if d else piece)
    pieces = 1

    dq_whole = []
    for q in queries:
        whole = jnp.zeros((q[0].shape[0], tok), bf16)
        for d in range(n_tensor):
            at = lax.rem(tensor + d, n_tensor) * sub
            whole = lax.dynamic_update_slice_in_dim(whole, q[d], at, 1)
        dq_whole.append(whole)
    outputs_and_qkv = lax.all_gather(carried, "tensor", axis=0)
    outputs = outputs_and_qkv[:, :sub].reshape(tok, width)
    qkv = outputs_and_qkv[:, sub:]
    qkv = (qkv, swap(qkv))
    stacked = jnp.concatenate(
        dq_whole + [both, jnp.zeros((-3 * cols % 128, tok), bf16)], axis=0
    )
    qkv_grad = jnp.einsum(
        "td,ct->dc", low_one, stacked, preferred_element_type=f32
    ).astype(bf16)
    qkv_mine = lax.dynamic_slice_in_dim(qkv_grad, core * half, half, 0)
    qkv_theirs = lax.dynamic_slice_in_dim(qkv_grad, (1 - core) * half, half, 0)
    qkv_folded = scatter_begin(qkv_mine[None], qkv_theirs[None])

    input_sub, small = last(
        place, grads, pieces, qkv, x_sub, after(grad_mid, qkv_folded), table, mid_sums, fc_sums
    )
    input_gradient = spread(gather_direct(input_sub))
    outputs = after(outputs, input_sub).astype(f32)[None]
    qkv_grads = scatter_second(scatter_first(qkv_folded))[0]

    if grouped and n_tensor == 4 and n_shard == 2:
        small += swap(small)
        small += along_x(small)
        small += along_y(small)
        small += lax.ppermute(small, "tensor", [(0, 1), (1, 0), (2, 3), (3, 2)])
        small += lax.ppermute(small, "tensor", [(0, 2), (2, 0), (1, 3), (3, 1)])
    else:
        small = lax.psum(small, ("shard", "context", "tensor"))
    fc_total = lax.dynamic_index_in_dim(small, 6 + tensor, 0, keepdims=False)
    qv_total = lax.dynamic_index_in_dim(small, 6 + n_tensor + tensor, 0, keepdims=False)
    qv_total = jnp.stack([qv_total[:cols], qv_total[2 * cols : 3 * cols]])
    return (
        outputs,
        input_gradient,
        qkv_grads[:, : 3 * cols].astype(f32).reshape(-1, 3, cols),
        wide_grads[:, 2 * ffw : 2 * ffw + cols].T,
        wide_grads[:, :ffw],
        wide_grads[:, ffw : 2 * ffw].T,
        qv_total,
        small[0],
        fc_total,
        small[1],
        small[4],
        small[5],
        small[2],
        small[3],
    )


def solution(mesh):
    sizes = dict(mesh.shape)
    placed = (
        P("shard", "context", None),
        P("shard", None),
        P("shard", None, "tensor"),
        P("tensor", "shard"),
        P("shard", "tensor"),
        P("tensor", "shard"),
        P(None, "tensor"),
        P(),
        P("tensor"),
        P(),
        P(),
        P(),
        P(),
        P(),
        P("shard", "context", None),
    )
    return jax.shard_map(
        functools.partial(body, sizes["shard"], sizes["context"], sizes["tensor"]),
        mesh=mesh,
        in_specs=placed,
        out_specs=(
            P("shard", "context", None),
            P("shard", "context", None),
            P(("shard", "context"), None, "tensor"),
            P("tensor", ("shard", "context")),
            P(("shard", "context"), "tensor"),
            P("tensor", ("shard", "context")),
            P(None, "tensor"),
            P(),
            P("tensor"),
            P(),
            P(),
            P(),
            P(),
            P(),
        ),
        check_vma=False,
    )
```

```python
import functools

import jax
import jax.numpy as jnp
from jax import lax
from jax.experimental import pallas as pl
from jax.experimental.pallas import tpu as pltpu
from jax.sharding import PartitionSpec as P

HD = 64
EPS = 1e-05
NEG = -1e30
SCALE = float(HD) ** -0.5
VMEM_LIMIT = 56 * 1024 * 1024
GROUPS = (3,)
BK_F, BQ_F = 512, 512
BK_B, BQ_B = 512, 512
f32 = jnp.float32
bf16 = jnp.bfloat16
VM = pl.BlockSpec(memory_space=pltpu.VMEM)
SM = pl.BlockSpec(memory_space=pltpu.SMEM)
HBM = pl.BlockSpec(memory_space=pl.ANY)


def nn(a, b):
    return lax.dot_general(a, b, (((1,), (0,)), ((), ())), preferred_element_type=f32)


def tn(a, b):
    return lax.dot_general(a, b, (((0,), (0,)), ((), ())), preferred_element_type=f32)


def nt(a, b):
    return lax.dot_general(a, b, (((1,), (1,)), ((), ())), preferred_element_type=f32)


def params():
    return pltpu.CompilerParams(vmem_limit_bytes=VMEM_LIMIT)


def cost(microseconds):
    return pl.CostEstimate(
        flops=int(microseconds * 1.15e9), bytes_accessed=1 << 20, transcendentals=0
    )


def shape(dims, kind=bf16):
    return jax.ShapeDtypeStruct(dims, kind)


def halves(core, width):
    half = width // 2
    own = pl.ds(pl.multiple_of(core * half, 128), half)
    other = pl.ds(pl.multiple_of((1 - core) * half, 128), half)
    return own, other


def norm(value):
    centred = value - jnp.mean(value, axis=-1, keepdims=True)
    inverse = lax.rsqrt(jnp.mean(centred * centred, axis=-1, keepdims=True) + EPS)
    return centred * inverse, inverse


def norm_gradient(grad, normed, inverse, gain):
    scaled = grad * gain
    return inverse * (
        scaled
        - jnp.mean(scaled, axis=-1, keepdims=True)
        - normed * jnp.mean(scaled * normed, axis=-1, keepdims=True)
    )


def project_kernel(sc, x, w_own, w_other, b_qv, rows, low, qt, kt, vt):
    own, other = halves(sc[2], x.shape[1])
    cols = qt.shape[0]
    normed, _ = norm(x[...].astype(f32))
    low[...] = (normed * rows[0:1, :] + rows[1:2, :]).astype(bf16)
    projected = nn(low[:, own], w_own[...]) + nn(low[:, other], w_other[...])
    qt[...] = ((projected[:, :cols] + b_qv[0:1, :]) * SCALE).T.astype(bf16)
    kt[...] = projected[:, cols : 2 * cols].T.astype(bf16)
    vt[...] = (projected[:, 2 * cols :] + b_qv[1:2, :]).T.astype(bf16)


def project(place, x, w_own, w_other, b_qv, table):
    tok, width = x.shape
    cols = b_qv.shape[1]
    rows = min(256, tok)
    fixed = lambda a: pl.BlockSpec(a.shape, lambda i: (0,) * a.ndim)
    across = pl.BlockSpec((cols, rows), lambda i: (0, i))
    return pl.pallas_call(
        project_kernel,
        grid=(tok // rows,),
        in_specs=[SM, pl.BlockSpec((rows, width), lambda i: (i, 0))]
        + [fixed(a) for a in (w_own, w_other, b_qv, table)],
        out_specs=[pl.BlockSpec((rows, width), lambda i: (i, 0)), across, across, across],
        out_shape=[shape((tok, width))] + [shape((cols, tok))] * 3,
        compiler_params=params(),
        cost_estimate=cost(7),
        name="project",
    )(place, x, w_own, w_other, b_qv, table)


def key_loop(sc, i, step, carry):
    lo, full, diag, end = sc[4 * i + 4], sc[4 * i + 5], sc[4 * i + 6], sc[4 * i + 7]
    carry = lax.fori_loop(lo, full, functools.partial(step, True), carry)
    carry = lax.fori_loop(full, diag, functools.partial(step, False), carry)
    return lax.fori_loop(diag, end, functools.partial(step, True), carry)


def tile_mask(j, bk, bq, start, qpos):
    kpos = j * bk + lax.broadcasted_iota(jnp.int32, (bk, bq), 0)
    return (kpos >= start) & (kpos <= qpos)


def load_keys(sc, kv, held, sems):
    if len(kv) == 1:
        copies = [pltpu.make_async_copy(kv[0], held, sems.at[0])]
    else:
        k, k_x, k_yd, v, v_y, v_xd = kv
        rows = k.shape[0]
        pieces = [(k, 0, 0), (k_x, 0, 1), (k_yd.at[0], 0, 2), (k_yd.at[1], 0, 3)]
        pieces += [(v, 1, 0), (v_y, 1, 2), (v_xd.at[0], 1, 1), (v_xd.at[1], 1, 3)]
        copies = [
            pltpu.make_async_copy(
                piece, held.at[sc[1] ^ run, pl.ds(which * rows, rows), :], sems.at[n]
            )
            for n, (piece, which, run) in enumerate(pieces)
        ]
    for copy in copies:
        copy.start()
    for copy in copies:
        copy.wait()


def attend_kernel(first_head, heads, bk, bq, parts, n_kv, sc, qt, st, *refs):
    kv, refs = refs[:n_kv], refs[n_kv:]
    lse, ot, out, (held, acc, sems) = refs[0], refs[1], refs[2 : 2 + parts], refs[2 + parts :]
    i = pl.program_id(0)
    per = held.shape[2] // bk
    cols = heads * HD
    start = st[...]
    qpos = sc[0] + i * bq + lax.broadcasted_iota(jnp.int32, (1, bq), 1)

    @pl.when(i == 0)
    def _():
        load_keys(sc, kv, held, sems)

    acc[...] = jnp.zeros_like(acc)

    def step(masked, j, carry):
        r = j // per
        off = pl.multiple_of((j % per) * bk, bk)
        new = []
        if masked:
            ok = tile_mask(j, bk, bq, start, qpos)
        for h in range(heads):
            m, l = carry[h]
            hs = slice(h * HD, (h + 1) * HD)
            s = tn(
                held[r, hs, pl.ds(off, bk)],
                qt[(first_head + h) * HD : (first_head + h + 1) * HD, :],
            )
            if masked:
                s = jnp.where(ok, s, NEG)
            m2 = jnp.maximum(m, jnp.max(s, axis=0, keepdims=True))
            p = jnp.exp(s - m2)
            al = jnp.exp(m - m2)
            l = l * al + jnp.sum(p, axis=0, keepdims=True)
            v = held[r, cols + h * HD : cols + (h + 1) * HD, pl.ds(off, bk)]
            acc[hs, :] = acc[hs, :] * al + nn(v, p.astype(bf16))
            new.append((m2, l))
        return tuple(new)

    one = (jnp.full((1, bq), NEG, f32), jnp.zeros((1, bq), f32))
    res = key_loop(sc, i, step, (one,) * heads)
    here = pl.ds(pl.multiple_of(i * bq, bq), bq)
    for h in range(heads):
        m, l = res[h]
        ot[h * HD : (h + 1) * HD, here] = (acc[h * HD : (h + 1) * HD, :] / l).astype(bf16)
        lse[h : h + 1, :] = m + jnp.log(l)

    @pl.when(i == pl.num_programs(0) - 1)
    def _():
        send_parts(sc[3], ot, out)


def send_parts(me, source, out):
    parts, size = len(out), out[0].shape[1]
    for d in range(parts):
        if size % 128 == 0:
            at = pl.multiple_of(lax.rem(me + d, parts) * size, 128)
            out[d][...] = source[:, pl.ds(at, size)].astype(out[d].dtype)
        else:
            for n in range(parts):

                @pl.when(lax.rem(me + d, parts) == n)
                def _():
                    out[d][...] = source[:, n * size : (n + 1) * size].astype(out[d].dtype)


def take_parts(me, rows, parts, target):
    size = parts[0].shape[1]
    for d in range(len(parts)):
        if size % 128 == 0:
            at = pl.multiple_of(lax.rem(me + d, len(parts)) * size, 128)
            target[:, pl.ds(at, size)] = parts[d][rows, :]
        else:
            for n in range(len(parts)):

                @pl.when(lax.rem(me + d, len(parts)) == n)
                def _():
                    target[:, n * size : (n + 1) * size] = parts[d][rows, :]


def attend(scalars, starts, qt, kv, first_head, heads, bk, bq, parts):
    tok = qt.shape[1]
    cols = heads * HD
    runs = kv[0].shape[0] if len(kv) == 1 else 4
    bk, bq = min(bk, tok), min(bq, tok)
    whole = lambda a, b: pl.BlockSpec((a, b), lambda i: (0, 0))
    return pl.pallas_call(
        functools.partial(attend_kernel, first_head, heads, bk, bq, parts, len(kv)),
        grid=(tok // bq,),
        in_specs=[
            SM,
            pl.BlockSpec((qt.shape[0], bq), lambda i: (0, i)),
            pl.BlockSpec((1, bq), lambda i: (0, i)),
        ]
        + [HBM] * len(kv),
        out_specs=[pl.BlockSpec((heads, bq), lambda i: (0, i)), whole(cols, tok)]
        + [whole(cols, tok // parts)] * parts,
        scratch_shapes=[
            pltpu.VMEM((runs, 2 * cols, tok), bf16),
            pltpu.VMEM((cols, bq), f32),
            pltpu.SemaphoreType.DMA((8,)),
        ],
        out_shape=[shape((heads, tok), f32), shape((cols, tok))]
        + [shape((cols, tok // parts))] * parts,
        compiler_params=params(),
        cost_estimate=cost(20),
        name="attend",
    )(scalars(bk, bq), qt, starts, *kv)


def attend_back_kernel(first_head, heads, bk, bq, parts, n_kv, sc, qt, st, lse, ot, *refs):
    do_parts, refs = refs[:parts], refs[parts:]
    kv, refs = refs[:n_kv], refs[n_kv + 1 :]
    n_out = 1 if n_kv == 1 else 4
    dq, dkv, (held, acc, dqa, do_all, sems) = (
        refs[:parts],
        refs[parts : parts + n_out],
        refs[parts + n_out + 1 :],
    )
    i = pl.program_id(0)
    per = held.shape[2] // bk
    cols = heads * HD
    start = st[...]
    qpos = sc[0] + i * bq + lax.broadcasted_iota(jnp.int32, (1, bq), 1)
    here = pl.ds(pl.multiple_of(i * bq, bq), bq)

    @pl.when(i == 0)
    def _():
        acc[...] = jnp.zeros_like(acc)
        dqa[...] = jnp.zeros_like(dqa)
        take_parts(sc[3], slice(first_head * HD, (first_head + heads) * HD), do_parts, do_all)
        load_keys(sc, kv, held, sems)

    delta = [
        jnp.sum(
            do_all[h * HD : (h + 1) * HD, here].astype(f32)
            * ot[h * HD : (h + 1) * HD, :].astype(f32),
            axis=0,
            keepdims=True,
        )
        for h in range(heads)
    ]

    def step(masked, j, carry):
        r = j // per
        off = pl.multiple_of((j % per) * bk, bk)
        if masked:
            ok = tile_mask(j, bk, bq, start, qpos)
        for h in range(heads):
            hs = slice(h * HD, (h + 1) * HD)
            vs = slice(cols + h * HD, cols + (h + 1) * HD)
            k = held[r, hs, pl.ds(off, bk)]
            v = held[r, vs, pl.ds(off, bk)]
            q = qt[(first_head + h) * HD : (first_head + h + 1) * HD, :]
            do = do_all[hs, here]
            s = tn(k, q) - lse[h : h + 1, :]
            if masked:
                s = jnp.where(ok, s, NEG)
            p = jnp.exp(s)
            ds = (p * (tn(v, do) - delta[h])).astype(bf16)
            acc[r, vs, pl.ds(off, bk)] += nt(do, p.astype(bf16))
            acc[r, hs, pl.ds(off, bk)] += nt(q, ds)
            dqa[hs, here] += nn(k, ds)
        return carry

    key_loop(sc, i, step, 0)

    @pl.when(i == pl.num_programs(0) - 1)
    def _():
        dqa[...] = dqa[...] * SCALE
        send_parts(sc[3], dqa, dq)
        if n_out == 1:
            dkv[0][...] = acc[...].astype(bf16)
        else:
            for target, pair, rows in (
                (0, (0, 2), slice(0, cols)),
                (1, (1, 3), slice(0, cols)),
                (2, (0, 1), slice(cols, 2 * cols)),
                (3, (2, 3), slice(cols, 2 * cols)),
            ):
                for n in range(2):
                    dkv[target][n] = acc[sc[1] ^ pair[n], rows, :].astype(bf16)


def attend_back(scalars, starts, qt, lse, ot, do_parts, kv, carried, first_head, heads, bk, bq):
    tok = qt.shape[1]
    cols = heads * HD
    parts = len(do_parts)
    runs = kv[0].shape[0] if len(kv) == 1 else 4
    bk, bq = min(bk, tok), min(bq, tok)
    whole = lambda *dims: pl.BlockSpec(dims, lambda i: (0,) * len(dims))
    out_kv = [(runs, 2 * cols, tok)] if len(kv) == 1 else [(2, cols, tok)] * 4
    return pl.pallas_call(
        functools.partial(attend_back_kernel, first_head, heads, bk, bq, parts, len(kv)),
        grid=(tok // bq,),
        in_specs=[
            SM,
            pl.BlockSpec((qt.shape[0], bq), lambda i: (0, i)),
            pl.BlockSpec((1, bq), lambda i: (0, i)),
            pl.BlockSpec((heads, bq), lambda i: (0, i)),
            pl.BlockSpec((cols, bq), lambda i: (0, i)),
        ]
        + [whole(*d.shape) for d in do_parts]
        + [HBM] * (len(kv) + 1),
        out_specs=[whole(cols, tok // parts)] * parts + [whole(*d) for d in out_kv] + [HBM],
        scratch_shapes=[
            pltpu.VMEM((runs, 2 * cols, tok), bf16),
            pltpu.VMEM((runs, 2 * cols, tok), f32),
            pltpu.VMEM((cols, tok), f32),
            pltpu.VMEM((cols, tok), bf16),
            pltpu.SemaphoreType.DMA((8,)),
        ],
        out_shape=[shape((cols, tok // parts))] * parts
        + [shape(d) for d in out_kv]
        + [shape(carried.shape)],
        input_output_aliases={5 + parts + len(kv): parts + len(out_kv)},
        compiler_params=params(),
        cost_estimate=cost(26),
        name="attend_back",
    )(scalars(bk, bq), qt, starts, lse, ot, *do_parts, *kv, carried)


ROOT = 0.7978845608028654


def middle_kernel(n_att, parts, sc, *refs):
    att, refs = refs[:n_att], refs[n_att:]
    x, cot, of_own, of_other, dn_own, dn_other, rows = refs[:7]
    refs = refs[7:]
    outputs, grad_mid, sums, fc_sums = refs[:4]
    d_att, (g_own, g_other) = refs[4 : 4 + parts], refs[4 + parts : 6 + parts]
    mid, att_t, low, low_t, cot_t, mlp, back = refs[6 + parts :]
    d = pl.program_id(0)
    width = x.shape[1]
    own, other = halves(sc[2], width)
    half = width // 2
    ffw = dn_own.shape[1]
    count = ffw // half
    cols = att_t.shape[0] // parts
    b_out, b_down, gain, shift = (rows[n : n + 1, :] for n in range(2, 6))

    @pl.when(d == 0)
    def _():
        group = n_att // parts
        row = 0
        for part in range(parts):
            for g in range(group):
                piece = att[part * group + g]
                att_t[row : row + piece.shape[0], :] = piece[...]
                row += piece.shape[0]
        att_low = att_t[...].T
        mine = theirs = 0.0
        for part in range(parts):
            piece = att_low[:, part * cols : (part + 1) * cols]
            mine += nn(piece, of_own[part, :cols, :])
            theirs += nn(piece, of_other[part, :cols, :])
        mid[:, own] = mine
        mid[:, other] = theirs
        mid[...] = x[...].astype(f32) + mid[...] + b_out
        normed, _ = norm(mid[...])
        low[...] = (normed * gain + shift).astype(bf16)
        low_t[...] = low[...].T
        cot_t[...] = cot[...].T
        mlp[...] = jnp.zeros_like(mlp)
        back[...] = jnp.zeros_like(back)

    own_rows = pl.ds(pl.multiple_of(sc[2] * half, half), half)
    other_rows = pl.ds(pl.multiple_of((1 - sc[2]) * half, half), half)
    terms = of_own[d, cols : cols + 16, :].astype(f32)
    pieces = [slice(cols + 16 + n * half, cols + 16 + (n + 1) * half) for n in range(count)]
    u = [
        nn(low[:, own], of_own[d, at, :])
        + nn(low[:, other], of_other[d, at, :])
        + sum(terms[t * count + n : t * count + n + 1, :] for t in range(3))
        for n, at in enumerate(pieces)
    ]
    u = jnp.concatenate(u, axis=1)
    t = jnp.tanh(ROOT * (u + 0.044715 * (u * u * u)))
    act = (0.5 * u * (1.0 + t)).astype(bf16)
    slope = 0.5 * (1.0 + t) + (0.5 * ROOT) * u * (1.0 - t * t) * (1.0 + 0.134145 * (u * u))
    d_act = nt(cot[:, own], dn_own[0]) + nt(cot[:, other], dn_other[0])
    dh = (d_act * slope).astype(bf16)
    mlp[:, own] += nn(act, dn_own[0])
    mlp[:, other] += nn(act, dn_other[0])
    for n, at in enumerate(pieces):
        dh_n = dh[:, n * half : (n + 1) * half]
        back[:, own] += nt(dh_n, of_own[d, at, :])
        back[:, other] += nt(dh_n, of_other[d, at, :])
    g_own[d, :, :ffw] = nn(low_t[own_rows, :], dh).astype(bf16)
    g_other[d, :, :ffw] = nn(low_t[other_rows, :], dh).astype(bf16)
    g_own[d, :, ffw : 2 * ffw] = nn(cot_t[own_rows, :], act).astype(bf16)
    g_other[d, :, ffw : 2 * ffw] = nn(cot_t[other_rows, :], act).astype(bf16)
    fc_sums[lax.rem(sc[3] - d + parts, parts)] = jnp.sum(dh.astype(f32), axis=0, keepdims=True)

    @pl.when(d == parts - 1)
    def _():
        normed, inverse = norm(mid[...])
        outputs[...] = (mid[...] + mlp[...] + b_down).astype(bf16)
        upper = cot[...].astype(f32)
        grad = back[...]
        down = upper + norm_gradient(grad, normed, inverse, gain)
        grad_mid[...] = down
        sums[0:1, :] = jnp.sum(down, axis=0, keepdims=True)
        sums[1:2, :] = jnp.sum(upper, axis=0, keepdims=True)
        sums[2:3, :] = jnp.sum(grad * normed, axis=0, keepdims=True)
        sums[3:4, :] = jnp.sum(grad, axis=0, keepdims=True)
        low[...] = down.astype(bf16)
        low_t[...] = low[...].T
        g_own[:, :, 2 * ffw + cols :] = jnp.zeros_like(g_own[:, :, 2 * ffw + cols :])
        g_other[:, :, 2 * ffw + cols :] = jnp.zeros_like(g_other[:, :, 2 * ffw + cols :])
        for part in range(parts):
            at = slice(part * cols, (part + 1) * cols)
            g_own[part, :, 2 * ffw : 2 * ffw + cols] = nt(low_t[own_rows, :], att_t[at, :]).astype(bf16)
            g_other[part, :, 2 * ffw : 2 * ffw + cols] = nt(low_t[other_rows, :], att_t[at, :]).astype(bf16)
            d_att[part][...] = (
                nt(of_own[part, :cols, :], low[:, own]) + nt(of_other[part, :cols, :], low[:, other])
            ).astype(bf16)


def middle(place, att, x, cot, of, dn, cols, table):
    parts, ffw, half = dn[0].shape
    sub, width = x.shape
    whole = lambda *dims: pl.BlockSpec(
        dims, lambda i, sc: (0,) * len(dims), pipeline_mode=pl.Buffered(1)
    )
    placed = pl.BlockSpec(
        (1, ffw, half), lambda i, sc: (i, 0, 0)
    )
    once = lambda a: whole(*a.shape)
    grads = (parts, half, 128 * ((2 * ffw + cols + 127) // 128))
    return pl.pallas_call(
        functools.partial(middle_kernel, len(att), parts),
        grid_spec=pltpu.PrefetchScalarGridSpec(
            num_scalar_prefetch=1,
            grid=(parts,),
            in_specs=[once(a) for a in att]
            + [once(x), once(cot), once(of[0]), once(of[1]), placed, placed, once(table)],
            out_specs=[whole(sub, width), whole(sub, width), whole(4, width), whole(parts, 1, ffw)]
            + [whole(cols, sub)] * parts
            + [whole(*grads)] * 2,
            scratch_shapes=[
                pltpu.VMEM((sub, width), f32),
                pltpu.VMEM((parts * cols, sub), bf16),
                pltpu.VMEM((sub, width), bf16),
                pltpu.VMEM((width, sub), bf16),
                pltpu.VMEM((width, sub), bf16),
                pltpu.VMEM((sub, width), f32),
                pltpu.VMEM((sub, width), f32),
            ],
        ),
        out_shape=[
            shape((sub, width)),
            shape((sub, width), f32),
            shape((4, width), f32),
            shape((parts, 1, ffw), f32),
        ]
        + [shape((cols, sub))] * parts
        + [shape(grads)] * 2,
        compiler_params=params(),
        cost_estimate=cost(19),
        name="middle",
    )(place, *att, x, cot, of[0], of[1], dn[0], dn[1], table)


def last_kernel(parts, pieces, sc, *refs):
    grads, refs = refs[: parts * pieces], refs[parts * pieces :]
    w_own, w_other, x, grad_mid, rows, mid_sums, fc_sums, out, sums, back_t, stacked = refs
    half = w_own.shape[1]
    wide = w_own.shape[2]
    own_rows = pl.ds(pl.multiple_of(sc[2] * half, half), half)
    other_rows = pl.ds(pl.multiple_of((1 - sc[2]) * half, half), half)
    ones = jnp.ones((8, x.shape[0]), bf16)
    sums[...] = jnp.zeros_like(sums)
    stacked[...] = jnp.zeros_like(stacked)
    for part in range(parts):
        row = 0
        for n in range(pieces):
            piece = grads[part * pieces + n]
            stacked[row : row + piece.shape[0], :] = piece[...]
            row += piece.shape[0]
        at = lax.rem(sc[3] - part + parts, parts)
        mine, theirs = nn(w_own[at], stacked[...]), nn(w_other[at], stacked[...])
        if part == 0:
            back_t[own_rows, :], back_t[other_rows, :] = mine, theirs
        else:
            back_t[own_rows, :] += mine
            back_t[other_rows, :] += theirs
        sums[pl.ds(6 + parts + at, 1), :wide] = nt(ones, stacked[...])[0:1, :]
    back = back_t[...].T
    normed, inverse = norm(x[...].astype(f32))
    out[...] = (grad_mid[...] + norm_gradient(back, normed, inverse, rows[0:1, :])).astype(bf16)
    sums[0:4, :] = mid_sums[...]
    sums[4:5, :] = jnp.sum(back * normed, axis=0, keepdims=True)
    sums[5:6, :] = jnp.sum(back, axis=0, keepdims=True)
    for part in range(parts):
        sums[6 + part : 7 + part, :] = fc_sums[part]


def last(place, grads, pieces, w, x, grad_mid, table, mid_sums, fc_sums):
    parts = w[0].shape[0]
    sub, width = x.shape
    rows = 8 * ((6 + 2 * parts + 7) // 8)
    return pl.pallas_call(
        functools.partial(last_kernel, parts, pieces),
        in_specs=[SM] + [VM] * (len(grads) + 7),
        out_specs=[VM, VM],
        out_shape=[shape((sub, width)), shape((rows, width), f32)],
        scratch_shapes=[pltpu.VMEM((width, sub), f32), pltpu.VMEM((w[0].shape[2], sub), bf16)],
        compiler_params=params(),
        cost_estimate=cost(6),
        name="last",
    )(place, *grads, w[0], w[1], x, grad_mid, table, mid_sums, fc_sums)


def fold_kernel(cut, sc, mine, theirs, lo_send, lo_keep, hi_send, hi_keep):
    i = pl.program_id(0)
    total = (mine[...].astype(f32) + theirs[...].astype(f32)).astype(bf16)
    lo, hi = total[None, :, :, :cut], total[None, :, :, cut:]

    @pl.when(i < 2)
    def _():
        lo_send[...] = lo

    @pl.when(i >= 2)
    def _():
        lo_keep[...] = lo

    @pl.when((i == 1) | (i == 2))
    def _():
        hi_send[...] = hi

    @pl.when((i == 0) | (i == 3))
    def _():
        hi_keep[...] = hi


def fold(place, mine, theirs):
    parts, rows, wide = mine.shape
    size = rows // 4
    cut = (wide // 256) * 128 if wide % 256 == 0 else (wide // 256 + 1) * 128
    block = pl.BlockSpec(
        (parts, size, wide),
        lambda i, sc: (
            0,
            sc[1] ^ jnp.where(i == 0, 1, jnp.where(i == 1, 3, jnp.where(i == 2, 2, 0))),
            0,
        ),
    )
    out = lambda width, index: pl.BlockSpec(
        (1, parts, size, width), lambda i, sc: (index(i), 0, 0, 0)
    )
    lo, hi = cut, wide - cut
    return pl.pallas_call(
        functools.partial(fold_kernel, cut),
        grid_spec=pltpu.PrefetchScalarGridSpec(
            num_scalar_prefetch=1,
            grid=(4,),
            in_specs=[block, block],
            out_specs=[
                out(lo, lambda i: jnp.minimum(i, 1)),
                out(lo, lambda i: jnp.where(i == 3, 0, 1)),
                out(hi, lambda i: jnp.where(i < 2, 1, 0)),
                out(hi, lambda i: jnp.where(i == 3, 0, 1)),
            ],
        ),
        out_shape=[
            shape((2, parts, size, lo)),
            shape((2, parts, size, lo)),
            shape((2, parts, size, hi)),
            shape((2, parts, size, hi)),
        ],
        compiler_params=params(),
        cost_estimate=cost(1 + 6 * parts / 4),
        name="fold",
    )(place, mine, theirs)


def body(
    n_shard,
    n_context,
    n_tensor,
    inputs,
    segments,
    w_qkv,
    w_out,
    w_fc,
    w_down,
    b_qv,
    b_out,
    b_fc,
    b_down,
    first_norm_gain,
    first_norm_bias,
    second_norm_gain,
    second_norm_bias,
    cotangent,
):
    _, tok, width = inputs.shape
    length = segments.shape[1]
    half, _, cols = w_qkv.shape
    heads = cols // HD
    ffw = w_fc.shape[1]
    sub = tok // n_tensor
    context = lax.axis_index("context")
    tensor = lax.axis_index("tensor")
    core = lax.axis_index("shard")
    first = context * tok
    place = jnp.stack([first, context, core, tensor]).astype(jnp.int32)
    grouped = n_context == 4
    x = inputs[0]
    cot = cotangent[0]
    row = lambda v: v[None, :]
    zero = jnp.zeros_like(b_out)
    table = jnp.concatenate(
        [
            first_norm_gain,
            first_norm_bias,
            b_out,
            b_down,
            second_norm_gain,
            second_norm_bias,
            zero,
            zero,
        ]
    ).reshape(8, width)
    after = lambda v, dep: lax.optimization_barrier((v, dep))[0]

    swap = lambda v: lax.ppermute(v, "shard", [(0, 1), (1, 0)])
    along_x = lambda v: lax.ppermute(v, "context", [(0, 1), (1, 0), (2, 3), (3, 2)])
    along_y = lambda v: lax.ppermute(v, "context", [(0, 2), (2, 0), (1, 3), (3, 1)])
    shift_by = lambda v, d: lax.ppermute(
        v, "tensor", [(s, (s + d) % n_tensor) for s in range(n_tensor)]
    )

    def gather_direct(v):
        return [v] + [shift_by(v, d) for d in range(1, n_tensor)]

    def gather_begin(v):
        if n_tensor != 4:
            return tuple(gather_direct(v))
        move = lambda perm: lax.ppermute(v, "tensor", perm)
        return (
            v,
            move([(0, 2), (1, 3), (2, 0), (3, 1)]),
            move([(0, 1), (1, 2), (2, 3)]),
            move([(3, 2), (2, 1), (1, 0)]),
        )

    def gather_end(state, hold=()):
        if n_tensor != 4:
            return list(state)
        v, two, right, left = state
        two = after(two, hold)
        far = lax.ppermute(two, "tensor", [(2, 3), (1, 0)])
        return [
            v,
            jnp.where(tensor == 0, far, right),
            two,
            jnp.where(tensor == 3, far, left),
        ]

    def scatter_line(pieces):
        if n_tensor != 4:
            total = pieces[0].astype(f32)
            for d in range(1, n_tensor):
                total += shift_by(pieces[d].astype(bf16), -d).astype(f32)
            return total
        move = lambda a, perm: lax.ppermute(a.astype(bf16), "tensor", perm)
        far = move(jnp.where(tensor == 0, pieces[1], pieces[3]), [(0, 1), (3, 2)])
        right = move(pieces[3], [(0, 1), (1, 2), (2, 3)])
        left = move(pieces[1], [(3, 2), (2, 1), (1, 0)])
        two = move(
            pieces[2].astype(f32) + far.astype(f32), [(0, 2), (1, 3), (2, 0), (3, 1)]
        )
        return (
            pieces[0].astype(f32) + right.astype(f32) + left.astype(f32) + two.astype(f32)
        )

    def scatter_begin(mine, theirs):
        theirs = swap(theirs)
        if not grouped:
            both = (mine.astype(f32) + theirs.astype(f32)).astype(bf16)
            return lax.psum_scatter(both, "context", scatter_dimension=1, tiled=True)
        return fold(place, mine, theirs)

    def scatter_first(state):
        if not grouped:
            return state
        lo_send, lo_keep, hi_send, hi_keep = state
        r, s = along_x(lo_send).astype(f32), along_y(hi_send).astype(f32)
        return (
            lo_keep[0].astype(f32) + r[0],
            hi_keep[0].astype(f32) + s[0],
            (lo_keep[1].astype(f32) + r[1]).astype(bf16),
            (hi_keep[1].astype(f32) + s[1]).astype(bf16),
        )

    def scatter_second(state):
        if not grouped:
            return state
        lo, hi, lo_send, hi_send = state
        lo += along_y(lo_send).astype(f32)
        hi += along_x(hi_send).astype(f32)
        return jnp.concatenate([lo, hi], axis=2)

    bounds = [jnp.sum((segments[0] < d).astype(jnp.int32)) for d in range(1, 5)]
    seg = lax.dynamic_slice_in_dim(segments[0], first, tok, 0)
    starts = jnp.zeros_like(seg)
    for d in range(1, 5):
        starts = jnp.where(seg == d, bounds[d - 1], starts)

    def scalars(bk, bq):
        count = tok // bq
        begin = starts.reshape(count, bq)
        base = first + jnp.arange(count, dtype=jnp.int32) * bq
        lo = begin[:, 0] // bk
        diag = base // bk
        end = (base + bq + bk - 1) // bk
        full = jnp.minimum(jnp.maximum((begin[:, -1] + bk - 1) // bk, lo), diag)
        table = jnp.stack([lo, full, diag, end], axis=1).reshape(-1)
        return jnp.concatenate([place, table.astype(jnp.int32)])

    qkv_own = w_qkv.reshape(half, 3 * cols)
    low_one, qt, kt, vt = project(
        place,
        x,
        qkv_own,
        swap(qkv_own),
        b_qv,
        table,
    )

    terms, rest = [], b_fc
    for _ in range(3):
        term = lax.reduce_precision(rest, 8, 7)
        terms.append(term.astype(bf16).reshape(ffw // half, half))
        rest = rest - term
    terms = jnp.concatenate(terms, axis=0)
    terms = jnp.pad(terms, ((0, 16 - terms.shape[0]), (0, 0)))
    packed = jnp.concatenate([w_out, terms, w_fc[:, :half], w_fc[:, half:]], axis=0)
    packed = gather_begin(packed)
    kv = []
    hold = ()
    head = 0
    for g in GROUPS:
        rows = slice(head * HD, (head + g) * HD)
        head += g
        k, v = kt[rows], vt[rows]
        if grouped:
            kx, vy = along_x(k), along_y(v)
            k_two, v_two = jnp.stack([k, kx]), jnp.stack([v, vy])
            k_two, v_two = after((k_two, v_two), packed[1:])
            k_yd, v_xd = along_y(k_two), along_x(v_two)
            hold = (k_two, v_two)
            kv.append([k, kx, k_yd, v, vy, v_xd])
        else:
            kv.append([lax.all_gather(jnp.concatenate([k, v], axis=0), "context", axis=0)])

    dn = gather_begin(after(w_down, packed[1]))
    saved = []
    att = [[] for _ in range(n_tensor)]
    head = 0
    for g, held in zip(GROUPS, kv):
        results = attend(scalars, row(starts), after(qt, packed[1:]), held, head, g, BK_F, BQ_F, n_tensor)
        lse, ot, *out = results
        saved.append((lse, ot))
        att[0].append(out[0])
        for d in range(1, n_tensor):
            att[d].append(shift_by(out[d], d))
        head += g

    of = jnp.stack(after(gather_end(packed, hold), att[1:]))
    of = (of, swap(of))
    dn = jnp.stack(gather_end(dn, att[1:]))
    dn = (dn, swap(dn))
    x_sub = lax.dynamic_slice_in_dim(x, tensor * sub, sub, 0)
    cot_sub = lax.dynamic_slice_in_dim(cot, tensor * sub, sub, 0)
    outputs_sub, grad_mid, mid_sums, fc_sums, *rest = middle(
        place,
        [piece for part in att for piece in part],
        x_sub,
        cot_sub,
        of,
        dn,
        cols,
        table,
    )
    d_att, (g_own, g_other) = rest[:n_tensor], rest[n_tensor:]
    do_parts = [d_att[0]] + [
        shift_by(d_att[d], -d) for d in range(1, n_tensor)
    ]

    def spread(pieces):
        whole = jnp.zeros((tok, width), f32)
        for d in range(n_tensor):
            at = lax.rem(tensor - d + n_tensor, n_tensor) * sub
            whole = lax.dynamic_update_slice_in_dim(whole, pieces[d].astype(f32), at, 0)
        return whole[None]

    folded = scatter_begin(g_own, g_other)
    hop_one = folded[0] if grouped else folded
    qkv_wide = jnp.pad(qkv_own, ((0, 0), (0, width - 3 * cols)))
    carried = jnp.concatenate([outputs_sub, qkv_wide], axis=0)
    folded = scatter_begin(g_own, g_other)
    hop_one = folded[0] if grouped else folded
    qkv_wide = jnp.pad(qkv_own, ((0, 0), (0, width - 3 * cols)))
    outputs_and_qkv = lax.all_gather(
        jnp.concatenate([outputs_sub, qkv_wide], axis=0), "tensor", axis=0
    )
    wide = scatter_first(folded)
    wide_sends = wide[2:]
    wide = scatter_second(wide)

    dq_pieces, dkv_pieces, dqkv = [], [], []
    head = 0
    queries, keys, values = [], [], []
    sent = [[] for _ in range(n_tensor)]
    for g, held, (lse, ot) in zip(GROUPS, kv, saved):
        out = attend_back(
            scalars, row(starts), after(qt, hop_one), lse, ot, do_parts, held, carried, head, g, BK_B, BQ_B
        )
        back_done = out[-1]
        *out, carried = out
        dq, dkv = after(out[:n_tensor], wide_sends), out[n_tensor:]
        if grouped:
            dk_keep, dk_send, dv_keep, dv_send = dkv
            dk_send, dv_send = after((dk_send, dv_send), wide_sends)
            r = along_x(dk_send).astype(f32)
            s = along_y(dv_send).astype(f32)
            r2 = along_y((dk_keep[1].astype(f32) + r[1]).astype(bf16)).astype(f32)
            s2 = along_x((dv_keep[1].astype(f32) + s[1]).astype(bf16)).astype(f32)
            dk = (dk_keep[0].astype(f32) + r[0] + r2).astype(bf16)
            dv = (dv_keep[0].astype(f32) + s[0] + s2).astype(bf16)
        else:
            both = lax.psum_scatter(dkv[0], "context", scatter_dimension=0, tiled=True)[0]
            dk, dv = both[: g * HD], both[g * HD :]
        queries.append(dq)
        keys.append(dk)
        values.append(dv)
        head += g

    wide_grads = scatter_line([wide[d] for d in range(n_tensor)])

    def part_of(v, d):
        at = lax.rem(tensor + d, n_tensor) * sub
        return lax.dynamic_slice_in_dim(v, at, sub, 1)

    grads = []
    both = jnp.concatenate(keys + values, axis=0)
    for d in range(n_tensor):
        piece = jnp.concatenate([q[d] for q in queries] + [part_of(both, d)], axis=0)
        grads.append(shift_by(piece, d) if d else piece)
    pieces = 1

    dq_whole = []
    for q in queries:
        whole = jnp.zeros((q[0].shape[0], tok), bf16)
        for d in range(n_tensor):
            at = lax.rem(tensor + d, n_tensor) * sub
            whole = lax.dynamic_update_slice_in_dim(whole, q[d], at, 1)
        dq_whole.append(whole)
    outputs_and_qkv = lax.all_gather(carried, "tensor", axis=0)
    outputs = outputs_and_qkv[:, :sub].reshape(tok, width)
    qkv = outputs_and_qkv[:, sub:]
    qkv = (qkv, swap(qkv))
    stacked = jnp.concatenate(
        dq_whole + [both, jnp.zeros((-3 * cols % 128, tok), bf16)], axis=0
    )
    qkv_grad = jnp.einsum(
        "td,ct->dc", low_one, stacked, preferred_element_type=f32
    ).astype(bf16)
    qkv_mine = lax.dynamic_slice_in_dim(qkv_grad, core * half, half, 0)
    qkv_theirs = lax.dynamic_slice_in_dim(qkv_grad, (1 - core) * half, half, 0)
    qkv_folded = scatter_begin(qkv_mine[None], qkv_theirs[None])

    input_sub, small = last(
        place, grads, pieces, qkv, x_sub, after(grad_mid, qkv_folded), table, mid_sums, fc_sums
    )
    input_gradient = spread(gather_direct(input_sub))
    outputs = after(outputs, input_sub).astype(f32)[None]
    qkv_grads = scatter_second(scatter_first(qkv_folded))[0]

    if grouped and n_tensor == 4 and n_shard == 2:
        small += lax.ppermute(small, "tensor", [(0, 2), (2, 0), (1, 3), (3, 1)])
        small += lax.ppermute(small, "tensor", [(0, 1), (1, 0), (2, 3), (3, 2)])
        small += swap(small)
        small += along_x(small)
        small += along_y(small)
    else:
        small = lax.psum(small, ("shard", "context", "tensor"))
    fc_total = lax.dynamic_index_in_dim(small, 6 + tensor, 0, keepdims=False)
    qv_total = lax.dynamic_index_in_dim(small, 6 + n_tensor + tensor, 0, keepdims=False)
    qv_total = jnp.stack([qv_total[:cols], qv_total[2 * cols : 3 * cols]])
    return (
        outputs,
        input_gradient,
        qkv_grads[:, : 3 * cols].astype(f32).reshape(-1, 3, cols),
        wide_grads[:, 2 * ffw : 2 * ffw + cols].T,
        wide_grads[:, :ffw],
        wide_grads[:, ffw : 2 * ffw].T,
        qv_total,
        small[0],
        fc_total,
        small[1],
        small[4],
        small[5],
        small[2],
        small[3],
    )


def solution(mesh):
    sizes = dict(mesh.shape)
    placed = (
        P("shard", "context", None),
        P("shard", None),
        P("shard", None, "tensor"),
        P("tensor", "shard"),
        P("shard", "tensor"),
        P("tensor", "shard"),
        P(None, "tensor"),
        P(),
        P("tensor"),
        P(),
        P(),
        P(),
        P(),
        P(),
        P("shard", "context", None),
    )
    return jax.shard_map(
        functools.partial(body, sizes["shard"], sizes["context"], sizes["tensor"]),
        mesh=mesh,
        in_specs=placed,
        out_specs=(
            P("shard", "context", None),
            P("shard", "context", None),
            P(("shard", "context"), None, "tensor"),
            P("tensor", ("shard", "context")),
            P(("shard", "context"), "tensor"),
            P("tensor", ("shard", "context")),
            P(None, "tensor"),
            P(),
            P("tensor"),
            P(),
            P(),
            P(),
            P(),
            P(),
        ),
        check_vma=False,
    )
```

```python
import functools

import jax
import jax.numpy as jnp
from jax import lax
from jax.experimental import pallas as pl
from jax.experimental.pallas import tpu as pltpu
from jax.sharding import PartitionSpec as P

HD = 64
EPS = 1e-05
NEG = -1e30
SCALE = float(HD) ** -0.5
VMEM_LIMIT = 56 * 1024 * 1024
GROUPS = (3,)
BK_F, BQ_F = 512, 512
BK_B, BQ_B = 512, 512
f32 = jnp.float32
bf16 = jnp.bfloat16
VM = pl.BlockSpec(memory_space=pltpu.VMEM)
SM = pl.BlockSpec(memory_space=pltpu.SMEM)
HBM = pl.BlockSpec(memory_space=pl.ANY)


def nn(a, b):
    return lax.dot_general(a, b, (((1,), (0,)), ((), ())), preferred_element_type=f32)


def tn(a, b):
    return lax.dot_general(a, b, (((0,), (0,)), ((), ())), preferred_element_type=f32)


def nt(a, b):
    return lax.dot_general(a, b, (((1,), (1,)), ((), ())), preferred_element_type=f32)


def params():
    return pltpu.CompilerParams(vmem_limit_bytes=VMEM_LIMIT)


def cost(microseconds):
    return pl.CostEstimate(
        flops=int(microseconds * 1.15e9), bytes_accessed=1 << 20, transcendentals=0
    )


def shape(dims, kind=bf16):
    return jax.ShapeDtypeStruct(dims, kind)


def halves(core, width):
    half = width // 2
    own = pl.ds(pl.multiple_of(core * half, 128), half)
    other = pl.ds(pl.multiple_of((1 - core) * half, 128), half)
    return own, other


def norm(value):
    centred = value - jnp.mean(value, axis=-1, keepdims=True)
    inverse = lax.rsqrt(jnp.mean(centred * centred, axis=-1, keepdims=True) + EPS)
    return centred * inverse, inverse


def norm_gradient(grad, normed, inverse, gain):
    scaled = grad * gain
    return inverse * (
        scaled
        - jnp.mean(scaled, axis=-1, keepdims=True)
        - normed * jnp.mean(scaled * normed, axis=-1, keepdims=True)
    )


def project_kernel(sc, x, w_own, w_other, b_qv, rows, low, qt, kt, vt):
    own, other = halves(sc[2], x.shape[1])
    cols = qt.shape[0]
    normed, _ = norm(x[...].astype(f32))
    low[...] = (normed * rows[0:1, :] + rows[1:2, :]).astype(bf16)
    projected = nn(low[:, own], w_own[...]) + nn(low[:, other], w_other[...])
    qt[...] = ((projected[:, :cols] + b_qv[0:1, :]) * SCALE).T.astype(bf16)
    kt[...] = projected[:, cols : 2 * cols].T.astype(bf16)
    vt[...] = (projected[:, 2 * cols :] + b_qv[1:2, :]).T.astype(bf16)


def project(place, x, w_own, w_other, b_qv, table):
    tok, width = x.shape
    cols = b_qv.shape[1]
    rows = min(256, tok)
    fixed = lambda a: pl.BlockSpec(a.shape, lambda i: (0,) * a.ndim)
    across = pl.BlockSpec((cols, rows), lambda i: (0, i))
    return pl.pallas_call(
        project_kernel,
        grid=(tok // rows,),
        in_specs=[SM, pl.BlockSpec((rows, width), lambda i: (i, 0))]
        + [fixed(a) for a in (w_own, w_other, b_qv, table)],
        out_specs=[pl.BlockSpec((rows, width), lambda i: (i, 0)), across, across, across],
        out_shape=[shape((tok, width))] + [shape((cols, tok))] * 3,
        compiler_params=params(),
        cost_estimate=cost(7),
        name="project",
    )(place, x, w_own, w_other, b_qv, table)


def key_loop(sc, i, step, carry):
    lo, full, diag, end = sc[4 * i + 4], sc[4 * i + 5], sc[4 * i + 6], sc[4 * i + 7]
    carry = lax.fori_loop(lo, full, functools.partial(step, True), carry)
    carry = lax.fori_loop(full, diag, functools.partial(step, False), carry)
    return lax.fori_loop(diag, end, functools.partial(step, True), carry)


def tile_mask(j, bk, bq, start, qpos):
    kpos = j * bk + lax.broadcasted_iota(jnp.int32, (bk, bq), 0)
    return (kpos >= start) & (kpos <= qpos)


def load_keys(sc, kv, held, sems):
    if len(kv) == 1:
        copies = [pltpu.make_async_copy(kv[0], held, sems.at[0])]
    else:
        k, k_x, k_yd, v, v_y, v_xd = kv
        rows = k.shape[0]
        pieces = [(k, 0, 0), (k_x, 0, 1), (k_yd.at[0], 0, 2), (k_yd.at[1], 0, 3)]
        pieces += [(v, 1, 0), (v_y, 1, 2), (v_xd.at[0], 1, 1), (v_xd.at[1], 1, 3)]
        copies = [
            pltpu.make_async_copy(
                piece, held.at[sc[1] ^ run, pl.ds(which * rows, rows), :], sems.at[n]
            )
            for n, (piece, which, run) in enumerate(pieces)
        ]
    for copy in copies:
        copy.start()
    for copy in copies:
        copy.wait()


def attend_kernel(first_head, heads, bk, bq, parts, n_kv, sc, qt, st, *refs):
    kv, refs = refs[:n_kv], refs[n_kv:]
    lse, ot, out, (held, acc, sems) = refs[0], refs[1], refs[2 : 2 + parts], refs[2 + parts :]
    i = pl.program_id(0)
    per = held.shape[2] // bk
    cols = heads * HD
    start = st[...]
    qpos = sc[0] + i * bq + lax.broadcasted_iota(jnp.int32, (1, bq), 1)

    @pl.when(i == 0)
    def _():
        load_keys(sc, kv, held, sems)

    acc[...] = jnp.zeros_like(acc)

    def step(masked, j, carry):
        r = j // per
        off = pl.multiple_of((j % per) * bk, bk)
        new = []
        if masked:
            ok = tile_mask(j, bk, bq, start, qpos)
        for h in range(heads):
            m, l = carry[h]
            hs = slice(h * HD, (h + 1) * HD)
            s = tn(
                held[r, hs, pl.ds(off, bk)],
                qt[(first_head + h) * HD : (first_head + h + 1) * HD, :],
            )
            if masked:
                s = jnp.where(ok, s, NEG)
            m2 = jnp.maximum(m, jnp.max(s, axis=0, keepdims=True))
            p = jnp.exp(s - m2)
            al = jnp.exp(m - m2)
            l = l * al + jnp.sum(p, axis=0, keepdims=True)
            v = held[r, cols + h * HD : cols + (h + 1) * HD, pl.ds(off, bk)]
            acc[hs, :] = acc[hs, :] * al + nn(v, p.astype(bf16))
            new.append((m2, l))
        return tuple(new)

    one = (jnp.full((1, bq), NEG, f32), jnp.zeros((1, bq), f32))
    res = key_loop(sc, i, step, (one,) * heads)
    here = pl.ds(pl.multiple_of(i * bq, bq), bq)
    for h in range(heads):
        m, l = res[h]
        ot[h * HD : (h + 1) * HD, here] = (acc[h * HD : (h + 1) * HD, :] / l).astype(bf16)
        lse[h : h + 1, :] = m + jnp.log(l)

    @pl.when(i == pl.num_programs(0) - 1)
    def _():
        send_parts(sc[3], ot, out)


def send_parts(me, source, out):
    parts, size = len(out), out[0].shape[1]
    for d in range(parts):
        if size % 128 == 0:
            at = pl.multiple_of(lax.rem(me + d, parts) * size, 128)
            out[d][...] = source[:, pl.ds(at, size)].astype(out[d].dtype)
        else:
            for n in range(parts):

                @pl.when(lax.rem(me + d, parts) == n)
                def _():
                    out[d][...] = source[:, n * size : (n + 1) * size].astype(out[d].dtype)


def take_parts(me, rows, parts, target):
    size = parts[0].shape[1]
    for d in range(len(parts)):
        if size % 128 == 0:
            at = pl.multiple_of(lax.rem(me + d, len(parts)) * size, 128)
            target[:, pl.ds(at, size)] = parts[d][rows, :]
        else:
            for n in range(len(parts)):

                @pl.when(lax.rem(me + d, len(parts)) == n)
                def _():
                    target[:, n * size : (n + 1) * size] = parts[d][rows, :]


def attend(scalars, starts, qt, kv, first_head, heads, bk, bq, parts):
    tok = qt.shape[1]
    cols = heads * HD
    runs = kv[0].shape[0] if len(kv) == 1 else 4
    bk, bq = min(bk, tok), min(bq, tok)
    whole = lambda a, b: pl.BlockSpec((a, b), lambda i: (0, 0))
    return pl.pallas_call(
        functools.partial(attend_kernel, first_head, heads, bk, bq, parts, len(kv)),
        grid=(tok // bq,),
        in_specs=[
            SM,
            pl.BlockSpec((qt.shape[0], bq), lambda i: (0, i)),
            pl.BlockSpec((1, bq), lambda i: (0, i)),
        ]
        + [HBM] * len(kv),
        out_specs=[pl.BlockSpec((heads, bq), lambda i: (0, i)), whole(cols, tok)]
        + [whole(cols, tok // parts)] * parts,
        scratch_shapes=[
            pltpu.VMEM((runs, 2 * cols, tok), bf16),
            pltpu.VMEM((cols, bq), f32),
            pltpu.SemaphoreType.DMA((8,)),
        ],
        out_shape=[shape((heads, tok), f32), shape((cols, tok))]
        + [shape((cols, tok // parts))] * parts,
        compiler_params=params(),
        cost_estimate=cost(20),
        name="attend",
    )(scalars(bk, bq), qt, starts, *kv)


def attend_back_kernel(first_head, heads, bk, bq, parts, n_kv, sc, qt, st, lse, ot, *refs):
    do_parts, refs = refs[:parts], refs[parts:]
    kv, refs = refs[:n_kv], refs[n_kv + 1 :]
    n_out = 1 if n_kv == 1 else 4
    dq, dkv, (held, acc, dqa, do_all, sems) = (
        refs[:parts],
        refs[parts : parts + n_out],
        refs[parts + n_out + 1 :],
    )
    i = pl.program_id(0)
    per = held.shape[2] // bk
    cols = heads * HD
    start = st[...]
    qpos = sc[0] + i * bq + lax.broadcasted_iota(jnp.int32, (1, bq), 1)
    here = pl.ds(pl.multiple_of(i * bq, bq), bq)

    @pl.when(i == 0)
    def _():
        acc[...] = jnp.zeros_like(acc)
        dqa[...] = jnp.zeros_like(dqa)
        take_parts(sc[3], slice(first_head * HD, (first_head + heads) * HD), do_parts, do_all)
        load_keys(sc, kv, held, sems)

    delta = [
        jnp.sum(
            do_all[h * HD : (h + 1) * HD, here].astype(f32)
            * ot[h * HD : (h + 1) * HD, :].astype(f32),
            axis=0,
            keepdims=True,
        )
        for h in range(heads)
    ]

    def step(masked, j, carry):
        r = j // per
        off = pl.multiple_of((j % per) * bk, bk)
        if masked:
            ok = tile_mask(j, bk, bq, start, qpos)
        for h in range(heads):
            hs = slice(h * HD, (h + 1) * HD)
            vs = slice(cols + h * HD, cols + (h + 1) * HD)
            k = held[r, hs, pl.ds(off, bk)]
            v = held[r, vs, pl.ds(off, bk)]
            q = qt[(first_head + h) * HD : (first_head + h + 1) * HD, :]
            do = do_all[hs, here]
            s = tn(k, q) - lse[h : h + 1, :]
            if masked:
                s = jnp.where(ok, s, NEG)
            p = jnp.exp(s)
            ds = (p * (tn(v, do) - delta[h])).astype(bf16)
            acc[r, vs, pl.ds(off, bk)] += nt(do, p.astype(bf16))
            acc[r, hs, pl.ds(off, bk)] += nt(q, ds)
            dqa[hs, here] += nn(k, ds)
        return carry

    key_loop(sc, i, step, 0)

    @pl.when(i == pl.num_programs(0) - 1)
    def _():
        dqa[...] = dqa[...] * SCALE
        send_parts(sc[3], dqa, dq)
        if n_out == 1:
            dkv[0][...] = acc[...].astype(bf16)
        else:
            for target, pair, rows in (
                (0, (0, 2), slice(0, cols)),
                (1, (1, 3), slice(0, cols)),
                (2, (0, 1), slice(cols, 2 * cols)),
                (3, (2, 3), slice(cols, 2 * cols)),
            ):
                for n in range(2):
                    dkv[target][n] = acc[sc[1] ^ pair[n], rows, :].astype(bf16)


def attend_back(scalars, starts, qt, lse, ot, do_parts, kv, carried, first_head, heads, bk, bq):
    tok = qt.shape[1]
    cols = heads * HD
    parts = len(do_parts)
    runs = kv[0].shape[0] if len(kv) == 1 else 4
    bk, bq = min(bk, tok), min(bq, tok)
    whole = lambda *dims: pl.BlockSpec(dims, lambda i: (0,) * len(dims))
    out_kv = [(runs, 2 * cols, tok)] if len(kv) == 1 else [(2, cols, tok)] * 4
    return pl.pallas_call(
        functools.partial(attend_back_kernel, first_head, heads, bk, bq, parts, len(kv)),
        grid=(tok // bq,),
        in_specs=[
            SM,
            pl.BlockSpec((qt.shape[0], bq), lambda i: (0, i)),
            pl.BlockSpec((1, bq), lambda i: (0, i)),
            pl.BlockSpec((heads, bq), lambda i: (0, i)),
            pl.BlockSpec((cols, bq), lambda i: (0, i)),
        ]
        + [whole(*d.shape) for d in do_parts]
        + [HBM] * (len(kv) + 1),
        out_specs=[whole(cols, tok // parts)] * parts + [whole(*d) for d in out_kv] + [HBM],
        scratch_shapes=[
            pltpu.VMEM((runs, 2 * cols, tok), bf16),
            pltpu.VMEM((runs, 2 * cols, tok), f32),
            pltpu.VMEM((cols, tok), f32),
            pltpu.VMEM((cols, tok), bf16),
            pltpu.SemaphoreType.DMA((8,)),
        ],
        out_shape=[shape((cols, tok // parts))] * parts
        + [shape(d) for d in out_kv]
        + [shape(carried.shape)],
        input_output_aliases={5 + parts + len(kv): parts + len(out_kv)},
        compiler_params=params(),
        cost_estimate=cost(26),
        name="attend_back",
    )(scalars(bk, bq), qt, starts, lse, ot, *do_parts, *kv, carried)


ROOT = 0.7978845608028654


def middle_kernel(n_att, parts, sc, *refs):
    att, refs = refs[:n_att], refs[n_att:]
    x, cot, of_own, of_other, dn_own, dn_other, rows = refs[:7]
    refs = refs[7:]
    outputs, grad_mid, sums, fc_sums = refs[:4]
    d_att, (g_own, g_other) = refs[4 : 4 + parts], refs[4 + parts : 6 + parts]
    mid, att_t, low, low_t, cot_t, mlp, back = refs[6 + parts :]
    d = pl.program_id(0)
    width = x.shape[1]
    own, other = halves(sc[2], width)
    half = width // 2
    ffw = dn_own.shape[1]
    count = ffw // half
    cols = att_t.shape[0] // parts
    b_out, b_down, gain, shift = (rows[n : n + 1, :] for n in range(2, 6))

    @pl.when(d == 0)
    def _():
        group = n_att // parts
        row = 0
        for part in range(parts):
            for g in range(group):
                piece = att[part * group + g]
                att_t[row : row + piece.shape[0], :] = piece[...]
                row += piece.shape[0]
        att_low = att_t[...].T
        mine = theirs = 0.0
        for part in range(parts):
            piece = att_low[:, part * cols : (part + 1) * cols]
            mine += nn(piece, of_own[part, :cols, :])
            theirs += nn(piece, of_other[part, :cols, :])
        mid[:, own] = mine
        mid[:, other] = theirs
        mid[...] = x[...].astype(f32) + mid[...] + b_out
        normed, _ = norm(mid[...])
        low[...] = (normed * gain + shift).astype(bf16)
        low_t[...] = low[...].T
        cot_t[...] = cot[...].T
        mlp[...] = jnp.zeros_like(mlp)
        back[...] = jnp.zeros_like(back)

    own_rows = pl.ds(pl.multiple_of(sc[2] * half, half), half)
    other_rows = pl.ds(pl.multiple_of((1 - sc[2]) * half, half), half)
    terms = of_own[d, cols : cols + 16, :].astype(f32)
    pieces = [slice(cols + 16 + n * half, cols + 16 + (n + 1) * half) for n in range(count)]
    u = [
        nn(low[:, own], of_own[d, at, :])
        + nn(low[:, other], of_other[d, at, :])
        + sum(terms[t * count + n : t * count + n + 1, :] for t in range(3))
        for n, at in enumerate(pieces)
    ]
    u = jnp.concatenate(u, axis=1)
    t = jnp.tanh(ROOT * (u + 0.044715 * (u * u * u)))
    act = (0.5 * u * (1.0 + t)).astype(bf16)
    slope = 0.5 * (1.0 + t) + (0.5 * ROOT) * u * (1.0 - t * t) * (1.0 + 0.134145 * (u * u))
    d_act = nt(cot[:, own], dn_own[0]) + nt(cot[:, other], dn_other[0])
    dh = (d_act * slope).astype(bf16)
    mlp[:, own] += nn(act, dn_own[0])
    mlp[:, other] += nn(act, dn_other[0])
    for n, at in enumerate(pieces):
        dh_n = dh[:, n * half : (n + 1) * half]
        back[:, own] += nt(dh_n, of_own[d, at, :])
        back[:, other] += nt(dh_n, of_other[d, at, :])
    g_own[d, :, :ffw] = nn(low_t[own_rows, :], dh).astype(bf16)
    g_other[d, :, :ffw] = nn(low_t[other_rows, :], dh).astype(bf16)
    g_own[d, :, ffw : 2 * ffw] = nn(cot_t[own_rows, :], act).astype(bf16)
    g_other[d, :, ffw : 2 * ffw] = nn(cot_t[other_rows, :], act).astype(bf16)
    fc_sums[lax.rem(sc[3] - d + parts, parts)] = jnp.sum(dh.astype(f32), axis=0, keepdims=True)

    @pl.when(d == parts - 1)
    def _():
        normed, inverse = norm(mid[...])
        outputs[...] = (mid[...] + mlp[...] + b_down).astype(bf16)
        upper = cot[...].astype(f32)
        grad = back[...]
        down = upper + norm_gradient(grad, normed, inverse, gain)
        grad_mid[...] = down
        sums[0:1, :] = jnp.sum(down, axis=0, keepdims=True)
        sums[1:2, :] = jnp.sum(upper, axis=0, keepdims=True)
        sums[2:3, :] = jnp.sum(grad * normed, axis=0, keepdims=True)
        sums[3:4, :] = jnp.sum(grad, axis=0, keepdims=True)
        low[...] = down.astype(bf16)
        low_t[...] = low[...].T
        g_own[:, :, 2 * ffw + cols :] = jnp.zeros_like(g_own[:, :, 2 * ffw + cols :])
        g_other[:, :, 2 * ffw + cols :] = jnp.zeros_like(g_other[:, :, 2 * ffw + cols :])
        for part in range(parts):
            at = slice(part * cols, (part + 1) * cols)
            g_own[part, :, 2 * ffw : 2 * ffw + cols] = nt(low_t[own_rows, :], att_t[at, :]).astype(bf16)
            g_other[part, :, 2 * ffw : 2 * ffw + cols] = nt(low_t[other_rows, :], att_t[at, :]).astype(bf16)
            d_att[part][...] = (
                nt(of_own[part, :cols, :], low[:, own]) + nt(of_other[part, :cols, :], low[:, other])
            ).astype(bf16)


def middle(place, att, x, cot, of, dn, cols, table):
    parts, ffw, half = dn[0].shape
    sub, width = x.shape
    whole = lambda *dims: pl.BlockSpec(
        dims, lambda i, sc: (0,) * len(dims), pipeline_mode=pl.Buffered(1)
    )
    placed = pl.BlockSpec(
        (1, ffw, half), lambda i, sc: (i, 0, 0)
    )
    once = lambda a: whole(*a.shape)
    grads = (parts, half, 128 * ((2 * ffw + cols + 127) // 128))
    return pl.pallas_call(
        functools.partial(middle_kernel, len(att), parts),
        grid_spec=pltpu.PrefetchScalarGridSpec(
            num_scalar_prefetch=1,
            grid=(parts,),
            in_specs=[once(a) for a in att]
            + [once(x), once(cot), once(of[0]), once(of[1]), placed, placed, once(table)],
            out_specs=[whole(sub, width), whole(sub, width), whole(4, width), whole(parts, 1, ffw)]
            + [whole(cols, sub)] * parts
            + [whole(*grads)] * 2,
            scratch_shapes=[
                pltpu.VMEM((sub, width), f32),
                pltpu.VMEM((parts * cols, sub), bf16),
                pltpu.VMEM((sub, width), bf16),
                pltpu.VMEM((width, sub), bf16),
                pltpu.VMEM((width, sub), bf16),
                pltpu.VMEM((sub, width), f32),
                pltpu.VMEM((sub, width), f32),
            ],
        ),
        out_shape=[
            shape((sub, width)),
            shape((sub, width), f32),
            shape((4, width), f32),
            shape((parts, 1, ffw), f32),
        ]
        + [shape((cols, sub))] * parts
        + [shape(grads)] * 2,
        compiler_params=params(),
        cost_estimate=cost(19),
        name="middle",
    )(place, *att, x, cot, of[0], of[1], dn[0], dn[1], table)


def last_kernel(parts, pieces, sc, *refs):
    grads, refs = refs[: parts * pieces], refs[parts * pieces :]
    w_own, w_other, x, grad_mid, rows, mid_sums, fc_sums, out, sums, back_t, stacked = refs
    half = w_own.shape[1]
    wide = w_own.shape[2]
    own_rows = pl.ds(pl.multiple_of(sc[2] * half, half), half)
    other_rows = pl.ds(pl.multiple_of((1 - sc[2]) * half, half), half)
    ones = jnp.ones((8, x.shape[0]), bf16)
    sums[...] = jnp.zeros_like(sums)
    stacked[...] = jnp.zeros_like(stacked)
    for part in range(parts):
        row = 0
        for n in range(pieces):
            piece = grads[part * pieces + n]
            stacked[row : row + piece.shape[0], :] = piece[...]
            row += piece.shape[0]
        at = lax.rem(sc[3] - part + parts, parts)
        mine, theirs = nn(w_own[at], stacked[...]), nn(w_other[at], stacked[...])
        if part == 0:
            back_t[own_rows, :], back_t[other_rows, :] = mine, theirs
        else:
            back_t[own_rows, :] += mine
            back_t[other_rows, :] += theirs
        sums[pl.ds(6 + parts + at, 1), :wide] = nt(ones, stacked[...])[0:1, :]
    back = back_t[...].T
    normed, inverse = norm(x[...].astype(f32))
    out[...] = (grad_mid[...] + norm_gradient(back, normed, inverse, rows[0:1, :])).astype(bf16)
    sums[0:4, :] = mid_sums[...]
    sums[4:5, :] = jnp.sum(back * normed, axis=0, keepdims=True)
    sums[5:6, :] = jnp.sum(back, axis=0, keepdims=True)
    for part in range(parts):
        sums[6 + part : 7 + part, :] = fc_sums[part]


def last(place, grads, pieces, w, x, grad_mid, table, mid_sums, fc_sums):
    parts = w[0].shape[0]
    sub, width = x.shape
    rows = 8 * ((6 + 2 * parts + 7) // 8)
    return pl.pallas_call(
        functools.partial(last_kernel, parts, pieces),
        in_specs=[SM] + [VM] * (len(grads) + 7),
        out_specs=[VM, VM],
        out_shape=[shape((sub, width)), shape((rows, width), f32)],
        scratch_shapes=[pltpu.VMEM((width, sub), f32), pltpu.VMEM((w[0].shape[2], sub), bf16)],
        compiler_params=params(),
        cost_estimate=cost(6),
        name="last",
    )(place, *grads, w[0], w[1], x, grad_mid, table, mid_sums, fc_sums)


def fold_kernel(cut, sc, mine, theirs, lo_send, lo_keep, hi_send, hi_keep):
    i = pl.program_id(0)
    total = (mine[...].astype(f32) + theirs[...].astype(f32)).astype(bf16)
    lo, hi = total[None, :, :, :cut], total[None, :, :, cut:]

    @pl.when(i < 2)
    def _():
        lo_send[...] = lo

    @pl.when(i >= 2)
    def _():
        lo_keep[...] = lo

    @pl.when((i == 1) | (i == 2))
    def _():
        hi_send[...] = hi

    @pl.when((i == 0) | (i == 3))
    def _():
        hi_keep[...] = hi


def fold(place, mine, theirs):
    parts, rows, wide = mine.shape
    size = rows // 4
    cut = (wide // 256) * 128 if wide % 256 == 0 else (wide // 256 + 1) * 128
    block = pl.BlockSpec(
        (parts, size, wide),
        lambda i, sc: (
            0,
            sc[1] ^ jnp.where(i == 0, 1, jnp.where(i == 1, 3, jnp.where(i == 2, 2, 0))),
            0,
        ),
    )
    out = lambda width, index: pl.BlockSpec(
        (1, parts, size, width), lambda i, sc: (index(i), 0, 0, 0)
    )
    lo, hi = cut, wide - cut
    return pl.pallas_call(
        functools.partial(fold_kernel, cut),
        grid_spec=pltpu.PrefetchScalarGridSpec(
            num_scalar_prefetch=1,
            grid=(4,),
            in_specs=[block, block],
            out_specs=[
                out(lo, lambda i: jnp.minimum(i, 1)),
                out(lo, lambda i: jnp.where(i == 3, 0, 1)),
                out(hi, lambda i: jnp.where(i < 2, 1, 0)),
                out(hi, lambda i: jnp.where(i == 3, 0, 1)),
            ],
        ),
        out_shape=[
            shape((2, parts, size, lo)),
            shape((2, parts, size, lo)),
            shape((2, parts, size, hi)),
            shape((2, parts, size, hi)),
        ],
        compiler_params=params(),
        cost_estimate=cost(1 + 6 * parts / 4),
        name="fold",
    )(place, mine, theirs)


def body(
    n_shard,
    n_context,
    n_tensor,
    inputs,
    segments,
    w_qkv,
    w_out,
    w_fc,
    w_down,
    b_qv,
    b_out,
    b_fc,
    b_down,
    first_norm_gain,
    first_norm_bias,
    second_norm_gain,
    second_norm_bias,
    cotangent,
):
    _, tok, width = inputs.shape
    length = segments.shape[1]
    half, _, cols = w_qkv.shape
    heads = cols // HD
    ffw = w_fc.shape[1]
    sub = tok // n_tensor
    context = lax.axis_index("context")
    tensor = lax.axis_index("tensor")
    core = lax.axis_index("shard")
    first = context * tok
    place = jnp.stack([first, context, core, tensor]).astype(jnp.int32)
    grouped = n_context == 4
    x = inputs[0]
    cot = cotangent[0]
    row = lambda v: v[None, :]
    zero = jnp.zeros_like(b_out)
    table = jnp.concatenate(
        [
            first_norm_gain,
            first_norm_bias,
            b_out,
            b_down,
            second_norm_gain,
            second_norm_bias,
            zero,
            zero,
        ]
    ).reshape(8, width)
    after = lambda v, dep: lax.optimization_barrier((v, dep))[0]

    swap = lambda v: lax.ppermute(v, "shard", [(0, 1), (1, 0)])
    along_x = lambda v: lax.ppermute(v, "context", [(0, 1), (1, 0), (2, 3), (3, 2)])
    along_y = lambda v: lax.ppermute(v, "context", [(0, 2), (2, 0), (1, 3), (3, 1)])
    shift_by = lambda v, d: lax.ppermute(
        v, "tensor", [(s, (s + d) % n_tensor) for s in range(n_tensor)]
    )

    def gather_direct(v):
        return [v] + [shift_by(v, d) for d in range(1, n_tensor)]

    def gather_begin(v):
        if n_tensor != 4:
            return tuple(gather_direct(v))
        move = lambda perm: lax.ppermute(v, "tensor", perm)
        return (
            v,
            move([(0, 2), (1, 3), (2, 0), (3, 1)]),
            move([(0, 1), (1, 2), (2, 3)]),
            move([(3, 2), (2, 1), (1, 0)]),
        )

    def gather_end(state, hold=()):
        if n_tensor != 4:
            return list(state)
        v, two, right, left = state
        two = after(two, hold)
        far = lax.ppermute(two, "tensor", [(2, 3), (1, 0)])
        return [
            v,
            jnp.where(tensor == 0, far, right),
            two,
            jnp.where(tensor == 3, far, left),
        ]

    def scatter_line(pieces):
        if n_tensor != 4:
            total = pieces[0].astype(f32)
            for d in range(1, n_tensor):
                total += shift_by(pieces[d].astype(bf16), -d).astype(f32)
            return total
        move = lambda a, perm: lax.ppermute(a.astype(bf16), "tensor", perm)
        far = move(jnp.where(tensor == 0, pieces[1], pieces[3]), [(0, 1), (3, 2)])
        right = move(pieces[3], [(0, 1), (1, 2), (2, 3)])
        left = move(pieces[1], [(3, 2), (2, 1), (1, 0)])
        two = move(
            pieces[2].astype(f32) + far.astype(f32), [(0, 2), (1, 3), (2, 0), (3, 1)]
        )
        return (
            pieces[0].astype(f32) + right.astype(f32) + left.astype(f32) + two.astype(f32)
        )

    def scatter_begin(mine, theirs):
        theirs = swap(theirs)
        if not grouped:
            both = (mine.astype(f32) + theirs.astype(f32)).astype(bf16)
            return lax.psum_scatter(both, "context", scatter_dimension=1, tiled=True)
        return fold(place, mine, theirs)

    def scatter_first(state):
        if not grouped:
            return state
        lo_send, lo_keep, hi_send, hi_keep = state
        r, s = along_x(lo_send).astype(f32), along_y(hi_send).astype(f32)
        return (
            lo_keep[0].astype(f32) + r[0],
            hi_keep[0].astype(f32) + s[0],
            (lo_keep[1].astype(f32) + r[1]).astype(bf16),
            (hi_keep[1].astype(f32) + s[1]).astype(bf16),
        )

    def scatter_second(state):
        if not grouped:
            return state
        lo, hi, lo_send, hi_send = state
        lo += along_y(lo_send).astype(f32)
        hi += along_x(hi_send).astype(f32)
        return jnp.concatenate([lo, hi], axis=2)

    bounds = [jnp.sum((segments[0] < d).astype(jnp.int32)) for d in range(1, 5)]
    seg = lax.dynamic_slice_in_dim(segments[0], first, tok, 0)
    starts = jnp.zeros_like(seg)
    for d in range(1, 5):
        starts = jnp.where(seg == d, bounds[d - 1], starts)

    def scalars(bk, bq):
        count = tok // bq
        begin = starts.reshape(count, bq)
        base = first + jnp.arange(count, dtype=jnp.int32) * bq
        lo = begin[:, 0] // bk
        diag = base // bk
        end = (base + bq + bk - 1) // bk
        full = jnp.minimum(jnp.maximum((begin[:, -1] + bk - 1) // bk, lo), diag)
        table = jnp.stack([lo, full, diag, end], axis=1).reshape(-1)
        return jnp.concatenate([place, table.astype(jnp.int32)])

    qkv_own = w_qkv.reshape(half, 3 * cols)
    low_one, qt, kt, vt = project(
        place,
        x,
        qkv_own,
        swap(qkv_own),
        b_qv,
        table,
    )

    terms, rest = [], b_fc
    for _ in range(3):
        term = lax.reduce_precision(rest, 8, 7)
        terms.append(term.astype(bf16).reshape(ffw // half, half))
        rest = rest - term
    terms = jnp.concatenate(terms, axis=0)
    terms = jnp.pad(terms, ((0, 16 - terms.shape[0]), (0, 0)))
    packed = jnp.concatenate([w_out, terms, w_fc[:, :half], w_fc[:, half:]], axis=0)
    packed = gather_begin(packed)
    kv = []
    hold = ()
    head = 0
    for g in GROUPS:
        rows = slice(head * HD, (head + g) * HD)
        head += g
        k, v = kt[rows], vt[rows]
        if grouped:
            kx, vy = along_x(k), along_y(v)
            k_two, v_two = jnp.stack([k, kx]), jnp.stack([v, vy])
            k_two, v_two = after((k_two, v_two), packed[1:])
            k_yd, v_xd = along_y(k_two), along_x(v_two)
            hold = (k_two, v_two)
            kv.append([k, kx, k_yd, v, vy, v_xd])
        else:
            kv.append([lax.all_gather(jnp.concatenate([k, v], axis=0), "context", axis=0)])

    dn = gather_begin(after(w_down, packed[1]))
    saved = []
    att = [[] for _ in range(n_tensor)]
    head = 0
    for g, held in zip(GROUPS, kv):
        results = attend(scalars, row(starts), after(qt, packed[1:]), held, head, g, BK_F, BQ_F, n_tensor)
        lse, ot, *out = results
        saved.append((lse, ot))
        att[0].append(out[0])
        for d in range(1, n_tensor):
            att[d].append(shift_by(out[d], d))
        head += g

    of = jnp.stack(after(gather_end(packed, hold), att[1:]))
    of = (of, swap(of))
    dn = jnp.stack(gather_end(dn, att[1:]))
    dn = (dn, swap(dn))
    x_sub = lax.dynamic_slice_in_dim(x, tensor * sub, sub, 0)
    cot_sub = lax.dynamic_slice_in_dim(cot, tensor * sub, sub, 0)
    outputs_sub, grad_mid, mid_sums, fc_sums, *rest = middle(
        place,
        [piece for part in att for piece in part],
        x_sub,
        cot_sub,
        of,
        dn,
        cols,
        table,
    )
    d_att, (g_own, g_other) = rest[:n_tensor], rest[n_tensor:]
    do_parts = [d_att[0]] + [
        shift_by(d_att[d], -d) for d in range(1, n_tensor)
    ]

    def spread(pieces):
        whole = jnp.zeros((tok, width), f32)
        for d in range(n_tensor):
            at = lax.rem(tensor - d + n_tensor, n_tensor) * sub
            whole = lax.dynamic_update_slice_in_dim(whole, pieces[d].astype(f32), at, 0)
        return whole[None]

    folded = scatter_begin(g_own, g_other)
    hop_one = folded[0] if grouped else folded
    qkv_wide = jnp.pad(qkv_own, ((0, 0), (0, width - 3 * cols)))
    carried = jnp.concatenate([outputs_sub, qkv_wide], axis=0)
    folded = scatter_begin(g_own, g_other)
    hop_one = folded[0] if grouped else folded
    qkv_wide = jnp.pad(qkv_own, ((0, 0), (0, width - 3 * cols)))
    outputs_and_qkv = lax.all_gather(
        jnp.concatenate([outputs_sub, qkv_wide], axis=0), "tensor", axis=0
    )
    wide = scatter_first(folded)
    wide_sends = wide[2:]
    wide = scatter_second(wide)

    dq_pieces, dkv_pieces, dqkv = [], [], []
    head = 0
    queries, keys, values = [], [], []
    sent = [[] for _ in range(n_tensor)]
    for g, held, (lse, ot) in zip(GROUPS, kv, saved):
        out = attend_back(
            scalars, row(starts), after(qt, hop_one), lse, ot, do_parts, held, carried, head, g, BK_B, BQ_B
        )
        back_done = out[-1]
        *out, carried = out
        dq, dkv = out[:n_tensor], out[n_tensor:]
        if grouped:
            dk_keep, dk_send, dv_keep, dv_send = dkv
            r = along_x(dk_send).astype(f32)
            s = along_y(dv_send).astype(f32)
            r2 = along_y((dk_keep[1].astype(f32) + r[1]).astype(bf16)).astype(f32)
            s2 = along_x((dv_keep[1].astype(f32) + s[1]).astype(bf16)).astype(f32)
            dk = (dk_keep[0].astype(f32) + r[0] + r2).astype(bf16)
            dv = (dv_keep[0].astype(f32) + s[0] + s2).astype(bf16)
        else:
            both = lax.psum_scatter(dkv[0], "context", scatter_dimension=0, tiled=True)[0]
            dk, dv = both[: g * HD], both[g * HD :]
        queries.append(dq)
        keys.append(dk)
        values.append(dv)
        head += g

    wide_grads = scatter_line([wide[d] for d in range(n_tensor)])

    def part_of(v, d):
        at = lax.rem(tensor + d, n_tensor) * sub
        return lax.dynamic_slice_in_dim(v, at, sub, 1)

    grads = []
    both = jnp.concatenate(keys + values, axis=0)
    for d in range(n_tensor):
        piece = jnp.concatenate([q[d] for q in queries] + [part_of(both, d)], axis=0)
        grads.append(shift_by(piece, d) if d else piece)
    pieces = 1

    dq_whole = []
    for q in queries:
        whole = jnp.zeros((q[0].shape[0], tok), bf16)
        for d in range(n_tensor):
            at = lax.rem(tensor + d, n_tensor) * sub
            whole = lax.dynamic_update_slice_in_dim(whole, q[d], at, 1)
        dq_whole.append(whole)
    outputs_and_qkv = lax.all_gather(carried, "tensor", axis=0)
    outputs = outputs_and_qkv[:, :sub].reshape(tok, width)
    qkv = outputs_and_qkv[:, sub:]
    qkv = (qkv, swap(qkv))
    stacked = jnp.concatenate(
        dq_whole + [both, jnp.zeros((-3 * cols % 128, tok), bf16)], axis=0
    )
    qkv_grad = jnp.einsum(
        "td,ct->dc", low_one, stacked, preferred_element_type=f32
    ).astype(bf16)
    qkv_mine = lax.dynamic_slice_in_dim(qkv_grad, core * half, half, 0)
    qkv_theirs = lax.dynamic_slice_in_dim(qkv_grad, (1 - core) * half, half, 0)
    qkv_folded = scatter_begin(qkv_mine[None], qkv_theirs[None])

    input_sub, small = last(
        place, grads, pieces, qkv, x_sub, after(grad_mid, qkv_folded), table, mid_sums, fc_sums
    )
    input_gradient = spread(gather_direct(input_sub))
    outputs = after(outputs, input_sub).astype(f32)[None]
    qkv_grads = scatter_second(scatter_first(qkv_folded))[0]

    if grouped and n_tensor == 4 and n_shard == 2:
        small += lax.ppermute(small, "tensor", [(0, 2), (2, 0), (1, 3), (3, 1)])
        small += lax.ppermute(small, "tensor", [(0, 1), (1, 0), (2, 3), (3, 2)])
        small += swap(small)
        small += along_x(small)
        small += along_y(small)
    else:
        small = lax.psum(small, ("shard", "context", "tensor"))
    fc_total = lax.dynamic_index_in_dim(small, 6 + tensor, 0, keepdims=False)
    qv_total = lax.dynamic_index_in_dim(small, 6 + n_tensor + tensor, 0, keepdims=False)
    qv_total = jnp.stack([qv_total[:cols], qv_total[2 * cols : 3 * cols]])
    return (
        outputs,
        input_gradient,
        qkv_grads[:, : 3 * cols].astype(f32).reshape(-1, 3, cols),
        wide_grads[:, 2 * ffw : 2 * ffw + cols].T,
        wide_grads[:, :ffw],
        wide_grads[:, ffw : 2 * ffw].T,
        qv_total,
        small[0],
        fc_total,
        small[1],
        small[4],
        small[5],
        small[2],
        small[3],
    )


def solution(mesh):
    sizes = dict(mesh.shape)
    placed = (
        P("shard", "context", None),
        P("shard", None),
        P("shard", None, "tensor"),
        P("tensor", "shard"),
        P("shard", "tensor"),
        P("tensor", "shard"),
        P(None, "tensor"),
        P(),
        P("tensor"),
        P(),
        P(),
        P(),
        P(),
        P(),
        P("shard", "context", None),
    )
    return jax.shard_map(
        functools.partial(body, sizes["shard"], sizes["context"], sizes["tensor"]),
        mesh=mesh,
        in_specs=placed,
        out_specs=(
            P("shard", "context", None),
            P("shard", "context", None),
            P(("shard", "context"), None, "tensor"),
            P("tensor", ("shard", "context")),
            P(("shard", "context"), "tensor"),
            P("tensor", ("shard", "context")),
            P(None, "tensor"),
            P(),
            P("tensor"),
            P(),
            P(),
            P(),
            P(),
            P(),
        ),
        check_vma=False,
    )
```
